32 devices in a mesh: pb: 8 (over y, x, core), ka: 4 (over z).
Axes of the slice: x: 2, y: 2, z: 4, core: 2. Of those that a mesh axis runs over, the one named last changes fastest.
Arguments:
- atoms: bfloat16 [24576, 128], P('pb'), may hold values from -6 to 6
- atom_gain: float32 [128], replicated, may hold values from 0.1 to 1.9
- atom_qkv: bfloat16 [128, 384], replicated, may hold values from -0.5 to 0.5
- atom_proj: bfloat16 [128, 128], replicated, may hold values from -0.5 to 0.5
- atom_bias: bfloat16 [4, 24576, 128], P(None, 'pb'), may hold values from -4 to 250
- window_shift: int32 [768], P('pb'), may hold values from -64 to -32, as said below
- token_of_atom: int32 [24576], P('pb'), may hold values from 0 to 3071, as said below
- agg_weight: bfloat16 [128, 768], replicated, may hold values from -0.5 to 0.5
- token_gain: float32 [768], replicated, may hold values from 0.1 to 1.9
- token_q: bfloat16 [768, 768], replicated, may hold values from -0.21875 to 0.21875
- token_kv: bfloat16 [768, 1536], replicated, may hold values from -0.21875 to 0.21875
- token_o: bfloat16 [768, 768], replicated, may hold values from -0.21875 to 0.21875
- pair_bias: bfloat16 [16, 3072, 3072], P(None, 'pb', 'ka'), may hold values from -4 to 250
Outputs:
- atom_out: bfloat16 [24576, 128], P('pb')
- tokens_out: bfloat16 [3072, 768], P('pb')
The draws below stay inside these ranges and needn't reach their ends.
Inputs may be any that keep to these rules, and one draw needn't show every extreme that they name: token_of_atom never falls along the atoms and names every token at least once. Of the 3072 atoms of one index of pb, all but its last ones belong to that index's own 384 tokens; for every index but the final one, its last 192 to 384 atoms belong to the tokens of the index after, and the final index's atoms are all its own. In every draw some index has all of its last 384 atoms in the index after. The key window of query block b begins at atom 32 b + window_shift[b]; both ends of the range occur in every draw.
All inputs are finite; a program needn't handle non-finite values.
Results may differ from the reference program's by a relative error of at most 0.0095.
Values may be sent and summed in bfloat16 or wider, within the bound.
No kernel may reach another device: no remote copies, remote signals or barrier semaphores. Data moves between devices by JAX's collectives and lax.ppermute only.
A program may use at most 128 MiB of HBM per device.

```python
import math
import jax
import jax.numpy as jnp
from jax import lax

CA = 128
AH = 4
CT = 768
TH = 16
WIN_Q = 32
WIN_K = 128
TOK_DEV = 384
ATOM_DEV = 3072
SHIFT_MAX = 384
TOKENS = 3072
ATOMS = 24576
KEY_DEV = 768
N_KA = 4


def token_starts(key):
    shards = TOKENS // TOK_DEV
    key_drift, key_order, key_weight = jax.random.split(jax.random.fold_in(key, 11), 3)
    drift = jax.random.randint(key_drift, (shards + 1,), -SHIFT_MAX, -(SHIFT_MAX // 2) + 1, dtype=jnp.int32)
    order = jax.random.permutation(key_order, shards - 1) + 1
    drift = drift.at[order[0]].set(-SHIFT_MAX)
    drift = drift.at[0].set(0).at[shards].set(0)
    borders = jnp.arange(shards + 1, dtype=jnp.int32) * ATOM_DEV + drift
    surplus = borders[1:] - borders[:-1] - TOK_DEV
    weights = jax.random.randint(key_weight, (shards, TOK_DEV), 1, 33, dtype=jnp.int32)
    before = jnp.cumsum(weights, axis=1) - weights
    totals = jnp.sum(weights, axis=1)
    starts = borders[:-1, None] + jnp.arange(TOK_DEV, dtype=jnp.int32)[None, :] + before * surplus[:, None] // totals[:, None]
    return starts.reshape(-1)


def draw_token_of_atom(key, part):
    starts = token_starts(key)
    atom_index = jnp.arange(ATOMS, dtype=jnp.int32)
    return (jnp.searchsorted(starts, atom_index, side='right') - 1).astype(jnp.int32)


def draw_window_shift(key, part):
    windows = ATOMS // WIN_Q
    key_value, key_order = jax.random.split(jax.random.fold_in(key, 23), 2)
    shifts = jax.random.randint(key_value, (windows,), -(WIN_K // 2), WIN_Q - WIN_K // 2 + 1, dtype=jnp.int32)
    order = jax.random.permutation(key_order, windows)
    shifts = shifts.at[order[0]].set(-(WIN_K // 2)).at[order[1]].set(WIN_Q - WIN_K // 2)
    return shifts


def spiky_bias(key, shape):
    key_base = jax.random.fold_in(key, 0)
    base = jax.random.truncated_normal(key_base, -4.0, 4.0, shape, jnp.float32)
    return base.astype(jnp.bfloat16)


def draw_atom_bias(key, part):
    return spiky_bias(jax.random.fold_in(key, 31), (AH, ATOMS, WIN_K))


def draw_pair_bias(key, part):
    return spiky_bias(jax.random.fold_in(key, 47), (TH, TOKENS, TOKENS))


def block_levels(key, extent, pieces, smallest, top_value):
    loudness, own = 1.0, jax.random.fold_in(key, 6)
    for position, shards_of in pieces:
        heights = jnp.exp(jax.random.uniform(jax.random.fold_in(own, position), (shards_of,), jnp.float32, smallest / len(pieces), top_value / len(pieces)))
        loudness = loudness * jnp.repeat(heights, extent[position] // shards_of).reshape([-1 if axis == position else 1 for axis in range(len(extent))])
    return loudness


def noise(own_key, extent, deviation, bound, cuts=(), kind=jnp.bfloat16):
    loudness = block_levels(own_key, extent, cuts, -0.22, 0.18) if cuts else 1.0
    result = jax.random.normal(own_key, extent, jnp.float32) * deviation * loudness
    return jnp.minimum(jnp.maximum(result, -bound), bound).astype(kind)


def setup_inputs(seed: int = 0) -> dict:
    keys = jax.random.split(jax.random.key(seed), 14)
    return {
        "atoms": noise(keys[0], (ATOMS, CA), 1.0, 6.0, ((0, 8),)),
        "atom_gain": jnp.clip(1.0 + 0.18 * jax.random.normal(keys[1], (CA,), jnp.float32), 0.1, 1.9),
        "atom_qkv": noise(keys[2], (CA, 3 * CA), CA ** -0.5, 0.5),
        "atom_proj": noise(keys[3], (CA, CA), CA ** -0.5, 0.5),
        "atom_bias": draw_atom_bias(jax.random.fold_in(keys[13], 71), 0),
        "window_shift": draw_window_shift(jax.random.fold_in(keys[13], 71), 0),
        "token_of_atom": draw_token_of_atom(jax.random.fold_in(keys[13], 71), 0),
        "agg_weight": noise(keys[7], (CA, CT), CA ** -0.5, 0.5),
        "token_gain": jnp.clip(1.0 + 0.18 * jax.random.normal(keys[8], (CT,), jnp.float32), 0.1, 1.9),
        "token_q": noise(keys[9], (CT, CT), CT ** -0.5, 0.21875),
        "token_kv": noise(keys[10], (CT, 2 * CT), CT ** -0.5, 0.21875),
        "token_o": noise(keys[11], (CT, CT), CT ** -0.5, 0.21875),
        "pair_bias": draw_pair_bias(jax.random.fold_in(keys[13], 71), 0),
    }


def layer_norm(values, gain_vec):
    as_float = values.astype(jnp.float32)
    centre = lax.optimization_barrier(jnp.mean(as_float, axis=-1, keepdims=True))
    spread = lax.optimization_barrier(jnp.mean(jnp.square(as_float - centre), axis=-1, keepdims=True))
    return (as_float - centre) * lax.rsqrt(spread + 1e-05) * gain_vec

def reference(atoms, atom_gain, atom_qkv, atom_proj, atom_bias, window_shift, token_of_atom, agg_weight, token_gain, token_q, token_kv, token_o, pair_bias):
    atom_head = CA // AH
    half_win = WIN_K // 2
    normed = layer_norm(atoms, atom_gain).astype(jnp.bfloat16)
    projected = jnp.dot(normed, atom_qkv, preferred_element_type=jnp.float32).astype(jnp.bfloat16)
    blocks = ATOMS // WIN_Q
    padded = jnp.pad(projected[:, CA:], ((half_win, half_win), (0, 0)))
    window_first = jnp.arange(blocks, dtype=jnp.int32) * WIN_Q + window_shift.astype(jnp.int32)
    key_index = window_first[:, None] + jnp.arange(WIN_K, dtype=jnp.int32)[None, :]
    gathered = padded[key_index + half_win]
    in_range = (key_index >= 0) & (key_index < ATOMS)
    query_heads = projected[:, :CA].reshape(blocks, WIN_Q, AH, atom_head).astype(jnp.float32)
    key_heads = gathered[:, :, :CA].reshape(blocks, WIN_K, AH, atom_head).astype(jnp.float32)
    value_heads = gathered[:, :, CA:].reshape(blocks, WIN_K, AH, atom_head).astype(jnp.float32)
    scores = jnp.einsum('bqhd,bkhd->hbqk', query_heads, key_heads) / math.sqrt(atom_head)
    scores = scores + atom_bias.astype(jnp.float32).reshape(AH, blocks, WIN_Q, WIN_K)
    scores = jnp.where(in_range[None, :, None, :], scores, -jnp.inf)
    exp_terms = jnp.exp(scores - lax.optimization_barrier(jnp.max(scores, axis=-1, keepdims=True)))
    weights = (exp_terms / lax.optimization_barrier(jnp.sum(exp_terms, axis=-1, keepdims=True))).astype(jnp.bfloat16)
    atom_mixed = jnp.einsum('hbqk,bkhd->bqhd', weights.astype(jnp.float32), value_heads)
    atom_mixed = atom_mixed.reshape(ATOMS, CA).astype(jnp.bfloat16)
    atom_out = (atoms.astype(jnp.float32) + jnp.dot(atom_mixed, atom_proj, preferred_element_type=jnp.float32)).astype(jnp.bfloat16)
    hidden = jax.nn.silu(jnp.dot(atom_out, agg_weight, preferred_element_type=jnp.float32)).astype(jnp.bfloat16)
    token_sums = jax.ops.segment_sum(hidden.astype(jnp.float32), token_of_atom, num_segments=TOKENS)
    token_counts = jax.ops.segment_sum(jnp.ones((ATOMS,), jnp.float32), token_of_atom, num_segments=TOKENS)
    token_repr = (token_sums / token_counts[:, None]).astype(jnp.bfloat16)
    token_normed = layer_norm(token_repr, token_gain).astype(jnp.bfloat16)
    queries = jnp.dot(token_normed, token_q, preferred_element_type=jnp.float32).astype(jnp.bfloat16)
    keyvals = jnp.dot(token_normed, token_kv, preferred_element_type=jnp.float32).astype(jnp.bfloat16)
    token_head = CT // TH
    key_blocks = keyvals[:, :CT].reshape(N_KA, KEY_DEV, TH, token_head).astype(jnp.float32)
    value_blocks = keyvals[:, CT:].reshape(N_KA, KEY_DEV, TH, token_head).astype(jnp.float32)
    block_rows = math.gcd(TOKENS, 512)

    def one_block(first_row):
        query_rows = lax.dynamic_slice_in_dim(queries, first_row, block_rows, 0)
        query_rows = query_rows.reshape(block_rows, TH, token_head).astype(jnp.float32)
        bias_rows = lax.dynamic_slice_in_dim(pair_bias, first_row, block_rows, 1).astype(jnp.float32)
        bias_rows = bias_rows.reshape(TH, block_rows, N_KA, KEY_DEV)
        block_scores = jnp.einsum('qhd,nkhd->hqnk', query_rows, key_blocks) / math.sqrt(token_head) + bias_rows
        block_max = lax.optimization_barrier(jnp.max(block_scores, axis=-1, keepdims=True))
        block_exp = jnp.exp(block_scores - block_max)
        rounded = block_exp.astype(jnp.bfloat16).astype(jnp.float32)
        block_mix = jnp.einsum('hqnk,nkhd->hqnd', rounded, value_blocks)
        block_totals = lax.optimization_barrier(jnp.sum(block_exp, axis=-1))
        block_top = block_max[..., 0]
        row_max = lax.optimization_barrier(jnp.max(block_top, axis=-1, keepdims=True))
        factor = jnp.exp(block_top - row_max)
        mixed_sum = lax.optimization_barrier(jnp.sum(block_mix * factor[..., None], axis=2))
        total_sum = lax.optimization_barrier(jnp.sum(block_totals * factor, axis=-1))
        token_mixed = mixed_sum / total_sum[..., None]
        return token_mixed.transpose(1, 0, 2).reshape(block_rows, CT).astype(jnp.bfloat16)
    first_rows = jnp.arange(TOKENS // block_rows, dtype=jnp.int32) * block_rows
    token_mix = lax.map(one_block, first_rows).reshape(TOKENS, CT)
    tokens_out = (token_repr.astype(jnp.float32) + jnp.dot(token_mix, token_o, preferred_element_type=jnp.float32)).astype(jnp.bfloat16)
    return (atom_out, tokens_out)
```

```python
import functools
import math

import jax
import jax.numpy as jnp
from jax import lax
from jax.experimental import pallas as pl
from jax.experimental.pallas import tpu as pltpu
from jax.sharding import PartitionSpec as P

AH = 4
TH = 16
WIN_Q = 32
WIN_K = 128
SHIFT_MAX = 384
LANES = 128
F32 = jnp.float32
BF16 = jnp.bfloat16
VMEM_LIMIT = 40 * 1024 * 1024


def full(shape):
    return pl.BlockSpec(shape, lambda *_: (0,) * len(shape))


def params():
    return pltpu.CompilerParams(vmem_limit_bytes=VMEM_LIMIT)


def norm_rows(as_float, gain):
    centre = jnp.mean(as_float, axis=-1, keepdims=True)
    spread = jnp.mean(jnp.square(as_float - centre), axis=-1, keepdims=True)
    return (as_float - centre) * lax.rsqrt(spread + 1e-05) * gain


def dot(a, b):
    return jnp.dot(a, b, preferred_element_type=F32)


def dot_nt(a, b):
    return lax.dot_general(a, b, (((1,), (1,)), ((), ())), preferred_element_type=F32)


def atom_kernel(
    chunks,
    atom_total,
    tok_rows,
    shift_ref,
    pos_ref,
    atoms_ref,
    left_ref,
    right_ref,
    gain_ref,
    qkv_ref,
    proj_ref,
    bias_ref,
    tok_ref,
    out_ref,
    msg_ref,
    q_s,
    k_s,
    v_s,
    mix_s,
):
    step = pl.program_id(0)
    rows, width = atoms_ref.shape
    size = out_ref.shape[0]
    half = WIN_K // 2
    head = width // AH
    shard = pos_ref[0]

    @pl.when(step == 0)
    def _():
        gain = gain_ref[...]

        def project(values):
            normed = norm_rows(values.astype(F32), gain).astype(BF16)
            return dot(normed, qkv_ref[...])

        def one(c, carry):
            at = pl.multiple_of(c * size, size)
            res = project(atoms_ref[pl.ds(at, size), :])
            q_s[pl.ds(at, size), :] = (res[:, :width] * (1.0 / math.sqrt(head))).astype(BF16)
            k_s[pl.ds(at + half, size), :] = res[:, width : 2 * width]
            v_s[pl.ds(at + half, size), :] = res[:, 2 * width :]
            return carry

        lax.fori_loop(0, chunks, one, 0)
        for ref, at in ((left_ref, 0), (right_ref, half + rows)):
            res = project(ref[...])
            k_s[at : at + half, :] = res[:, width : 2 * width]
            v_s[at : at + half, :] = res[:, 2 * width :]

    lane = lax.broadcasted_iota(jnp.int32, (WIN_Q, width), 1)
    heads = [(lane >= h * head) & (lane < (h + 1) * head) for h in range(AH)]
    slot = lax.broadcasted_iota(jnp.int32, (1, WIN_K), 1)
    per = size // WIN_Q

    def block(b, carry):
        number = step * per + b
        first = number * WIN_Q + shift_ref[number]
        keys = k_s[pl.ds(first + half, WIN_K), :].astype(BF16)
        values = v_s[pl.ds(first + half, WIN_K), :].astype(BF16)
        at = pl.multiple_of(number * WIN_Q, WIN_Q)
        local = pl.multiple_of(b * WIN_Q, WIN_Q)
        query = q_s[pl.ds(at, WIN_Q), :].astype(F32)
        stacked = jnp.concatenate([jnp.where(m, query, 0.0) for m in heads], axis=0).astype(BF16)
        scores = dot_nt(stacked, keys)
        bias = bias_ref[:, pl.ds(local, WIN_Q), :].astype(F32).reshape(AH * WIN_Q, WIN_K)
        index = slot + (first + shard * rows)
        keep = (index >= 0) & (index < atom_total)
        scores = jnp.where(keep, scores + bias, -jnp.inf)
        terms = jnp.exp(scores - jnp.max(scores, axis=-1, keepdims=True))
        weights = (terms / jnp.sum(terms, axis=-1, keepdims=True)).astype(BF16)
        mixed = dot(weights, values)
        merged = jnp.zeros((WIN_Q, width), F32)
        for h in range(AH):
            merged = jnp.where(heads[h], mixed[h * WIN_Q : (h + 1) * WIN_Q], merged)
        mix_s[pl.ds(local, WIN_Q), :] = merged.astype(BF16)
        return carry

    lax.fori_loop(0, per, block, 0, unroll=4)
    at = pl.multiple_of(step * size, size)
    own = atoms_ref[pl.ds(at, size), :].astype(F32)
    result = (own + dot(mix_s[...], proj_ref[...])).astype(BF16)
    out_ref[...] = result

    @pl.when(step == chunks - 1)
    def _():
        ids = tok_ref[tok_ref.shape[0] - 8 :, :]
        code = jnp.maximum(ids - (shard + 1) * tok_rows + 1, 0)
        high = (code >> 4).astype(F32)
        low = (code & 15).astype(F32)
        msg_ref[:size, :] = result
        msg_ref[size:, :] = jnp.concatenate([high, low], axis=0).astype(BF16)


def atom_attention(shift, pos, atoms, left, right, gain, qkv, proj, bias, tok2d, tok_rows, atom_total):
    rows, width = atoms.shape
    size = SHIFT_MAX
    chunks = rows // size
    half = WIN_K // 2
    return pl.pallas_call(
        functools.partial(atom_kernel, chunks, atom_total, tok_rows),
        grid_spec=pltpu.PrefetchScalarGridSpec(
            num_scalar_prefetch=2,
            grid=(chunks,),
            in_specs=[
                full((rows, width)),
                full((half, width)),
                full((half, width)),
                full((1, width)),
                full(qkv.shape),
                full(proj.shape),
                pl.BlockSpec((AH, size, WIN_K), lambda i, *_: (0, i, 0)),
                full(tok2d.shape),
            ],
            out_specs=[
                pl.BlockSpec((size, width), lambda i, *_: (i, 0)),
                full((size + 16, width)),
            ],
            scratch_shapes=[
                pltpu.VMEM((rows, width), BF16),
                pltpu.VMEM((rows + 2 * half, width), F32),
                pltpu.VMEM((rows + 2 * half, width), F32),
                pltpu.VMEM((size, width), BF16),
            ],
        ),
        out_shape=[
            jax.ShapeDtypeStruct((rows, width), BF16),
            jax.ShapeDtypeStruct((size + 16, width), BF16),
        ],
        compiler_params=params(),
        cost_estimate=pl.CostEstimate(flops=8 * 10**9, bytes_accessed=6 * 10**6, transcendentals=2 * 10**6),
        name="atom_attention",
    )(shift, pos, atoms, left, right, gain, qkv, proj, bias, tok2d)


def activate(rows, weight_half):
    u = dot(rows, weight_half)
    return (u + u * jnp.tanh(u)).astype(BF16)


def pool_kernel(tok_rows, pos_ref, out_ref, weight_ref, tok_ref, sum_ref, cnt_ref):
    step = pl.program_id(0)
    size = out_ref.shape[0]
    lines = size // LANES
    base = pos_ref[0] * tok_rows
    token = lax.broadcasted_iota(jnp.int32, (tok_rows, LANES), 0)
    weight_half = (weight_ref[...].astype(F32) * 0.5).astype(BF16)
    hidden = activate(out_ref[...], weight_half)
    ones = []
    for j in range(lines):
        ids = tok_ref[pl.ds(step * lines + j, 1), :] - base
        ones.append(jnp.where(token == ids, 1.0, 0.0))
    hot = jnp.concatenate(ones, axis=1).astype(BF16)
    count = functools.reduce(jnp.add, ones)
    part = dot(hot, hidden)

    @pl.when(step == 0)
    def _():
        sum_ref[...] = part
        cnt_ref[...] = count

    @pl.when(step > 0)
    def _():
        sum_ref[...] += part
        cnt_ref[...] += count


def pool(pos, atom_out, weight, tok2d, tok_rows):
    rows, width = atom_out.shape
    feats = weight.shape[1]
    size = 512
    return pl.pallas_call(
        functools.partial(pool_kernel, tok_rows),
        grid_spec=pltpu.PrefetchScalarGridSpec(
            num_scalar_prefetch=1,
            grid=(rows // size,),
            in_specs=[
                pl.BlockSpec((size, width), lambda i, *_: (i, 0)),
                full(weight.shape),
                full(tok2d.shape),
            ],
            out_specs=[full((tok_rows, feats)), full((tok_rows, LANES))],
        ),
        out_shape=[
            jax.ShapeDtypeStruct((tok_rows, feats), F32),
            jax.ShapeDtypeStruct((tok_rows, LANES), F32),
        ],
        compiler_params=params(),
        cost_estimate=pl.CostEstimate(flops=4 * 10**9, bytes_accessed=3 * 10**6, transcendentals=2 * 10**6),
        name="pool",
    )(pos, atom_out, weight, tok2d)


def finish_kernel(msg_ref, weight_ref, sum_ref, cnt_ref, gain_ref, repr_ref, normed_ref):
    tok_rows = sum_ref.shape[0]
    size = msg_ref.shape[0] - 16
    lines = size // LANES
    token = lax.broadcasted_iota(jnp.int32, (tok_rows, LANES), 0).astype(F32)
    weight_half = (weight_ref[...].astype(F32) * 0.5).astype(BF16)
    hidden = activate(msg_ref[:size, :], weight_half)
    codes = msg_ref[size:, :].astype(F32)
    ids = codes[:8] * 16.0 + codes[8:] - 1.0
    ones = [jnp.where(token == ids[8 - lines + j : 9 - lines + j], 1.0, 0.0) for j in range(lines)]
    hot = jnp.concatenate(ones, axis=1).astype(BF16)
    count = functools.reduce(jnp.add, ones) + cnt_ref[...]
    sums = sum_ref[...] + dot(hot, hidden)
    token_repr = (sums / jnp.sum(count, axis=1, keepdims=True)).astype(BF16)
    repr_ref[...] = token_repr
    normed_ref[...] = norm_rows(token_repr.astype(F32), gain_ref[...]).astype(BF16)


def finish(msg, weight, sums, counts, gain):
    shape = sums.shape
    return pl.pallas_call(
        finish_kernel,
        out_shape=[jax.ShapeDtypeStruct(shape, BF16)] * 2,
        compiler_params=params(),
        cost_estimate=pl.CostEstimate(flops=4 * 10**8, bytes_accessed=3 * 10**6, transcendentals=3 * 10**5),
        name="token_finish",
    )(msg, weight, sums, counts, gain)


HEADS_STEP = 4


def pack_lse(lse):
    lane = lax.broadcasted_iota(jnp.int32, lse.shape, 1)
    high = lse.astype(BF16).astype(F32)
    rest = lse - high
    middle = rest.astype(BF16).astype(F32)
    low = rest - middle
    return jnp.where(
        lane < TH,
        high,
        jnp.where(lane < 2 * TH, pltpu.roll(middle, TH, 1), pltpu.roll(low, 2 * TH, 1)),
    ).astype(BF16)


def unpack_lse(coded):
    value = coded.astype(F32)
    return value + pltpu.roll(value, LANES - TH, 1) + pltpu.roll(value, LANES - 2 * TH, 1)


def attend_step(step, half, q_ref, k_ref, v_ref, bias_ref, o_s, lse_s):
    rows = o_s.shape[0]
    odd = lax.rem(step, 2)
    base = pl.multiple_of((step // 2) * 384 + odd * 128, 128)
    window = pl.ds(base, 256)
    at = pl.multiple_of(half * rows, rows)
    query = q_ref[pl.ds(at, rows), window].astype(F32)
    keys = k_ref[:, window]
    values = v_ref[:, window]
    lane = lax.broadcasted_iota(jnp.int32, (rows, 256), 1)
    spot = lax.broadcasted_iota(jnp.int32, (rows, LANES), 1)
    result = o_s[:, window]
    lse = lse_s[...]
    for j in range(HEADS_STEP):
        begin = 48 * j + 64 * odd
        mask = (lane >= begin) & (lane < begin + 48)
        scores = dot_nt(jnp.where(mask, query, 0.0).astype(BF16), keys) + bias_ref[j].astype(F32)
        top = jnp.max(scores, axis=-1, keepdims=True)
        terms = jnp.exp(scores - top)
        total = jnp.sum(terms, axis=-1, keepdims=True)
        mixed = dot(terms.astype(BF16), values)
        result = jnp.where(mask, mixed / total, result)
        lse = jnp.where(spot == step * HEADS_STEP + j, top + jnp.log(total), lse)
    o_s[:, window] = result
    lse_s[...] = lse


def send_kernel(steps, sc_ref, q_ref, own_ref, other_ref, wkv_ref, bias_ref, k_ref, v_ref, msg_ref, o_s, lse_s, x_s):
    step = pl.program_id(0)
    rows, feats = own_ref.shape

    @pl.when(step == 0)
    def _():
        core = sc_ref[1]
        x_s[pl.ds(pl.multiple_of(core * rows, rows), rows), :] = own_ref[...]
        x_s[pl.ds(pl.multiple_of((1 - core) * rows, rows), rows), :] = other_ref[...]
        for r in range(0, 2 * rows, rows):
            k_ref[r : r + rows, :] = dot(x_s[r : r + rows, :], wkv_ref[:, :feats]).astype(BF16)
            v_ref[r : r + rows, :] = dot(x_s[r : r + rows, :], wkv_ref[:, feats:]).astype(BF16)
        lse_s[...] = jnp.zeros_like(lse_s)

    attend_step(step, sc_ref[0], q_ref, k_ref, v_ref, bias_ref, o_s, lse_s)

    @pl.when(step == steps - 1)
    def _():
        msg_ref[:, :feats] = o_s[...].astype(BF16)
        msg_ref[:, feats:] = pack_lse(lse_s[...])


def keep_kernel(sc_ref, q_ref, k_ref, v_ref, bias_ref, o_ref, lse_ref):
    step = pl.program_id(0)

    @pl.when(step == 0)
    def _():
        lse_ref[...] = jnp.zeros_like(lse_ref)

    attend_step(step, sc_ref[0], q_ref, k_ref, v_ref, bias_ref, o_ref, lse_ref)


def attention(sc, q, bias, keys, first):
    tok_rows, feats = q.shape
    rows = tok_rows // 2
    key_rows = bias.shape[2]
    steps = TH // HEADS_STEP
    bias_spec = pl.BlockSpec((HEADS_STEP, rows, key_rows), lambda i, s: (i, s[0], 0))
    kv_shape = (key_rows, feats)
    cost = pl.CostEstimate(flops=8 * 10**9, bytes_accessed=8 * 10**6, transcendentals=3 * 10**6)
    if first:
        own, other, wkv = keys
        return pl.pallas_call(
            functools.partial(send_kernel, steps),
            grid_spec=pltpu.PrefetchScalarGridSpec(
                num_scalar_prefetch=1,
                grid=(steps,),
                in_specs=[full(q.shape), full(own.shape), full(other.shape), full(wkv.shape), bias_spec],
                out_specs=[full(kv_shape), full(kv_shape), full((rows, feats + LANES))],
                scratch_shapes=[
                    pltpu.VMEM((rows, feats), F32),
                    pltpu.VMEM((rows, LANES), F32),
                    pltpu.VMEM(kv_shape, BF16),
                ],
            ),
            out_shape=[
                jax.ShapeDtypeStruct(kv_shape, BF16),
                jax.ShapeDtypeStruct(kv_shape, BF16),
                jax.ShapeDtypeStruct((rows, feats + LANES), BF16),
            ],
            compiler_params=params(),
            cost_estimate=cost,
            name="attend_send",
        )(sc, q, own, other, wkv, bias)
    k, v = keys
    return pl.pallas_call(
        keep_kernel,
        grid_spec=pltpu.PrefetchScalarGridSpec(
            num_scalar_prefetch=1,
            grid=(steps,),
            in_specs=[full(q.shape), full(kv_shape), full(kv_shape), bias_spec],
            out_specs=[full((rows, feats)), full((rows, LANES))],
        ),
        out_shape=[
            jax.ShapeDtypeStruct((rows, feats), F32),
            jax.ShapeDtypeStruct((rows, LANES), F32),
        ],
        compiler_params=params(),
        cost_estimate=cost,
        name="attend_keep",
    )(sc, q, k, v, bias)


def merged_rows(o_ref, lse_ref, msg_ref):
    rows, feats = o_ref.shape
    width = feats // TH
    other = msg_ref[:, :feats].astype(F32)
    lse_b = unpack_lse(msg_ref[:, feats:])
    spot = lax.broadcasted_iota(jnp.int32, (rows, LANES), 1)
    lse_a = lse_ref[...]
    lse_b = jnp.where(spot < TH, lse_b, lse_a)
    top = jnp.maximum(lse_a, lse_b)
    part_a = jnp.exp(lse_a - top)
    total = part_a + jnp.exp(lse_b - top)
    share = part_a / total
    high = share.astype(BF16)
    low = (share - high.astype(F32)).astype(BF16)
    head = lax.broadcasted_iota(jnp.int32, (LANES, feats), 0) * width
    column = lax.broadcasted_iota(jnp.int32, (LANES, feats), 1)
    spread = jnp.where((column >= head) & (column < head + width), 1.0, 0.0).astype(BF16)
    wide = dot(high, spread) + dot(low, spread)
    return other + wide * (o_ref[...] - other), top + jnp.log(total)


def merge_kernel(o_ref, lse_ref, msg_ref, out_ref, sum_ref, back_ref):
    mixed, lse = merged_rows(o_ref, lse_ref, msg_ref)
    feats = mixed.shape[1]
    out_ref[...] = mixed
    sum_ref[...] = lse
    back_ref[:, :feats] = mixed.astype(BF16)
    back_ref[:, feats:] = pack_lse(lse)


def merge(o, lse, msg):
    return pl.pallas_call(
        merge_kernel,
        out_shape=[
            jax.ShapeDtypeStruct(o.shape, F32),
            jax.ShapeDtypeStruct(lse.shape, F32),
            jax.ShapeDtypeStruct(msg.shape, BF16),
        ],
        compiler_params=params(),
        name="merge",
    )(o, lse, msg)


def last_kernel(half_ref, o_ref, lse_ref, msg_ref, repr_ref, weight_ref, out_ref):
    rows = o_ref.shape[0]
    mixed, _ = merged_rows(o_ref, lse_ref, msg_ref)
    own = repr_ref[pl.ds(pl.multiple_of(half_ref[0] * rows, rows), rows), :].astype(F32)
    out_ref[...] = (own + dot(mixed.astype(BF16), weight_ref[...])).astype(BF16)


def last_merge(half, o, lse, msg, token_repr, weight):
    return pl.pallas_call(
        last_kernel,
        in_specs=[pl.BlockSpec(memory_space=pltpu.SMEM)] + [pl.BlockSpec(memory_space=pltpu.VMEM)] * 5,
        out_shape=jax.ShapeDtypeStruct(o.shape, BF16),
        compiler_params=params(),
        name="merge_last",
    )(half, o, lse, msg, token_repr, weight)


def join_kernel(half_ref, own_ref, other_ref, out_ref):
    rows = own_ref.shape[0]
    out_ref[pl.ds(pl.multiple_of(half_ref[0] * rows, rows), rows), :] = own_ref[...]
    out_ref[pl.ds(pl.multiple_of((1 - half_ref[0]) * rows, rows), rows), :] = other_ref[...]


def join(half, own, other):
    rows, feats = own.shape
    return pl.pallas_call(
        join_kernel,
        in_specs=[pl.BlockSpec(memory_space=pltpu.SMEM)] + [pl.BlockSpec(memory_space=pltpu.VMEM)] * 2,
        out_shape=jax.ShapeDtypeStruct((2 * rows, feats), BF16),
        compiler_params=params(),
        name="join",
    )(half, own, other)


def bits_of(count):
    return [1 << b for b in range(count.bit_length() - 1)]


def key_block(normed):
    n_pb, n_ka = lax.axis_size("pb"), lax.axis_size("ka")
    cores = n_pb // n_ka
    chips = n_pb // cores
    shard, plane = lax.axis_index("pb"), lax.axis_index("ka")
    bits = bits_of(chips)
    core = lax.rem(shard, cores)
    away = jnp.bitwise_xor(shard // cores, plane)
    held = normed
    for r in range(len(bits)):
        pairs = []
        gets = jnp.bool_(False)
        for c in range(cores):
            order = bits if c % 2 == 0 else bits[::-1]
            known = sum(order[:r])
            for k in range(n_ka):
                for j in range(chips):
                    if (j ^ k) & ~known == 0:
                        pairs.append(((j * cores + c) * n_ka + k, ((j ^ order[r]) * cores + c) * n_ka + k))
            fresh = (jnp.bitwise_and(away, ~(known + order[r])) == 0) & (jnp.bitwise_and(away, order[r]) != 0)
            gets = gets | (fresh & (core == c))
        moved = lax.ppermute(held, ("pb", "ka"), pairs)
        held = jnp.where(gets, moved, held)
    swap = [(p, p ^ 1) for p in range(n_pb)]
    return held, lax.ppermute(held, "pb", swap)


def body(
    atoms,
    atom_gain,
    atom_qkv,
    atom_proj,
    atom_bias,
    window_shift,
    token_of_atom,
    agg_weight,
    token_gain,
    token_q,
    token_kv,
    token_o,
    pair_bias,
):
    n_pb, n_ka = lax.axis_size("pb"), lax.axis_size("ka")
    shard, plane = lax.axis_index("pb"), lax.axis_index("ka")
    rows, width = atoms.shape
    tok_rows = pair_bias.shape[1]
    half = WIN_K // 2
    up = [(i, i + 1) for i in range(n_pb - 1)]
    down = [(i + 1, i) for i in range(n_pb - 1)]
    pos = shard.astype(jnp.int32).reshape(1)
    tok2d = token_of_atom.reshape(rows // LANES, LANES)
    left = lax.ppermute(atoms[rows - half :], "pb", up)
    right = lax.ppermute(atoms[:half], "pb", down)
    atom_out, msg = atom_attention(
        window_shift, pos, atoms, left, right, atom_gain.reshape(1, width), atom_qkv, atom_proj,
        atom_bias, tok2d, tok_rows, rows * n_pb,
    )
    behind = lax.ppermute(msg, "pb", up)
    sums, counts = pool(pos, atom_out, agg_weight, tok2d, tok_rows)
    token_repr, normed = finish(behind, agg_weight, sums, counts, token_gain.reshape(1, -1))
    own_keys, other_keys = key_block(normed)
    scale = 1.0 / math.sqrt(token_q.shape[1] // TH)
    queries = (dot(normed, token_q) * scale).astype(BF16)
    parity = lax.rem(plane, 2).astype(jnp.int32)
    core = lax.rem(shard, n_pb // n_ka).astype(jnp.int32)
    k, v, near = attention(
        jnp.stack([1 - parity, core]), queries, pair_bias, (own_keys, other_keys, token_kv), True
    )
    got = lax.ppermute(near, "ka", [(i, i ^ 1) for i in range(n_ka)])
    o, lse = attention(jnp.stack([parity, core]), queries, pair_bias, (k, v), False)
    for bit in bits_of(n_ka)[1:]:
        o, lse, far = merge(o, lse, got)
        got = lax.ppermute(far, "ka", [(i, i ^ bit) for i in range(n_ka)])
    part = last_merge(parity.reshape(1), o, lse, got, token_repr, token_o)
    rest = lax.ppermute(part, "ka", [(i, i ^ 1) for i in range(n_ka)])
    return atom_out, join(parity.reshape(1), part, rest)


def solution(mesh):
    return jax.shard_map(
        body,
        mesh=mesh,
        in_specs=(
            P("pb", None),
            P(),
            P(),
            P(),
            P(None, "pb", None),
            P("pb"),
            P("pb"),
            P(),
            P(),
            P(),
            P(),
            P(),
            P(None, "pb", "ka"),
        ),
        out_specs=(P("pb", None), P("pb", None)),
        check_vma=False,
    )
```

```python
import functools
import math

import jax
import jax.numpy as jnp
from jax import lax
from jax.experimental import pallas as pl
from jax.experimental.pallas import tpu as pltpu
from jax.sharding import PartitionSpec as P

AH = 4
TH = 16
WIN_Q = 32
WIN_K = 128
SHIFT_MAX = 384
LANES = 128
F32 = jnp.float32
BF16 = jnp.bfloat16
VMEM_LIMIT = 56 * 1024 * 1024
VMEM_SMALL = 24 * 1024 * 1024


def full(shape):
    return pl.BlockSpec(shape, lambda *_: (0,) * len(shape))


def params(limit=VMEM_LIMIT):
    return pltpu.CompilerParams(vmem_limit_bytes=limit)


def norm_rows(as_float, gain):
    centre = jnp.mean(as_float, axis=-1, keepdims=True)
    spread = jnp.mean(jnp.square(as_float - centre), axis=-1, keepdims=True)
    return (as_float - centre) * lax.rsqrt(spread + 1e-05) * gain


def dot(a, b):
    return jnp.dot(a, b, preferred_element_type=F32)


def dot_nt(a, b):
    return lax.dot_general(a, b, (((1,), (1,)), ((), ())), preferred_element_type=F32)


def atom_kernel(
    chunks,
    atom_total,
    tok_rows,
    shift_ref,
    pos_ref,
    atoms_ref,
    left_ref,
    right_ref,
    gain_ref,
    qkv_ref,
    proj_ref,
    bias_ref,
    tok_ref,
    out_ref,
    msg_ref,
    q_s,
    k_s,
    v_s,
):
    step = pl.program_id(0)
    rows, width = atoms_ref.shape
    size = out_ref.shape[0]
    half = WIN_K // 2
    head = width // AH
    shard = pos_ref[0]

    @pl.when(step == 0)
    def _():
        gain = gain_ref[...]

        def project(values):
            normed = norm_rows(values.astype(F32), gain).astype(BF16)
            return dot(normed, qkv_ref[...])

        def keep(res, at, count):
            k_s[pl.ds(at, count), :] = res[:, width : 2 * width].astype(BF16)
            v_s[pl.ds(at, count), :width] = res[:, 2 * width :].astype(BF16)
            v_s[pl.ds(at, count), width:] = jnp.ones((count, width), BF16)

        def one(c, carry):
            at = pl.multiple_of(c * size, size)
            res = project(atoms_ref[pl.ds(at, size), :])
            q_s[pl.ds(at, size), :] = (res[:, :width] * (1.0 / math.sqrt(head))).astype(BF16)
            keep(res, pl.multiple_of(at + half, half), size)
            return carry

        lax.fori_loop(0, chunks, one, 0, unroll=2)
        keep(project(left_ref[...]), 0, half)
        keep(project(right_ref[...]), half + rows, half)

    group = WIN_K // WIN_Q
    atoms_group = group * WIN_Q
    lane_q = lax.broadcasted_iota(jnp.int32, (WIN_Q, width), 1)
    heads = [(lane_q >= h * head) & (lane_q < (h + 1) * head) for h in range(AH)]
    lane = lax.broadcasted_iota(jnp.int32, (AH * WIN_Q, WIN_K), 1)
    slot = lax.broadcasted_iota(jnp.int32, (1, WIN_K), 1)
    for g in range(size // atoms_group):
        local = g * atoms_group
        at = pl.multiple_of(step * size + local, atoms_group)
        keys = k_s[pl.ds(at, 2 * WIN_K), :]
        values = v_s[pl.ds(at, 2 * WIN_K), :]
        query = q_s[pl.ds(at, atoms_group), :].astype(F32)
        stacked = jnp.concatenate(
            [
                jnp.where(m, query[i * WIN_Q : (i + 1) * WIN_Q], 0.0).astype(BF16)
                for i in range(group)
                for m in heads
            ],
            axis=0,
        )
        scores = dot_nt(stacked, keys)
        weights = []
        for i in range(group):
            offset = i * WIN_Q + half + shift_ref[(step * size + local) // WIN_Q + i]
            early = lane >= offset
            span = AH * WIN_Q
            mine = scores[i * span : (i + 1) * span]
            begin = local + i * WIN_Q
            bias = bias_ref[:, begin : begin + WIN_Q, :].astype(F32).reshape(span, WIN_K)
            index = slot + jnp.where(slot >= offset, 0, WIN_K) + (at + shard * rows - half)
            shut = jnp.where((index >= 0) & (index < atom_total), 0.0, -jnp.inf)
            logits = jnp.where(early, mine[:, :WIN_K], mine[:, WIN_K:]) + (
                pltpu.roll(bias, jnp.bitwise_and(offset, WIN_K - 1), 1) + shut
            )
            terms = jnp.exp(logits - jnp.max(logits, axis=-1, keepdims=True))
            weights.append(
                jnp.concatenate(
                    [jnp.where(early, terms, 0.0).astype(BF16), jnp.where(early, 0.0, terms).astype(BF16)],
                    axis=1,
                )
            )
        mixed = dot(jnp.concatenate(weights, axis=0), values)
        merged = []
        for i in range(group):
            acc = None
            for h in range(AH):
                top = (i * AH + h) * WIN_Q
                part = mixed[top : top + WIN_Q]
                acc = part if acc is None else jnp.where(jnp.concatenate([heads[h]] * 2, axis=1), part, acc)
            merged.append((acc[:, :width] / acc[:, width:]).astype(BF16))
        own = atoms_ref[pl.ds(at, atoms_group), :].astype(F32)
        result = own + dot(jnp.concatenate(merged, axis=0), proj_ref[...])
        out_ref[local : local + atoms_group, :] = result.astype(BF16)

    @pl.when(step == chunks - 1)
    def _():
        ids = tok_ref[tok_ref.shape[0] - 8 :, :]
        code = jnp.maximum(ids - (shard + 1) * tok_rows + 1, 0)
        high = (code >> 4).astype(F32)
        low = (code & 15).astype(F32)
        msg_ref[:size, :] = out_ref[...]
        msg_ref[size:, :] = jnp.concatenate([high, low], axis=0).astype(BF16)


def atom_attention(shift, pos, atoms, left, right, gain, qkv, proj, bias, tok2d, tok_rows, atom_total):
    rows, width = atoms.shape
    size = SHIFT_MAX
    chunks = rows // size
    half = WIN_K // 2
    return pl.pallas_call(
        functools.partial(atom_kernel, chunks, atom_total, tok_rows),
        grid_spec=pltpu.PrefetchScalarGridSpec(
            num_scalar_prefetch=2,
            grid=(chunks,),
            in_specs=[
                full((rows, width)),
                full((half, width)),
                full((half, width)),
                full((1, width)),
                full(qkv.shape),
                full(proj.shape),
                pl.BlockSpec((AH, size, WIN_K), lambda i, *_: (0, i, 0)),
                full(tok2d.shape),
            ],
            out_specs=[
                pl.BlockSpec((size, width), lambda i, *_: (i, 0)),
                full((size + 16, width)),
            ],
            scratch_shapes=[
                pltpu.VMEM((rows, width), BF16),
                pltpu.VMEM((rows + 2 * half, width), BF16),
                pltpu.VMEM((rows + 2 * half, 2 * width), BF16),
            ],
        ),
        out_shape=[
            jax.ShapeDtypeStruct((rows, width), BF16),
            jax.ShapeDtypeStruct((size + 16, width), BF16),
        ],
        compiler_params=params(),
        cost_estimate=pl.CostEstimate(flops=8 * 10**9, bytes_accessed=6 * 10**6, transcendentals=2 * 10**6),
        name="atom_attention",
    )(shift, pos, atoms, left, right, gain, qkv, proj, bias, tok2d)


def activate(rows, weight_half):
    u = dot(rows, weight_half)
    return (u + u * jnp.tanh(u)).astype(BF16)


def pool_kernel(tok_rows, pos_ref, out_ref, weight_ref, tok_ref, sum_ref, cnt_ref):
    step = pl.program_id(0)
    size = out_ref.shape[0]
    lines = size // LANES
    base = pos_ref[0] * tok_rows
    token = lax.broadcasted_iota(jnp.int32, (tok_rows, LANES), 0)
    weight_half = (weight_ref[...].astype(F32) * 0.5).astype(BF16)
    hidden = activate(out_ref[...], weight_half)
    ones = []
    for j in range(lines):
        ids = tok_ref[pl.ds(step * lines + j, 1), :] - base
        ones.append(jnp.where(token == ids, 1.0, 0.0))
    hot = jnp.concatenate(ones, axis=1).astype(BF16)
    count = functools.reduce(jnp.add, ones)
    part = dot(hot, hidden)

    @pl.when(step == 0)
    def _():
        sum_ref[...] = part
        cnt_ref[...] = count

    @pl.when(step > 0)
    def _():
        sum_ref[...] += part
        cnt_ref[...] += count


def pool(pos, atom_out, weight, tok2d, tok_rows):
    rows, width = atom_out.shape
    feats = weight.shape[1]
    size = 512
    return pl.pallas_call(
        functools.partial(pool_kernel, tok_rows),
        grid_spec=pltpu.PrefetchScalarGridSpec(
            num_scalar_prefetch=1,
            grid=(rows // size,),
            in_specs=[
                pl.BlockSpec((size, width), lambda i, *_: (i, 0)),
                full(weight.shape),
                full(tok2d.shape),
            ],
            out_specs=[full((tok_rows, feats)), full((tok_rows, LANES))],
        ),
        out_shape=[
            jax.ShapeDtypeStruct((tok_rows, feats), F32),
            jax.ShapeDtypeStruct((tok_rows, LANES), F32),
        ],
        compiler_params=params(),
        cost_estimate=pl.CostEstimate(flops=4 * 10**9, bytes_accessed=3 * 10**6, transcendentals=2 * 10**6),
        name="pool",
    )(pos, atom_out, weight, tok2d)


def finish_kernel(msg_ref, weight_ref, sum_ref, cnt_ref, gain_ref, repr_ref, normed_ref):
    tok_rows = sum_ref.shape[0]
    size = msg_ref.shape[0] - 16
    lines = size // LANES
    token = lax.broadcasted_iota(jnp.int32, (tok_rows, LANES), 0).astype(F32)
    weight_half = (weight_ref[...].astype(F32) * 0.5).astype(BF16)
    hidden = activate(msg_ref[:size, :], weight_half)
    codes = msg_ref[size:, :].astype(F32)
    ids = codes[:8] * 16.0 + codes[8:] - 1.0
    ones = [jnp.where(token == ids[8 - lines + j : 9 - lines + j], 1.0, 0.0) for j in range(lines)]
    hot = jnp.concatenate(ones, axis=1).astype(BF16)
    count = functools.reduce(jnp.add, ones) + cnt_ref[...]
    sums = sum_ref[...] + dot(hot, hidden)
    token_repr = (sums / jnp.sum(count, axis=1, keepdims=True)).astype(BF16)
    repr_ref[...] = token_repr
    normed_ref[...] = norm_rows(token_repr.astype(F32), gain_ref[...]).astype(BF16)


def finish(msg, weight, sums, counts, gain):
    shape = sums.shape
    return pl.pallas_call(
        finish_kernel,
        out_shape=[jax.ShapeDtypeStruct(shape, BF16)] * 2,
        compiler_params=params(VMEM_SMALL),
        cost_estimate=pl.CostEstimate(flops=4 * 10**8, bytes_accessed=3 * 10**6, transcendentals=3 * 10**5),
        name="token_finish",
    )(msg, weight, sums, counts, gain)


HEADS_STEP = 8


def pack_lse(lse):
    lane = lax.broadcasted_iota(jnp.int32, lse.shape, 1)
    high = lse.astype(BF16).astype(F32)
    rest = lse - high
    middle = rest.astype(BF16).astype(F32)
    low = rest - middle
    return jnp.where(
        lane < TH,
        high,
        jnp.where(lane < 2 * TH, pltpu.roll(middle, TH, 1), pltpu.roll(low, 2 * TH, 1)),
    ).astype(BF16)


def unpack_lse(coded):
    value = coded.astype(F32)
    return value + pltpu.roll(value, LANES - TH, 1) + pltpu.roll(value, LANES - 2 * TH, 1)


def attend_step(step, half, q_ref, k_ref, v_ref, bias_ref, o_s, lse_s):
    rows = o_s.shape[0]
    width = q_ref.shape[1] // TH
    span = HEADS_STEP * width
    at = pl.multiple_of(half * rows, rows)
    spot = lax.broadcasted_iota(jnp.int32, (rows, LANES), 1)
    lse = lse_s[...]
    for p in range(HEADS_STEP // 2):
        first = 2 * p * width
        low = first // LANES * LANES
        wide = -(-(first + 2 * width) // LANES) * LANES - low
        first -= low
        free = 0 if first >= 16 else 2 * width
        window = pl.ds(pl.multiple_of(step * span + low, LANES), wide)
        lane = lax.broadcasted_iota(jnp.int32, (rows, wide), 1)
        masks = [(lane >= first + j * width) & (lane < first + (j + 1) * width) for j in range(2)]
        query = q_ref[pl.ds(at, rows), window].astype(F32)
        stacked = jnp.concatenate([jnp.where(m, query, 0.0).astype(BF16) for m in masks], axis=0)
        bias = bias_ref[2 * p : 2 * p + 2].astype(F32)
        scores = dot_nt(stacked, k_ref[:, window]) + bias.reshape(2 * rows, bias.shape[2])
        top = jnp.max(scores, axis=-1, keepdims=True)
        terms = jnp.exp(scores - top).astype(BF16)
        values = v_ref[:, window]
        column = lax.broadcasted_iota(jnp.int32, values.shape, 1)
        used = (column >= first) & (column < first + 2 * width)
        mixed = dot(terms, jnp.where(used, values.astype(F32), 1.0).astype(BF16))
        total = mixed[:, free : free + 1]
        mixed = mixed / total
        sums = top + jnp.log(total)
        result = o_s[:, window]
        for j in range(2):
            result = jnp.where(masks[j], mixed[j * rows : (j + 1) * rows], result)
            lse = jnp.where(spot == step * HEADS_STEP + 2 * p + j, sums[j * rows : (j + 1) * rows], lse)
        o_s[:, window] = result
    lse_s[...] = lse


def send_kernel(steps, half_ref, core_ref, q_ref, own_ref, other_ref, wkv_ref, bias_ref, k_ref, v_ref, msg_ref, o_s, lse_s, x_s):
    step = pl.program_id(0)
    rows, feats = own_ref.shape

    @pl.when(step == 0)
    def _():
        core = core_ref[0]
        x_s[pl.ds(pl.multiple_of(core * rows, rows), rows), :] = own_ref[...]
        x_s[pl.ds(pl.multiple_of((1 - core) * rows, rows), rows), :] = other_ref[...]
        for r in range(0, 2 * rows, rows):
            k_ref[r : r + rows, :] = dot(x_s[r : r + rows, :], wkv_ref[:, :feats]).astype(BF16)
            v_ref[r : r + rows, :] = dot(x_s[r : r + rows, :], wkv_ref[:, feats:]).astype(BF16)
        lse_s[...] = jnp.zeros_like(lse_s)

    attend_step(step, half_ref[0], q_ref, k_ref, v_ref, bias_ref, o_s, lse_s)

    @pl.when(step == steps - 1)
    def _():
        msg_ref[:, :feats] = o_s[...].astype(BF16)
        msg_ref[:, feats:] = pack_lse(lse_s[...])


def keep_kernel(half_ref, q_ref, k_ref, v_ref, bias_ref, o_ref, lse_ref):
    step = pl.program_id(0)

    @pl.when(step == 0)
    def _():
        lse_ref[...] = jnp.zeros_like(lse_ref)

    attend_step(step, half_ref[0], q_ref, k_ref, v_ref, bias_ref, o_ref, lse_ref)


def attention(half, q, bias, keys, first):
    tok_rows, feats = q.shape
    rows = tok_rows // 2
    key_rows = bias.shape[2]
    steps = TH // HEADS_STEP
    bias_spec = pl.BlockSpec((HEADS_STEP, rows, key_rows), lambda i, s, *_: (i, s[0], 0))
    kv_shape = (key_rows, feats)
    cost = pl.CostEstimate(flops=8 * 10**9, bytes_accessed=8 * 10**6, transcendentals=3 * 10**6)
    if first:
        core, own, other, wkv = keys
        return pl.pallas_call(
            functools.partial(send_kernel, steps),
            grid_spec=pltpu.PrefetchScalarGridSpec(
                num_scalar_prefetch=2,
                grid=(steps,),
                in_specs=[full(q.shape), full(own.shape), full(other.shape), full(wkv.shape), bias_spec],
                out_specs=[full(kv_shape), full(kv_shape), full((rows, feats + LANES))],
                scratch_shapes=[
                    pltpu.VMEM((rows, feats), F32),
                    pltpu.VMEM((rows, LANES), F32),
                    pltpu.VMEM(kv_shape, BF16),
                ],
            ),
            out_shape=[
                jax.ShapeDtypeStruct(kv_shape, BF16),
                jax.ShapeDtypeStruct(kv_shape, BF16),
                jax.ShapeDtypeStruct((rows, feats + LANES), BF16),
            ],
            compiler_params=params(),
            cost_estimate=cost,
            name="attend_send",
        )(half, core, q, own, other, wkv, bias)
    k, v = keys
    return pl.pallas_call(
        keep_kernel,
        grid_spec=pltpu.PrefetchScalarGridSpec(
            num_scalar_prefetch=1,
            grid=(steps,),
            in_specs=[full(q.shape), full(kv_shape), full(kv_shape), bias_spec],
            out_specs=[full((rows, feats)), full((rows, LANES))],
        ),
        out_shape=[
            jax.ShapeDtypeStruct((rows, feats), F32),
            jax.ShapeDtypeStruct((rows, LANES), F32),
        ],
        compiler_params=params(),
        cost_estimate=cost,
        name="attend_keep",
    )(half, q, k, v, bias)


def merged_rows(o_ref, lse_ref, msg_ref):
    rows, feats = o_ref.shape
    width = feats // TH
    other = msg_ref[:, :feats].astype(F32)
    lse_b = unpack_lse(msg_ref[:, feats:])
    spot = lax.broadcasted_iota(jnp.int32, (rows, LANES), 1)
    lse_a = lse_ref[...]
    lse_b = jnp.where(spot < TH, lse_b, lse_a)
    top = jnp.maximum(lse_a, lse_b)
    part_a = jnp.exp(lse_a - top)
    total = part_a + jnp.exp(lse_b - top)
    share = part_a / total
    high = share.astype(BF16)
    low = (share - high.astype(F32)).astype(BF16)
    head = lax.broadcasted_iota(jnp.int32, (LANES, feats), 0) * width
    column = lax.broadcasted_iota(jnp.int32, (LANES, feats), 1)
    spread = jnp.where((column >= head) & (column < head + width), 1.0, 0.0).astype(BF16)
    wide = dot(high, spread) + dot(low, spread)
    return other + wide * (o_ref[...] - other), top + jnp.log(total)


def merge_kernel(o_ref, lse_ref, msg_ref, out_ref, sum_ref, back_ref):
    mixed, lse = merged_rows(o_ref, lse_ref, msg_ref)
    feats = mixed.shape[1]
    out_ref[...] = mixed
    sum_ref[...] = lse
    back_ref[:, :feats] = mixed.astype(BF16)
    back_ref[:, feats:] = pack_lse(lse)


def merge(o, lse, msg):
    return pl.pallas_call(
        merge_kernel,
        out_shape=[
            jax.ShapeDtypeStruct(o.shape, F32),
            jax.ShapeDtypeStruct(lse.shape, F32),
            jax.ShapeDtypeStruct(msg.shape, BF16),
        ],
        compiler_params=params(VMEM_SMALL),
        name="merge",
    )(o, lse, msg)


def last_kernel(half_ref, o_ref, lse_ref, msg_ref, repr_ref, weight_ref, out_ref):
    rows = o_ref.shape[0]
    mixed, _ = merged_rows(o_ref, lse_ref, msg_ref)
    own = repr_ref[pl.ds(pl.multiple_of(half_ref[0] * rows, rows), rows), :].astype(F32)
    out_ref[...] = (own + dot(mixed.astype(BF16), weight_ref[...])).astype(BF16)


def last_merge(half, o, lse, msg, token_repr, weight):
    return pl.pallas_call(
        last_kernel,
        in_specs=[pl.BlockSpec(memory_space=pltpu.SMEM)] + [pl.BlockSpec(memory_space=pltpu.VMEM)] * 5,
        out_shape=jax.ShapeDtypeStruct(o.shape, BF16),
        compiler_params=params(VMEM_SMALL),
        name="merge_last",
    )(half, o, lse, msg, token_repr, weight)


def join_kernel(half_ref, own_ref, other_ref, out_ref):
    rows = own_ref.shape[0]
    out_ref[pl.ds(pl.multiple_of(half_ref[0] * rows, rows), rows), :] = own_ref[...]
    out_ref[pl.ds(pl.multiple_of((1 - half_ref[0]) * rows, rows), rows), :] = other_ref[...]


def join(half, own, other):
    rows, feats = own.shape
    return pl.pallas_call(
        join_kernel,
        in_specs=[pl.BlockSpec(memory_space=pltpu.SMEM)] + [pl.BlockSpec(memory_space=pltpu.VMEM)] * 2,
        out_shape=jax.ShapeDtypeStruct((2 * rows, feats), BF16),
        compiler_params=params(VMEM_SMALL),
        name="join",
    )(half, own, other)


def bits_of(count):
    return [1 << b for b in range(count.bit_length() - 1)]


def key_block(normed):
    n_pb, n_ka = lax.axis_size("pb"), lax.axis_size("ka")
    cores = n_pb // n_ka
    chips = n_pb // cores
    shard, plane = lax.axis_index("pb"), lax.axis_index("ka")
    bits = bits_of(chips)
    core = lax.rem(shard, cores)
    away = jnp.bitwise_xor(shard // cores, plane)
    held = normed
    for r in range(len(bits)):
        pairs = []
        gets = jnp.bool_(False)
        for c in range(cores):
            order = bits if c % 2 == 0 else bits[::-1]
            known = sum(order[:r])
            for k in range(n_ka):
                for j in range(chips):
                    if (j ^ k) & ~known == 0:
                        pairs.append(((j * cores + c) * n_ka + k, ((j ^ order[r]) * cores + c) * n_ka + k))
            fresh = (jnp.bitwise_and(away, ~(known + order[r])) == 0) & (jnp.bitwise_and(away, order[r]) != 0)
            gets = gets | (fresh & (core == c))
        moved = lax.ppermute(held, ("pb", "ka"), pairs)
        held = jnp.where(gets, moved, held)
    swap = [(p, p ^ 1) for p in range(n_pb)]
    return held, lax.ppermute(held, "pb", swap)


def body(
    atoms,
    atom_gain,
    atom_qkv,
    atom_proj,
    atom_bias,
    window_shift,
    token_of_atom,
    agg_weight,
    token_gain,
    token_q,
    token_kv,
    token_o,
    pair_bias,
):
    n_pb, n_ka = lax.axis_size("pb"), lax.axis_size("ka")
    shard, plane = lax.axis_index("pb"), lax.axis_index("ka")
    rows, width = atoms.shape
    tok_rows = pair_bias.shape[1]
    half = WIN_K // 2
    up = [(i, i + 1) for i in range(n_pb - 1)]
    down = [(i + 1, i) for i in range(n_pb - 1)]
    pos = shard.astype(jnp.int32).reshape(1)
    tok2d = token_of_atom.reshape(rows // LANES, LANES)
    left = lax.ppermute(atoms[rows - half :], "pb", up)
    right = lax.ppermute(atoms[:half], "pb", down)
    atom_out, msg = atom_attention(
        window_shift, pos, atoms, left, right, atom_gain.reshape(1, width), atom_qkv, atom_proj,
        atom_bias, tok2d, tok_rows, rows * n_pb,
    )
    behind = lax.ppermute(msg, "pb", up)
    sums, counts = pool(pos, atom_out, agg_weight, tok2d, tok_rows)
    token_repr, normed = finish(behind, agg_weight, sums, counts, token_gain.reshape(1, -1))
    own_keys, other_keys = key_block(normed)
    scale = 1.0 / math.sqrt(token_q.shape[1] // TH)
    queries = (dot(normed, token_q) * scale).astype(BF16)
    parity = lax.rem(plane, 2).astype(jnp.int32)
    core = lax.rem(shard, n_pb // n_ka).astype(jnp.int32)
    k, v, near = attention(
        (1 - parity).reshape(1), queries, pair_bias, (core.reshape(1), own_keys, other_keys, token_kv), True
    )
    got = lax.ppermute(near, "ka", [(i, i ^ 1) for i in range(n_ka)])
    o, lse = attention(parity.reshape(1), queries, pair_bias, (k, v), False)
    for bit in bits_of(n_ka)[1:]:
        o, lse, far = merge(o, lse, got)
        got = lax.ppermute(far, "ka", [(i, i ^ bit) for i in range(n_ka)])
    part = last_merge(parity.reshape(1), o, lse, got, token_repr, token_o)
    rest = lax.ppermute(part, "ka", [(i, i ^ 1) for i in range(n_ka)])
    return atom_out, join(parity.reshape(1), part, rest)


def solution(mesh):
    return jax.shard_map(
        body,
        mesh=mesh,
        in_specs=(
            P("pb", None),
            P(),
            P(),
            P(),
            P(None, "pb", None),
            P("pb"),
            P("pb"),
            P(),
            P(),
            P(),
            P(),
            P(),
            P(None, "pb", "ka"),
        ),
        out_specs=(P("pb", None), P("pb", None)),
        check_vma=False,
    )
```

```python
import functools
import math

import jax
import jax.numpy as jnp
from jax import lax
from jax.experimental import pallas as pl
from jax.experimental.pallas import tpu as pltpu
from jax.sharding import PartitionSpec as P

AH = 4
TH = 16
WIN_Q = 32
WIN_K = 128
SHIFT_MAX = 384
LANES = 128
F32 = jnp.float32
BF16 = jnp.bfloat16
VMEM_LIMIT = 56 * 1024 * 1024
VMEM_SMALL = 24 * 1024 * 1024


def full(shape):
    return pl.BlockSpec(shape, lambda *_: (0,) * len(shape))


def params(limit=VMEM_LIMIT):
    return pltpu.CompilerParams(vmem_limit_bytes=limit)


def norm_rows(as_float, gain):
    centre = jnp.mean(as_float, axis=-1, keepdims=True)
    spread = jnp.mean(jnp.square(as_float - centre), axis=-1, keepdims=True)
    return (as_float - centre) * lax.rsqrt(spread + 1e-05) * gain


def dot(a, b):
    return jnp.dot(a, b, preferred_element_type=F32)


def dot_nt(a, b):
    return lax.dot_general(a, b, (((1,), (1,)), ((), ())), preferred_element_type=F32)


def atom_kernel(
    chunks,
    atom_total,
    tok_rows,
    shift_ref,
    pos_ref,
    atoms_ref,
    left_ref,
    right_ref,
    gain_ref,
    qkv_ref,
    proj_ref,
    bias_ref,
    tok_ref,
    out_ref,
    msg_ref,
    q_s,
    k_s,
    v_s,
):
    step = pl.program_id(0)
    rows, width = atoms_ref.shape
    size = out_ref.shape[0]
    half = WIN_K // 2
    head = width // AH
    shard = pos_ref[0]

    @pl.when(step == 0)
    def _():
        gain = gain_ref[...].reshape(1, width)

        def project(values):
            normed = norm_rows(values.astype(F32), gain).astype(BF16)
            return dot(normed, qkv_ref[...])

        def keep(res, at, count):
            k_s[pl.ds(at, count), :] = res[:, width : 2 * width].astype(BF16)
            v_s[pl.ds(at, count), :width] = res[:, 2 * width :].astype(BF16)
            v_s[pl.ds(at, count), width:] = jnp.ones((count, width), BF16)

        def one(c, carry):
            at = pl.multiple_of(c * size, size)
            res = project(atoms_ref[pl.ds(at, size), :])
            q_s[pl.ds(at, size), :] = (res[:, :width] * (1.0 / math.sqrt(head))).astype(BF16)
            keep(res, pl.multiple_of(at + half, half), size)
            return carry

        lax.fori_loop(0, chunks, one, 0, unroll=2)
        keep(project(left_ref[...]), 0, half)
        keep(project(right_ref[...]), half + rows, half)

    group = WIN_K // WIN_Q
    atoms_group = group * WIN_Q
    lane_q = lax.broadcasted_iota(jnp.int32, (WIN_Q, width), 1)
    heads = [(lane_q >= h * head) & (lane_q < (h + 1) * head) for h in range(AH)]
    lane = lax.broadcasted_iota(jnp.int32, (AH * WIN_Q, WIN_K), 1)
    slot = lax.broadcasted_iota(jnp.int32, (1, WIN_K), 1)
    for g in range(size // atoms_group):
        local = g * atoms_group
        at = pl.multiple_of(step * size + local, atoms_group)
        keys = k_s[pl.ds(at, 2 * WIN_K), :]
        values = v_s[pl.ds(at, 2 * WIN_K), :]
        query = q_s[pl.ds(at, atoms_group), :].astype(F32)
        stacked = jnp.concatenate(
            [
                jnp.where(m, query[i * WIN_Q : (i + 1) * WIN_Q], 0.0).astype(BF16)
                for i in range(group)
                for m in heads
            ],
            axis=0,
        )
        scores = dot_nt(stacked, keys)
        weights = []
        for i in range(group):
            offset = i * WIN_Q + half + shift_ref[(step * size + local) // WIN_Q + i]
            early = lane >= offset
            span = AH * WIN_Q
            mine = scores[i * span : (i + 1) * span]
            begin = local + i * WIN_Q
            bias = bias_ref[:, begin : begin + WIN_Q, :].astype(F32).reshape(span, WIN_K)
            index = slot + jnp.where(slot >= offset, 0, WIN_K) + (at + shard * rows - half)
            shut = jnp.where((index >= 0) & (index < atom_total), 0.0, -jnp.inf)
            logits = jnp.where(early, mine[:, :WIN_K], mine[:, WIN_K:]) + (
                pltpu.roll(bias, jnp.bitwise_and(offset, WIN_K - 1), 1) + shut
            )
            terms = jnp.exp(logits - jnp.max(logits, axis=-1, keepdims=True))
            weights.append(
                jnp.concatenate(
                    [jnp.where(early, terms, 0.0).astype(BF16), jnp.where(early, 0.0, terms).astype(BF16)],
                    axis=1,
                )
            )
        mixed = dot(jnp.concatenate(weights, axis=0), values)
        merged = []
        for i in range(group):
            acc = None
            for h in range(AH):
                top = (i * AH + h) * WIN_Q
                part = mixed[top : top + WIN_Q]
                acc = part if acc is None else jnp.where(jnp.concatenate([heads[h]] * 2, axis=1), part, acc)
            merged.append((acc[:, :width] / acc[:, width:]).astype(BF16))
        own = atoms_ref[pl.ds(at, atoms_group), :].astype(F32)
        result = own + dot(jnp.concatenate(merged, axis=0), proj_ref[...])
        out_ref[local : local + atoms_group, :] = result.astype(BF16)

    @pl.when(step == chunks - 1)
    def _():
        ids = tok_ref[tok_ref.shape[0] - 8 :, :]
        code = jnp.maximum(ids - (shard + 1) * tok_rows + 1, 0)
        high = (code >> 4).astype(F32)
        low = (code & 15).astype(F32)
        msg_ref[:size, :] = out_ref[...]
        msg_ref[size:, :] = jnp.concatenate([high, low], axis=0).astype(BF16)


def atom_attention(shift, pos, atoms, left, right, gain, qkv, proj, bias, tok2d, tok_rows, atom_total):
    rows, width = atoms.shape
    size = SHIFT_MAX
    chunks = rows // size
    half = WIN_K // 2
    return pl.pallas_call(
        functools.partial(atom_kernel, chunks, atom_total, tok_rows),
        grid_spec=pltpu.PrefetchScalarGridSpec(
            num_scalar_prefetch=2,
            grid=(chunks,),
            in_specs=[
                full((rows, width)),
                full((half, width)),
                full((half, width)),
                full((width,)),
                full(qkv.shape),
                full(proj.shape),
                pl.BlockSpec((AH, size, WIN_K), lambda i, *_: (0, i, 0)),
                full(tok2d.shape),
            ],
            out_specs=[
                pl.BlockSpec((size, width), lambda i, *_: (i, 0)),
                full((size + 16, width)),
            ],
            scratch_shapes=[
                pltpu.VMEM((rows, width), BF16),
                pltpu.VMEM((rows + 2 * half, width), BF16),
                pltpu.VMEM((rows + 2 * half, 2 * width), BF16),
            ],
        ),
        out_shape=[
            jax.ShapeDtypeStruct((rows, width), BF16),
            jax.ShapeDtypeStruct((size + 16, width), BF16),
        ],
        compiler_params=params(),
        cost_estimate=pl.CostEstimate(flops=8 * 10**9, bytes_accessed=6 * 10**6, transcendentals=2 * 10**6),
        name="atom_attention",
    )(shift, pos, atoms, left, right, gain, qkv, proj, bias, tok2d)


def activate(rows, weight_half):
    u = dot(rows, weight_half)
    return (u + u * jnp.tanh(u)).astype(BF16)


def pool_kernel(tok_rows, pos_ref, out_ref, weight_ref, tok_ref, sum_ref, cnt_ref):
    step = pl.program_id(0)
    size = out_ref.shape[0]
    lines = size // LANES
    base = pos_ref[0] * tok_rows
    token = lax.broadcasted_iota(jnp.int32, (tok_rows, LANES), 0)
    weight_half = (weight_ref[...].astype(F32) * 0.5).astype(BF16)
    hidden = activate(out_ref[...], weight_half)
    ones = []
    for j in range(lines):
        ids = tok_ref[pl.ds(step * lines + j, 1), :] - base
        ones.append(jnp.where(token == ids, 1.0, 0.0))
    hot = jnp.concatenate(ones, axis=1).astype(BF16)
    count = functools.reduce(jnp.add, ones)
    part = dot(hot, hidden)

    @pl.when(step == 0)
    def _():
        sum_ref[...] = part
        cnt_ref[...] = count

    @pl.when(step > 0)
    def _():
        sum_ref[...] += part
        cnt_ref[...] += count


def pool(pos, atom_out, weight, tok2d, tok_rows):
    rows, width = atom_out.shape
    feats = weight.shape[1]
    size = 512
    return pl.pallas_call(
        functools.partial(pool_kernel, tok_rows),
        grid_spec=pltpu.PrefetchScalarGridSpec(
            num_scalar_prefetch=1,
            grid=(rows // size,),
            in_specs=[
                pl.BlockSpec((size, width), lambda i, *_: (i, 0)),
                full(weight.shape),
                full(tok2d.shape),
            ],
            out_specs=[full((tok_rows, feats)), full((tok_rows, LANES))],
        ),
        out_shape=[
            jax.ShapeDtypeStruct((tok_rows, feats), F32),
            jax.ShapeDtypeStruct((tok_rows, LANES), F32),
        ],
        compiler_params=params(),
        cost_estimate=pl.CostEstimate(flops=4 * 10**9, bytes_accessed=3 * 10**6, transcendentals=2 * 10**6),
        name="pool",
    )(pos, atom_out, weight, tok2d)


def finish_kernel(msg_ref, weight_ref, sum_ref, cnt_ref, gain_ref, repr_ref, normed_ref):
    tok_rows = sum_ref.shape[0]
    size = msg_ref.shape[0] - 16
    lines = size // LANES
    token = lax.broadcasted_iota(jnp.int32, (tok_rows, LANES), 0).astype(F32)
    weight_half = (weight_ref[...].astype(F32) * 0.5).astype(BF16)
    hidden = activate(msg_ref[:size, :], weight_half)
    codes = msg_ref[size:, :].astype(F32)
    ids = codes[:8] * 16.0 + codes[8:] - 1.0
    ones = [jnp.where(token == ids[8 - lines + j : 9 - lines + j], 1.0, 0.0) for j in range(lines)]
    hot = jnp.concatenate(ones, axis=1).astype(BF16)
    count = functools.reduce(jnp.add, ones) + cnt_ref[...]
    sums = sum_ref[...] + dot(hot, hidden)
    token_repr = (sums / jnp.sum(count, axis=1, keepdims=True)).astype(BF16)
    repr_ref[...] = token_repr
    normed_ref[...] = norm_rows(token_repr.astype(F32), gain_ref[...].reshape(1, -1)).astype(BF16)


def finish(msg, weight, sums, counts, gain):
    shape = sums.shape
    return pl.pallas_call(
        finish_kernel,
        out_shape=[jax.ShapeDtypeStruct(shape, BF16)] * 2,
        compiler_params=params(VMEM_SMALL),
        cost_estimate=pl.CostEstimate(flops=4 * 10**8, bytes_accessed=3 * 10**6, transcendentals=3 * 10**5),
        name="token_finish",
    )(msg, weight, sums, counts, gain)


HEADS_STEP = 8


def pack_lse(lse):
    lane = lax.broadcasted_iota(jnp.int32, lse.shape, 1)
    high = lse.astype(BF16).astype(F32)
    rest = lse - high
    middle = rest.astype(BF16).astype(F32)
    low = rest - middle
    return jnp.where(
        lane < TH,
        high,
        jnp.where(lane < 2 * TH, pltpu.roll(middle, TH, 1), pltpu.roll(low, 2 * TH, 1)),
    ).astype(BF16)


def unpack_lse(coded):
    value = coded.astype(F32)
    return value + pltpu.roll(value, LANES - TH, 1) + pltpu.roll(value, LANES - 2 * TH, 1)


ROW_TILE = 32


def attend_step(step, half, q_ref, k_ref, v_ref, bias_ref, o_s, lse_s, work):
    rows = o_s.shape[0]
    width = q_ref.shape[1] // TH
    span = HEADS_STEP * width
    at = pl.multiple_of(half * rows, rows)
    spot = lax.broadcasted_iota(jnp.int32, (rows, LANES), 1)
    pairs = HEADS_STEP // 2
    score_s, term_s, top_s = work[:2], work[2:4], work[4:]

    def layout(p):
        first = 2 * p * width
        low = first // LANES * LANES
        wide = -(-(first + 2 * width) // LANES) * LANES - low
        lane = lax.broadcasted_iota(jnp.int32, (rows, wide), 1)
        first -= low
        masks = [(lane >= first + j * width) & (lane < first + (j + 1) * width) for j in range(2)]
        return pl.ds(pl.multiple_of(step * span + low, LANES), wide), first, masks

    def score(p):
        window, _, masks = layout(p)
        query = q_ref[pl.ds(at, rows), window].astype(F32)
        stacked = jnp.concatenate([jnp.where(m, query, 0.0).astype(BF16) for m in masks], axis=0)
        score_s[p % 2][...] = dot_nt(stacked, k_ref[:, window])

    def soften(p):
        for r in range(0, 2 * rows, ROW_TILE):
            bias = bias_ref[2 * p + r // rows, r % rows : r % rows + ROW_TILE, :].astype(F32)
            scores = score_s[p % 2][r : r + ROW_TILE, :] + bias
            top = jnp.max(scores, axis=-1, keepdims=True)
            term_s[p % 2][r : r + ROW_TILE, :] = jnp.exp(scores - top).astype(BF16)
            top_s[p % 2][r : r + ROW_TILE, :] = jnp.broadcast_to(top, (ROW_TILE, LANES))

    def mix(p):
        window, first, masks = layout(p)
        values = v_ref[:, window]
        column = lax.broadcasted_iota(jnp.int32, values.shape, 1)
        used = (column >= first) & (column < first + 2 * width)
        mixed = dot(term_s[p % 2][...], jnp.where(used, values.astype(F32), 1.0).astype(BF16))
        free = 0 if first >= 16 else 2 * width
        total = mixed[:, free : free + 1]
        mixed = mixed / total
        sums = top_s[p % 2][...] + jnp.log(total)
        result = o_s[:, window]
        lse = lse_s[...]
        for j in range(2):
            result = jnp.where(masks[j], mixed[j * rows : (j + 1) * rows], result)
            lse = jnp.where(spot == step * HEADS_STEP + 2 * p + j, sums[j * rows : (j + 1) * rows], lse)
        o_s[:, window] = result
        lse_s[...] = lse

    score(0)
    for p in range(pairs):
        if p + 1 < pairs:
            score(p + 1)
        soften(p)
        mix(p)


def work_scratch(rows, keys):
    return (
        [pltpu.VMEM((2 * rows, keys), F32)] * 2
        + [pltpu.VMEM((2 * rows, keys), BF16)] * 2
        + [pltpu.VMEM((2 * rows, LANES), F32)] * 2
    )


def send_kernel(steps, half_ref, core_ref, q_ref, own_ref, other_ref, wkv_ref, bias_ref, k_ref, v_ref, msg_ref, o_s, lse_s, x_s, *work):
    step = pl.program_id(0)
    rows, feats = own_ref.shape

    @pl.when(step == 0)
    def _():
        core = core_ref[0]
        x_s[pl.ds(pl.multiple_of(core * rows, rows), rows), :] = own_ref[...]
        x_s[pl.ds(pl.multiple_of((1 - core) * rows, rows), rows), :] = other_ref[...]
        for r in range(0, 2 * rows, rows):
            k_ref[r : r + rows, :] = dot(x_s[r : r + rows, :], wkv_ref[:, :feats]).astype(BF16)
            v_ref[r : r + rows, :] = dot(x_s[r : r + rows, :], wkv_ref[:, feats:]).astype(BF16)
        lse_s[...] = jnp.zeros_like(lse_s)

    attend_step(step, half_ref[0], q_ref, k_ref, v_ref, bias_ref, o_s, lse_s, work)

    @pl.when(step == steps - 1)
    def _():
        msg_ref[:, :feats] = o_s[...].astype(BF16)
        msg_ref[:, feats:] = pack_lse(lse_s[...])


def keep_kernel(half_ref, q_ref, k_ref, v_ref, bias_ref, o_ref, lse_ref, *work):
    step = pl.program_id(0)

    @pl.when(step == 0)
    def _():
        lse_ref[...] = jnp.zeros_like(lse_ref)

    attend_step(step, half_ref[0], q_ref, k_ref, v_ref, bias_ref, o_ref, lse_ref, work)


def attention(half, q, bias, keys, first):
    tok_rows, feats = q.shape
    rows = tok_rows // 2
    key_rows = bias.shape[2]
    steps = TH // HEADS_STEP
    bias_spec = pl.BlockSpec((HEADS_STEP, rows, key_rows), lambda i, s, *_: (i, s[0], 0))
    kv_shape = (key_rows, feats)
    cost = pl.CostEstimate(flops=8 * 10**9, bytes_accessed=8 * 10**6, transcendentals=3 * 10**6)
    if first:
        core, own, other, wkv = keys
        return pl.pallas_call(
            functools.partial(send_kernel, steps),
            grid_spec=pltpu.PrefetchScalarGridSpec(
                num_scalar_prefetch=2,
                grid=(steps,),
                in_specs=[full(q.shape), full(own.shape), full(other.shape), full(wkv.shape), bias_spec],
                out_specs=[full(kv_shape), full(kv_shape), full((rows, feats + LANES))],
                scratch_shapes=[
                    pltpu.VMEM((rows, feats), F32),
                    pltpu.VMEM((rows, LANES), F32),
                    pltpu.VMEM(kv_shape, BF16),
                    *work_scratch(rows, key_rows),
                ],
            ),
            out_shape=[
                jax.ShapeDtypeStruct(kv_shape, BF16),
                jax.ShapeDtypeStruct(kv_shape, BF16),
                jax.ShapeDtypeStruct((rows, feats + LANES), BF16),
            ],
            compiler_params=params(),
            cost_estimate=cost,
            name="attend_send",
        )(half, core, q, own, other, wkv, bias)
    k, v = keys
    return pl.pallas_call(
        keep_kernel,
        grid_spec=pltpu.PrefetchScalarGridSpec(
            num_scalar_prefetch=1,
            grid=(steps,),
            in_specs=[full(q.shape), full(kv_shape), full(kv_shape), bias_spec],
            out_specs=[full((rows, feats)), full((rows, LANES))],
            scratch_shapes=work_scratch(rows, key_rows),
        ),
        out_shape=[
            jax.ShapeDtypeStruct((rows, feats), F32),
            jax.ShapeDtypeStruct((rows, LANES), F32),
        ],
        compiler_params=params(),
        cost_estimate=cost,
        name="attend_keep",
    )(half, q, k, v, bias)


def merged_rows(o_ref, lse_ref, msg_ref):
    rows, feats = o_ref.shape
    width = feats // TH
    other = msg_ref[:, :feats].astype(F32)
    lse_b = unpack_lse(msg_ref[:, feats:])
    spot = lax.broadcasted_iota(jnp.int32, (rows, LANES), 1)
    lse_a = lse_ref[...]
    lse_b = jnp.where(spot < TH, lse_b, lse_a)
    top = jnp.maximum(lse_a, lse_b)
    part_a = jnp.exp(lse_a - top)
    total = part_a + jnp.exp(lse_b - top)
    share = part_a / total
    high = share.astype(BF16)
    low = (share - high.astype(F32)).astype(BF16)
    head = lax.broadcasted_iota(jnp.int32, (LANES, feats), 0) * width
    column = lax.broadcasted_iota(jnp.int32, (LANES, feats), 1)
    spread = jnp.where((column >= head) & (column < head + width), 1.0, 0.0).astype(BF16)
    wide = dot(high, spread) + dot(low, spread)
    return other + wide * (o_ref[...] - other), top + jnp.log(total)


def merge_kernel(o_ref, lse_ref, msg_ref, out_ref, sum_ref, back_ref):
    mixed, lse = merged_rows(o_ref, lse_ref, msg_ref)
    feats = mixed.shape[1]
    out_ref[...] = mixed
    sum_ref[...] = lse
    back_ref[:, :feats] = mixed.astype(BF16)
    back_ref[:, feats:] = pack_lse(lse)


def merge(o, lse, msg):
    return pl.pallas_call(
        merge_kernel,
        out_shape=[
            jax.ShapeDtypeStruct(o.shape, F32),
            jax.ShapeDtypeStruct(lse.shape, F32),
            jax.ShapeDtypeStruct(msg.shape, BF16),
        ],
        compiler_params=params(VMEM_SMALL),
        name="merge",
    )(o, lse, msg)


def last_kernel(half_ref, o_ref, lse_ref, msg_ref, repr_ref, weight_ref, out_ref):
    rows = o_ref.shape[0]
    mixed, _ = merged_rows(o_ref, lse_ref, msg_ref)
    own = repr_ref[pl.ds(pl.multiple_of(half_ref[0] * rows, rows), rows), :].astype(F32)
    out_ref[...] = (own + dot(mixed.astype(BF16), weight_ref[...])).astype(BF16)


def last_merge(half, o, lse, msg, token_repr, weight):
    return pl.pallas_call(
        last_kernel,
        in_specs=[pl.BlockSpec(memory_space=pltpu.SMEM)] + [pl.BlockSpec(memory_space=pltpu.VMEM)] * 5,
        out_shape=jax.ShapeDtypeStruct(o.shape, BF16),
        compiler_params=params(VMEM_SMALL),
        name="merge_last",
    )(half, o, lse, msg, token_repr, weight)


def join_kernel(half_ref, own_ref, other_ref, out_ref):
    rows = own_ref.shape[0]
    out_ref[pl.ds(pl.multiple_of(half_ref[0] * rows, rows), rows), :] = own_ref[...]
    out_ref[pl.ds(pl.multiple_of((1 - half_ref[0]) * rows, rows), rows), :] = other_ref[...]


def join(half, own, other):
    rows, feats = own.shape
    return pl.pallas_call(
        join_kernel,
        in_specs=[pl.BlockSpec(memory_space=pltpu.SMEM)] + [pl.BlockSpec(memory_space=pltpu.VMEM)] * 2,
        out_shape=jax.ShapeDtypeStruct((2 * rows, feats), BF16),
        compiler_params=params(VMEM_SMALL),
        name="join",
    )(half, own, other)


def bits_of(count):
    return [1 << b for b in range(count.bit_length() - 1)]


def key_block(normed):
    n_pb, n_ka = lax.axis_size("pb"), lax.axis_size("ka")
    cores = n_pb // n_ka
    chips = n_pb // cores
    shard, plane = lax.axis_index("pb"), lax.axis_index("ka")
    bits = bits_of(chips)
    core = lax.rem(shard, cores)
    away = jnp.bitwise_xor(shard // cores, plane)
    held = normed
    for r in range(len(bits)):
        pairs = []
        gets = jnp.bool_(False)
        for c in range(cores):
            order = bits if c % 2 == 0 else bits[::-1]
            known = sum(order[:r])
            for k in range(n_ka):
                for j in range(chips):
                    if (j ^ k) & ~known == 0:
                        pairs.append(((j * cores + c) * n_ka + k, ((j ^ order[r]) * cores + c) * n_ka + k))
            fresh = (jnp.bitwise_and(away, ~(known + order[r])) == 0) & (jnp.bitwise_and(away, order[r]) != 0)
            gets = gets | (fresh & (core == c))
        moved = lax.ppermute(held, ("pb", "ka"), pairs)
        held = jnp.where(gets, moved, held)
    swap = [(p, p ^ 1) for p in range(n_pb)]
    return held, lax.ppermute(held, "pb", swap)


def body(
    atoms,
    atom_gain,
    atom_qkv,
    atom_proj,
    atom_bias,
    window_shift,
    token_of_atom,
    agg_weight,
    token_gain,
    token_q,
    token_kv,
    token_o,
    pair_bias,
):
    n_pb, n_ka = lax.axis_size("pb"), lax.axis_size("ka")
    shard, plane = lax.axis_index("pb"), lax.axis_index("ka")
    rows, width = atoms.shape
    tok_rows = pair_bias.shape[1]
    half = WIN_K // 2
    up = [(i, i + 1) for i in range(n_pb - 1)]
    down = [(i + 1, i) for i in range(n_pb - 1)]
    pos = shard.astype(jnp.int32).reshape(1)
    tok2d = token_of_atom.reshape(rows // LANES, LANES)
    left = lax.ppermute(atoms[rows - half :], "pb", up)
    right = lax.ppermute(atoms[:half], "pb", down)
    atom_out, msg = atom_attention(
        window_shift, pos, atoms, left, right, atom_gain, atom_qkv, atom_proj,
        atom_bias, tok2d, tok_rows, rows * n_pb,
    )
    behind = lax.ppermute(msg, "pb", up)
    sums, counts = pool(pos, atom_out, agg_weight, tok2d, tok_rows)
    token_repr, normed = finish(behind, agg_weight, sums, counts, token_gain)
    own_keys, other_keys = key_block(normed)
    scale = 1.0 / math.sqrt(token_q.shape[1] // TH)
    queries = (dot(normed, token_q) * scale).astype(BF16)
    parity = jnp.bitwise_and(plane ^ (plane >> 1), 1).astype(jnp.int32)
    core = lax.rem(shard, n_pb // n_ka).astype(jnp.int32)
    k, v, near = attention(
        (1 - parity).reshape(1), queries, pair_bias, (core.reshape(1), own_keys, other_keys, token_kv), True
    )
    got = lax.ppermute(near, "ka", [(i, i ^ 1) for i in range(n_ka)])
    o, lse = attention(parity.reshape(1), queries, pair_bias, (k, v), False)
    for bit in bits_of(n_ka)[1:]:
        o, lse, far = merge(o, lse, got)
        got = lax.ppermute(far, "ka", [(i, i ^ (2 * bit - 1)) for i in range(n_ka)])
    part = last_merge(parity.reshape(1), o, lse, got, token_repr, token_o)
    rest = lax.ppermute(part, "ka", [(i, i ^ 1) for i in range(n_ka)])
    return atom_out, join(parity.reshape(1), part, rest)


def solution(mesh):
    return jax.shard_map(
        body,
        mesh=mesh,
        in_specs=(
            P("pb", None),
            P(),
            P(),
            P(),
            P(None, "pb", None),
            P("pb"),
            P("pb"),
            P(),
            P(),
            P(),
            P(),
            P(),
            P(None, "pb", "ka"),
        ),
        out_specs=(P("pb", None), P("pb", None)),
        check_vma=False,
    )
```

```python
import functools
import math

import jax
import jax.numpy as jnp
from jax import lax
from jax.experimental import pallas as pl
from jax.experimental.pallas import tpu as pltpu
from jax.sharding import PartitionSpec as P

AH = 4
TH = 16
WIN_Q = 32
WIN_K = 128
SHIFT_MAX = 384
PARTS = 2
LANES = 128
F32 = jnp.float32
BF16 = jnp.bfloat16
VMEM_LIMIT = 56 * 1024 * 1024
VMEM_SMALL = 24 * 1024 * 1024


def full(shape):
    return pl.BlockSpec(shape, lambda *_: (0,) * len(shape))


def params(limit=VMEM_LIMIT):
    return pltpu.CompilerParams(vmem_limit_bytes=limit)


def norm_rows(as_float, gain):
    centre = jnp.mean(as_float, axis=-1, keepdims=True)
    spread = jnp.mean(jnp.square(as_float - centre), axis=-1, keepdims=True)
    return (as_float - centre) * lax.rsqrt(spread + 1e-05) * gain


def dot(a, b):
    return jnp.dot(a, b, preferred_element_type=F32)


def dot_nt(a, b):
    return lax.dot_general(a, b, (((1,), (1,)), ((), ())), preferred_element_type=F32)


def atom_kernel(
    chunks,
    atom_total,
    tok_rows,
    shift_ref,
    pos_ref,
    atoms_ref,
    left_ref,
    right_ref,
    gain_ref,
    qkv_ref,
    proj_ref,
    bias_ref,
    tok_ref,
    out_ref,
    msg_ref,
    q_s,
    k_s,
    v_s,
):
    step = pl.program_id(0)
    rows, width = atoms_ref.shape
    size = out_ref.shape[0]
    half = WIN_K // 2
    head = width // AH
    shard = pos_ref[0]

    @pl.when(step == 0)
    def _():
        gain = gain_ref[...].reshape(1, width)

        def project(values):
            normed = norm_rows(values.astype(F32), gain).astype(BF16)
            return dot(normed, qkv_ref[...])

        def keep(res, at, count):
            k_s[pl.ds(at, count), :] = res[:, width : 2 * width].astype(BF16)
            v_s[pl.ds(at, count), :width] = res[:, 2 * width :].astype(BF16)
            v_s[pl.ds(at, count), width:] = jnp.ones((count, width), BF16)

        def one(c, carry):
            at = pl.multiple_of(c * size, size)
            res = project(atoms_ref[pl.ds(at, size), :])
            q_s[pl.ds(at, size), :] = (res[:, :width] * (1.0 / math.sqrt(head))).astype(BF16)
            keep(res, pl.multiple_of(at + half, half), size)
            return carry

        lax.fori_loop(0, chunks, one, 0, unroll=2)
        keep(project(left_ref[...]), 0, half)
        keep(project(right_ref[...]), half + rows, half)

    group = WIN_K // WIN_Q
    atoms_group = group * WIN_Q
    lane_q = lax.broadcasted_iota(jnp.int32, (WIN_Q, width), 1)
    heads = [(lane_q >= h * head) & (lane_q < (h + 1) * head) for h in range(AH)]
    lane = lax.broadcasted_iota(jnp.int32, (AH * WIN_Q, WIN_K), 1)
    slot = lax.broadcasted_iota(jnp.int32, (1, WIN_K), 1)
    for g in range(size // atoms_group):
        local = g * atoms_group
        at = pl.multiple_of(step * size + local, atoms_group)
        keys = k_s[pl.ds(at, 2 * WIN_K), :]
        values = v_s[pl.ds(at, 2 * WIN_K), :]
        query = q_s[pl.ds(at, atoms_group), :].astype(F32)
        stacked = jnp.concatenate(
            [
                jnp.where(m, query[i * WIN_Q : (i + 1) * WIN_Q], 0.0).astype(BF16)
                for i in range(group)
                for m in heads
            ],
            axis=0,
        )
        scores = dot_nt(stacked, keys)
        weights = []
        for i in range(group):
            offset = i * WIN_Q + half + shift_ref[(step * size + local) // WIN_Q + i]
            early = lane >= offset
            span = AH * WIN_Q
            mine = scores[i * span : (i + 1) * span]
            begin = local + i * WIN_Q
            bias = bias_ref[:, begin : begin + WIN_Q, :].astype(F32).reshape(span, WIN_K)
            index = slot + jnp.where(slot >= offset, 0, WIN_K) + (at + shard * rows - half)
            shut = jnp.where((index >= 0) & (index < atom_total), 0.0, -jnp.inf)
            logits = jnp.where(early, mine[:, :WIN_K], mine[:, WIN_K:]) + (
                pltpu.roll(bias, jnp.bitwise_and(offset, WIN_K - 1), 1) + shut
            )
            terms = jnp.exp(logits - jnp.max(logits, axis=-1, keepdims=True))
            weights.append(
                jnp.concatenate(
                    [jnp.where(early, terms, 0.0).astype(BF16), jnp.where(early, 0.0, terms).astype(BF16)],
                    axis=1,
                )
            )
        mixed = dot(jnp.concatenate(weights, axis=0), values)
        merged = []
        for i in range(group):
            acc = None
            for h in range(AH):
                top = (i * AH + h) * WIN_Q
                part = mixed[top : top + WIN_Q]
                acc = part if acc is None else jnp.where(jnp.concatenate([heads[h]] * 2, axis=1), part, acc)
            merged.append((acc[:, :width] / acc[:, width:]).astype(BF16))
        own = atoms_ref[pl.ds(at, atoms_group), :].astype(F32)
        result = own + dot(jnp.concatenate(merged, axis=0), proj_ref[...])
        out_ref[local : local + atoms_group, :] = result.astype(BF16)

    @pl.when(step == chunks - 1)
    def _():
        ids = tok_ref[tok_ref.shape[0] - 8 :, :]
        code = jnp.maximum(ids - (shard + 1) * tok_rows + 1, 0)
        high = (code >> 4).astype(F32)
        low = (code & 15).astype(F32)
        msg_ref[:size, :] = out_ref[...]
        msg_ref[size:, :] = jnp.concatenate([high, low], axis=0).astype(BF16)


def atom_attention(shift, pos, atoms, left, right, gain, qkv, proj, bias, tok2d, tok_rows, atom_total):
    rows, width = atoms.shape
    size = SHIFT_MAX
    chunks = rows // size
    half = WIN_K // 2
    return pl.pallas_call(
        functools.partial(atom_kernel, chunks, atom_total, tok_rows),
        grid_spec=pltpu.PrefetchScalarGridSpec(
            num_scalar_prefetch=2,
            grid=(chunks,),
            in_specs=[
                full((rows, width)),
                full((half, width)),
                full((half, width)),
                full((width,)),
                full(qkv.shape),
                full(proj.shape),
                pl.BlockSpec((AH, size, WIN_K), lambda i, *_: (0, i, 0)),
                full(tok2d.shape),
            ],
            out_specs=[
                pl.BlockSpec((size, width), lambda i, *_: (i, 0)),
                full((size + 16, width)),
            ],
            scratch_shapes=[
                pltpu.VMEM((rows, width), BF16),
                pltpu.VMEM((rows + 2 * half, width), BF16),
                pltpu.VMEM((rows + 2 * half, 2 * width), BF16),
            ],
        ),
        out_shape=[
            jax.ShapeDtypeStruct((rows, width), BF16),
            jax.ShapeDtypeStruct((size + 16, width), BF16),
        ],
        compiler_params=params(),
        cost_estimate=pl.CostEstimate(flops=8 * 10**9, bytes_accessed=6 * 10**6, transcendentals=2 * 10**6),
        name="atom_attention",
    )(shift, pos, atoms, left, right, gain, qkv, proj, bias, tok2d)


def activate(rows, weight_half):
    u = dot(rows, weight_half)
    return (u + u * jnp.tanh(u)).astype(BF16)


def pool_kernel(tok_rows, pos_ref, out_ref, weight_ref, tok_ref, sum_ref, cnt_ref):
    step = pl.program_id(0)
    size = out_ref.shape[0]
    lines = size // LANES
    base = pos_ref[0] * tok_rows
    token = lax.broadcasted_iota(jnp.int32, (tok_rows, LANES), 0)
    weight_half = (weight_ref[...].astype(F32) * 0.5).astype(BF16)
    hidden = activate(out_ref[...], weight_half)
    ones = []
    for j in range(lines):
        ids = tok_ref[pl.ds(step * lines + j, 1), :] - base
        ones.append(jnp.where(token == ids, 1.0, 0.0))
    hot = jnp.concatenate(ones, axis=1).astype(BF16)
    count = functools.reduce(jnp.add, ones)
    part = dot(hot, hidden)

    @pl.when(step == 0)
    def _():
        sum_ref[...] = part
        cnt_ref[...] = count

    @pl.when(step > 0)
    def _():
        sum_ref[...] += part
        cnt_ref[...] += count


def pool(pos, atom_out, weight, tok2d, tok_rows, part):
    rows, width = atom_out.shape
    feats = weight.shape[1] // PARTS
    size = min(1024, rows)
    return pl.pallas_call(
        functools.partial(pool_kernel, tok_rows),
        grid_spec=pltpu.PrefetchScalarGridSpec(
            num_scalar_prefetch=1,
            grid=(rows // size,),
            in_specs=[
                pl.BlockSpec((size, width), lambda i, *_: (i, 0)),
                pl.BlockSpec((width, feats), lambda i, *_: (0, part)),
                full(tok2d.shape),
            ],
            out_specs=[full((tok_rows, feats)), full((tok_rows, LANES))],
        ),
        out_shape=[
            jax.ShapeDtypeStruct((tok_rows, feats), F32),
            jax.ShapeDtypeStruct((tok_rows, LANES), F32),
        ],
        compiler_params=params(VMEM_SMALL),
        cost_estimate=pl.CostEstimate(flops=2 * 10**9, bytes_accessed=2 * 10**6, transcendentals=10**6),
        name="pool",
    )(pos, atom_out, weight, tok2d)


def finish_kernel(msg_ref, weight_ref, sum_ref, cnt_ref, repr_ref):
    tok_rows = sum_ref.shape[0]
    size = msg_ref.shape[0] - 16
    lines = size // LANES
    token = lax.broadcasted_iota(jnp.int32, (tok_rows, LANES), 0).astype(F32)
    weight_half = (weight_ref[...].astype(F32) * 0.5).astype(BF16)
    hidden = activate(msg_ref[:size, :], weight_half)
    codes = msg_ref[size:, :].astype(F32)
    ids = codes[:8] * 16.0 + codes[8:] - 1.0
    ones = [jnp.where(token == ids[8 - lines + j : 9 - lines + j], 1.0, 0.0) for j in range(lines)]
    hot = jnp.concatenate(ones, axis=1).astype(BF16)
    count = functools.reduce(jnp.add, ones) + cnt_ref[...]
    sums = sum_ref[...] + dot(hot, hidden)
    repr_ref[...] = (sums / jnp.sum(count, axis=1, keepdims=True)).astype(BF16)


def finish(msg, weight, sums, counts, part):
    rows, feats = sums.shape
    return pl.pallas_call(
        finish_kernel,
        grid=(1,),
        in_specs=[
            full(msg.shape),
            pl.BlockSpec((weight.shape[0], feats), lambda i: (0, part)),
            full(sums.shape),
            full(counts.shape),
        ],
        out_specs=full((rows, feats)),
        out_shape=jax.ShapeDtypeStruct((rows, feats), BF16),
        compiler_params=params(VMEM_SMALL),
        cost_estimate=pl.CostEstimate(flops=2 * 10**8, bytes_accessed=2 * 10**6, transcendentals=2 * 10**5),
        name="token_finish",
    )(msg, weight, sums, counts)


def query_kernel(scale, a_ref, b_ref, gain_ref, weight_ref, out_ref):
    rows = jnp.concatenate([a_ref[...].astype(F32), b_ref[...].astype(F32)], axis=1)
    normed = norm_rows(rows, gain_ref[...].reshape(1, -1)).astype(BF16)
    out_ref[...] = (dot(normed, weight_ref[...]) * scale).astype(BF16)


def project_queries(halves, gain, weight):
    rows = halves[0].shape[0]
    return pl.pallas_call(
        functools.partial(query_kernel, 1.0 / math.sqrt(weight.shape[1] // TH)),
        out_shape=jax.ShapeDtypeStruct((rows, weight.shape[1]), BF16),
        compiler_params=params(VMEM_SMALL),
        cost_estimate=pl.CostEstimate(flops=5 * 10**8, bytes_accessed=3 * 10**6, transcendentals=0),
        name="queries",
    )(*halves, gain, weight)


HEADS_STEP = 8


def pack_lse(lse):
    lane = lax.broadcasted_iota(jnp.int32, lse.shape, 1)
    high = lse.astype(BF16).astype(F32)
    rest = lse - high
    middle = rest.astype(BF16).astype(F32)
    low = rest - middle
    return jnp.where(
        lane < TH,
        high,
        jnp.where(lane < 2 * TH, pltpu.roll(middle, TH, 1), pltpu.roll(low, 2 * TH, 1)),
    ).astype(BF16)


def unpack_lse(coded):
    value = coded.astype(F32)
    return value + pltpu.roll(value, LANES - TH, 1) + pltpu.roll(value, LANES - 2 * TH, 1)


ROW_TILE = 32


def attend_step(step, half, q_ref, k_ref, v_ref, bias_ref, o_s, lse_s, work):
    rows = o_s.shape[0]
    width = q_ref.shape[1] // TH
    span = HEADS_STEP * width
    at = pl.multiple_of(half * rows, rows)
    spot = lax.broadcasted_iota(jnp.int32, (rows, LANES), 1)
    pairs = HEADS_STEP // 2
    score_s, term_s, top_s = work[:2], work[2:4], work[4:]

    def layout(p):
        first = 2 * p * width
        low = first // LANES * LANES
        wide = -(-(first + 2 * width) // LANES) * LANES - low
        lane = lax.broadcasted_iota(jnp.int32, (rows, wide), 1)
        first -= low
        masks = [(lane >= first + j * width) & (lane < first + (j + 1) * width) for j in range(2)]
        return pl.ds(pl.multiple_of(step * span + low, LANES), wide), first, masks

    def score(p):
        window, _, masks = layout(p)
        query = q_ref[pl.ds(at, rows), window].astype(F32)
        stacked = jnp.concatenate([jnp.where(m, query, 0.0).astype(BF16) for m in masks], axis=0)
        score_s[p % 2][...] = dot_nt(stacked, k_ref[:, window])

    def soften(p):
        for r in range(0, 2 * rows, ROW_TILE):
            bias = bias_ref[2 * p + r // rows, r % rows : r % rows + ROW_TILE, :].astype(F32)
            scores = score_s[p % 2][r : r + ROW_TILE, :] + bias
            top = jnp.max(scores, axis=-1, keepdims=True)
            term_s[p % 2][r : r + ROW_TILE, :] = jnp.exp(scores - top).astype(BF16)
            top_s[p % 2][r : r + ROW_TILE, :] = jnp.broadcast_to(top, (ROW_TILE, LANES))

    def mix(p):
        window, first, masks = layout(p)
        values = v_ref[:, window]
        column = lax.broadcasted_iota(jnp.int32, values.shape, 1)
        used = (column >= first) & (column < first + 2 * width)
        mixed = dot(term_s[p % 2][...], jnp.where(used, values.astype(F32), 1.0).astype(BF16))
        free = 0 if first >= 16 else 2 * width
        total = mixed[:, free : free + 1]
        mixed = mixed / total
        sums = top_s[p % 2][...] + jnp.log(total)
        result = o_s[:, window]
        lse = lse_s[...]
        for j in range(2):
            result = jnp.where(masks[j], mixed[j * rows : (j + 1) * rows], result)
            lse = jnp.where(spot == step * HEADS_STEP + 2 * p + j, sums[j * rows : (j + 1) * rows], lse)
        o_s[:, window] = result
        lse_s[...] = lse

    score(0)
    for p in range(pairs):
        if p + 1 < pairs:
            score(p + 1)
        soften(p)
        mix(p)


def work_scratch(rows, keys):
    return (
        [pltpu.VMEM((2 * rows, keys), F32)] * 2
        + [pltpu.VMEM((2 * rows, keys), BF16)] * 2
        + [pltpu.VMEM((2 * rows, LANES), F32)] * 2
    )


def send_kernel(steps, half_ref, core_ref, q_ref, own_a, own_b, other_a, other_b, gain_ref, wkv_ref, bias_ref, k_ref, v_ref, msg_ref, o_s, lse_s, x_s, *work):
    step = pl.program_id(0)
    rows = own_a.shape[0]
    feats = k_ref.shape[1]

    @pl.when(step == 0)
    def _():
        core = core_ref[0]
        gain = gain_ref[...].reshape(1, feats)
        for place, parts in ((core, (own_a, own_b)), (1 - core, (other_a, other_b))):
            values = jnp.concatenate([part[...].astype(F32) for part in parts], axis=1)
            x_s[pl.ds(pl.multiple_of(place * rows, rows), rows), :] = norm_rows(values, gain).astype(BF16)
        for r in range(0, 2 * rows, rows):
            k_ref[r : r + rows, :] = dot(x_s[r : r + rows, :], wkv_ref[:, :feats]).astype(BF16)
            v_ref[r : r + rows, :] = dot(x_s[r : r + rows, :], wkv_ref[:, feats:]).astype(BF16)
        lse_s[...] = jnp.zeros_like(lse_s)

    attend_step(step, half_ref[0], q_ref, k_ref, v_ref, bias_ref, o_s, lse_s, work)

    @pl.when(step == steps - 1)
    def _():
        msg_ref[:, :feats] = o_s[...].astype(BF16)
        msg_ref[:, feats:] = pack_lse(lse_s[...])


def keep_kernel(half_ref, q_ref, k_ref, v_ref, bias_ref, o_ref, lse_ref, *work):
    step = pl.program_id(0)

    @pl.when(step == 0)
    def _():
        lse_ref[...] = jnp.zeros_like(lse_ref)

    attend_step(step, half_ref[0], q_ref, k_ref, v_ref, bias_ref, o_ref, lse_ref, work)


def attention(half, q, bias, keys, first):
    tok_rows, feats = q.shape
    rows = tok_rows // 2
    key_rows = bias.shape[2]
    steps = TH // HEADS_STEP
    bias_spec = pl.BlockSpec((HEADS_STEP, rows, key_rows), lambda i, s, *_: (i, s[0], 0))
    kv_shape = (key_rows, feats)
    cost = pl.CostEstimate(flops=8 * 10**9, bytes_accessed=8 * 10**6, transcendentals=3 * 10**6)
    if first:
        core, own, other, gain, wkv = keys
        return pl.pallas_call(
            functools.partial(send_kernel, steps),
            grid_spec=pltpu.PrefetchScalarGridSpec(
                num_scalar_prefetch=2,
                grid=(steps,),
                in_specs=[full(q.shape)]
                + [full(part.shape) for part in (*own, *other)]
                + [full(gain.shape), full(wkv.shape), bias_spec],
                out_specs=[full(kv_shape), full(kv_shape), full((rows, feats + LANES))],
                scratch_shapes=[
                    pltpu.VMEM((rows, feats), F32),
                    pltpu.VMEM((rows, LANES), F32),
                    pltpu.VMEM(kv_shape, BF16),
                    *work_scratch(rows, key_rows),
                ],
            ),
            out_shape=[
                jax.ShapeDtypeStruct(kv_shape, BF16),
                jax.ShapeDtypeStruct(kv_shape, BF16),
                jax.ShapeDtypeStruct((rows, feats + LANES), BF16),
            ],
            compiler_params=params(),
            cost_estimate=cost,
            name="attend_send",
        )(half, core, q, *own, *other, gain, wkv, bias)
    k, v = keys
    return pl.pallas_call(
        keep_kernel,
        grid_spec=pltpu.PrefetchScalarGridSpec(
            num_scalar_prefetch=1,
            grid=(steps,),
            in_specs=[full(q.shape), full(kv_shape), full(kv_shape), bias_spec],
            out_specs=[full((rows, feats)), full((rows, LANES))],
            scratch_shapes=work_scratch(rows, key_rows),
        ),
        out_shape=[
            jax.ShapeDtypeStruct((rows, feats), F32),
            jax.ShapeDtypeStruct((rows, LANES), F32),
        ],
        compiler_params=params(),
        cost_estimate=cost,
        name="attend_keep",
    )(half, q, k, v, bias)


def merged_rows(o_ref, lse_ref, msg_ref):
    rows, feats = o_ref.shape
    width = feats // TH
    other = msg_ref[:, :feats].astype(F32)
    lse_b = unpack_lse(msg_ref[:, feats:])
    spot = lax.broadcasted_iota(jnp.int32, (rows, LANES), 1)
    lse_a = lse_ref[...]
    lse_b = jnp.where(spot < TH, lse_b, lse_a)
    top = jnp.maximum(lse_a, lse_b)
    part_a = jnp.exp(lse_a - top)
    total = part_a + jnp.exp(lse_b - top)
    share = part_a / total
    high = share.astype(BF16)
    low = (share - high.astype(F32)).astype(BF16)
    head = lax.broadcasted_iota(jnp.int32, (LANES, feats), 0) * width
    column = lax.broadcasted_iota(jnp.int32, (LANES, feats), 1)
    spread = jnp.where((column >= head) & (column < head + width), 1.0, 0.0).astype(BF16)
    wide = dot(high, spread) + dot(low, spread)
    return other + wide * (o_ref[...] - other), top + jnp.log(total)


def merge_kernel(o_ref, lse_ref, msg_ref, out_ref, sum_ref, back_ref):
    mixed, lse = merged_rows(o_ref, lse_ref, msg_ref)
    feats = mixed.shape[1]
    out_ref[...] = mixed
    sum_ref[...] = lse
    back_ref[:, :feats] = mixed.astype(BF16)
    back_ref[:, feats:] = pack_lse(lse)


def merge(o, lse, msg):
    return pl.pallas_call(
        merge_kernel,
        out_shape=[
            jax.ShapeDtypeStruct(o.shape, F32),
            jax.ShapeDtypeStruct(lse.shape, F32),
            jax.ShapeDtypeStruct(msg.shape, BF16),
        ],
        compiler_params=params(VMEM_SMALL),
        name="merge",
    )(o, lse, msg)


def last_kernel(half_ref, o_ref, lse_ref, msg_ref, a_ref, b_ref, weight_ref, out_ref):
    rows = o_ref.shape[0]
    mixed, _ = merged_rows(o_ref, lse_ref, msg_ref)
    mine = pl.ds(pl.multiple_of(half_ref[0] * rows, rows), rows)
    own = jnp.concatenate([a_ref[mine, :].astype(F32), b_ref[mine, :].astype(F32)], axis=1)
    out_ref[...] = (own + dot(mixed.astype(BF16), weight_ref[...])).astype(BF16)


def last_merge(half, o, lse, msg, token_repr, weight):
    return pl.pallas_call(
        last_kernel,
        in_specs=[pl.BlockSpec(memory_space=pltpu.SMEM)] + [pl.BlockSpec(memory_space=pltpu.VMEM)] * 6,
        out_shape=jax.ShapeDtypeStruct(o.shape, BF16),
        compiler_params=params(VMEM_SMALL),
        name="merge_last",
    )(half, o, lse, msg, *token_repr, weight)


def join_kernel(half_ref, own_ref, other_ref, out_ref):
    rows = own_ref.shape[0]
    out_ref[pl.ds(pl.multiple_of(half_ref[0] * rows, rows), rows), :] = own_ref[...]
    out_ref[pl.ds(pl.multiple_of((1 - half_ref[0]) * rows, rows), rows), :] = other_ref[...]


def join(half, own, other):
    rows, feats = own.shape
    return pl.pallas_call(
        join_kernel,
        in_specs=[pl.BlockSpec(memory_space=pltpu.SMEM)] + [pl.BlockSpec(memory_space=pltpu.VMEM)] * 2,
        out_shape=jax.ShapeDtypeStruct((2 * rows, feats), BF16),
        compiler_params=params(VMEM_SMALL),
        name="join",
    )(half, own, other)


def bits_of(count):
    return [1 << b for b in range(count.bit_length() - 1)]


SENDERS = (
    (((1, 3, 2, 0), (3, 2, 0, 1)), ((0, 3, 2, 1), (3, 0, 1, 2)), ((2, 1, 0, 3), (2, 0, 3, 1)), ((3, 1, 0, 2), (3, 0, 2, 1))),
    (((2, 0, 1, 3), (2, 1, 3, 0)), ((2, 3, 0, 1), (1, 2, 3, 0)), ((3, 2, 1, 0), (1, 3, 0, 2)), ((2, 3, 1, 0), (0, 2, 3, 1))),
)


def key_part(rows, part):
    n_pb, n_ka = lax.axis_size("pb"), lax.axis_size("ka")
    cores = n_pb // n_ka
    pairs = []
    for k in range(n_ka):
        for c in range(cores):
            for sender in range(n_ka):
                chip = SENDERS[part][k][c][sender] if n_ka == 4 else sender ^ 1
                if chip != k:
                    pairs.append(((k * cores + c) * n_ka + sender, (chip * cores + c) * n_ka + k))
    moved = lax.ppermute(rows, ("pb", "ka"), pairs)
    held = jnp.where(lax.axis_index("pb") // cores == lax.axis_index("ka"), rows, moved)
    return held, lax.ppermute(held, "pb", [(p, p ^ 1) for p in range(n_pb)])


def body(
    atoms,
    atom_gain,
    atom_qkv,
    atom_proj,
    atom_bias,
    window_shift,
    token_of_atom,
    agg_weight,
    token_gain,
    token_q,
    token_kv,
    token_o,
    pair_bias,
):
    n_pb, n_ka = lax.axis_size("pb"), lax.axis_size("ka")
    shard, plane = lax.axis_index("pb"), lax.axis_index("ka")
    rows, width = atoms.shape
    tok_rows = pair_bias.shape[1]
    half = WIN_K // 2
    up = [(i, i + 1) for i in range(n_pb - 1)]
    down = [(i + 1, i) for i in range(n_pb - 1)]
    pos = shard.astype(jnp.int32).reshape(1)
    tok2d = token_of_atom.reshape(rows // LANES, LANES)
    left = lax.ppermute(atoms[rows - half :], "pb", up)
    right = lax.ppermute(atoms[:half], "pb", down)
    atom_out, msg = atom_attention(
        window_shift, pos, atoms, left, right, atom_gain, atom_qkv, atom_proj,
        atom_bias, tok2d, tok_rows, rows * n_pb,
    )
    behind = lax.ppermute(msg, "pb", up)
    token_repr, own_keys, other_keys = [], [], []
    for part in range(PARTS):
        sums, counts = pool(pos, atom_out, agg_weight, tok2d, tok_rows, part)
        token_repr.append(finish(behind, agg_weight, sums, counts, part))
    for part in range(PARTS):
        own, other = key_part(token_repr[part], part)
        own_keys.append(own)
        other_keys.append(other)
    queries = project_queries(token_repr, token_gain, token_q)
    parity = jnp.bitwise_and(plane ^ (plane >> 1), 1).astype(jnp.int32)
    core = lax.rem(shard, n_pb // n_ka).astype(jnp.int32)
    k, v, near = attention(
        (1 - parity).reshape(1), queries, pair_bias, (core.reshape(1), own_keys, other_keys, token_gain, token_kv), True
    )
    got = lax.ppermute(near, "ka", [(i, i ^ 1) for i in range(n_ka)])
    o, lse = attention(parity.reshape(1), queries, pair_bias, (k, v), False)
    for bit in bits_of(n_ka)[1:]:
        o, lse, far = merge(o, lse, got)
        got = lax.ppermute(far, "ka", [(i, i ^ (2 * bit - 1)) for i in range(n_ka)])
    part = last_merge(parity.reshape(1), o, lse, got, token_repr, token_o)
    rest = lax.ppermute(part, "ka", [(i, i ^ 1) for i in range(n_ka)])
    return atom_out, join(parity.reshape(1), part, rest)


def solution(mesh):
    return jax.shard_map(
        body,
        mesh=mesh,
        in_specs=(
            P("pb", None),
            P(),
            P(),
            P(),
            P(None, "pb", None),
            P("pb"),
            P("pb"),
            P(),
            P(),
            P(),
            P(),
            P(),
            P(None, "pb", "ka"),
        ),
        out_specs=(P("pb", None), P("pb", None)),
        check_vma=False,
    )
```

```python
import functools
import math

import jax
import jax.numpy as jnp
from jax import lax
from jax.experimental import pallas as pl
from jax.experimental.pallas import tpu as pltpu
from jax.sharding import PartitionSpec as P

AH = 4
TH = 16
WIN_Q = 32
WIN_K = 128
SHIFT_MAX = 384
PARTS = 2
LANES = 128
F32 = jnp.float32
BF16 = jnp.bfloat16
VMEM_LIMIT = 56 * 1024 * 1024
VMEM_SMALL = 24 * 1024 * 1024


def full(shape):
    return pl.BlockSpec(shape, lambda *_: (0,) * len(shape))


def params(limit=VMEM_LIMIT):
    return pltpu.CompilerParams(vmem_limit_bytes=limit)


def norm_rows(as_float, gain):
    centre = jnp.mean(as_float, axis=-1, keepdims=True)
    spread = jnp.mean(jnp.square(as_float - centre), axis=-1, keepdims=True)
    return (as_float - centre) * lax.rsqrt(spread + 1e-05) * gain


def dot(a, b):
    return jnp.dot(a, b, preferred_element_type=F32)


def dot_nt(a, b):
    return lax.dot_general(a, b, (((1,), (1,)), ((), ())), preferred_element_type=F32)


def atom_kernel(
    chunks,
    atom_total,
    tok_rows,
    shift_ref,
    pos_ref,
    atoms_ref,
    left_ref,
    right_ref,
    gain_ref,
    qkv_ref,
    proj_ref,
    bias_ref,
    tok_ref,
    out_ref,
    msg_ref,
    q_s,
    k_s,
    v_s,
):
    step = pl.program_id(0)
    rows, width = atoms_ref.shape
    size = out_ref.shape[0]
    half = WIN_K // 2
    head = width // AH
    shard = pos_ref[0]

    @pl.when(step == 0)
    def _():
        gain = gain_ref[...].reshape(1, width)

        def project(values):
            normed = norm_rows(values.astype(F32), gain).astype(BF16)
            return dot(normed, qkv_ref[...])

        def keep(res, at, count):
            k_s[pl.ds(at, count), :] = res[:, width : 2 * width].astype(BF16)
            v_s[pl.ds(at, count), :width] = res[:, 2 * width :].astype(BF16)
            v_s[pl.ds(at, count), width:] = jnp.ones((count, width), BF16)

        def one(c, carry):
            at = pl.multiple_of(c * size, size)
            res = project(atoms_ref[pl.ds(at, size), :])
            q_s[pl.ds(at, size), :] = (res[:, :width] * (1.0 / math.sqrt(head))).astype(BF16)
            keep(res, pl.multiple_of(at + half, half), size)
            return carry

        lax.fori_loop(0, chunks, one, 0, unroll=2)
        keep(project(left_ref[...]), 0, half)
        keep(project(right_ref[...]), half + rows, half)

    group = WIN_K // WIN_Q
    atoms_group = group * WIN_Q
    lane_q = lax.broadcasted_iota(jnp.int32, (WIN_Q, width), 1)
    heads = [(lane_q >= h * head) & (lane_q < (h + 1) * head) for h in range(AH)]
    lane = lax.broadcasted_iota(jnp.int32, (AH * WIN_Q, WIN_K), 1)
    slot = lax.broadcasted_iota(jnp.int32, (1, WIN_K), 1)
    for g in range(size // atoms_group):
        local = g * atoms_group
        at = pl.multiple_of(step * size + local, atoms_group)
        keys = k_s[pl.ds(at, 2 * WIN_K), :]
        values = v_s[pl.ds(at, 2 * WIN_K), :]
        query = q_s[pl.ds(at, atoms_group), :].astype(F32)
        stacked = jnp.concatenate(
            [
                jnp.where(m, query[i * WIN_Q : (i + 1) * WIN_Q], 0.0).astype(BF16)
                for i in range(group)
                for m in heads
            ],
            axis=0,
        )
        scores = dot_nt(stacked, keys)
        weights = []
        for i in range(group):
            offset = i * WIN_Q + half + shift_ref[(step * size + local) // WIN_Q + i]
            early = lane >= offset
            span = AH * WIN_Q
            mine = scores[i * span : (i + 1) * span]
            begin = local + i * WIN_Q
            bias = bias_ref[:, begin : begin + WIN_Q, :].astype(F32).reshape(span, WIN_K)
            index = slot + jnp.where(slot >= offset, 0, WIN_K) + (at + shard * rows - half)
            shut = jnp.where((index >= 0) & (index < atom_total), 0.0, -jnp.inf)
            logits = jnp.where(early, mine[:, :WIN_K], mine[:, WIN_K:]) + (
                pltpu.roll(bias, jnp.bitwise_and(offset, WIN_K - 1), 1) + shut
            )
            terms = jnp.exp(logits - jnp.max(logits, axis=-1, keepdims=True))
            weights.append(
                jnp.concatenate(
                    [jnp.where(early, terms, 0.0).astype(BF16), jnp.where(early, 0.0, terms).astype(BF16)],
                    axis=1,
                )
            )
        mixed = dot(jnp.concatenate(weights, axis=0), values)
        merged = []
        for i in range(group):
            acc = None
            for h in range(AH):
                top = (i * AH + h) * WIN_Q
                part = mixed[top : top + WIN_Q]
                acc = part if acc is None else jnp.where(jnp.concatenate([heads[h]] * 2, axis=1), part, acc)
            merged.append((acc[:, :width] / acc[:, width:]).astype(BF16))
        own = atoms_ref[pl.ds(at, atoms_group), :].astype(F32)
        result = own + dot(jnp.concatenate(merged, axis=0), proj_ref[...])
        out_ref[local : local + atoms_group, :] = result.astype(BF16)

    @pl.when(step == chunks - 1)
    def _():
        ids = tok_ref[tok_ref.shape[0] - 8 :, :]
        code = jnp.maximum(ids - (shard + 1) * tok_rows + 1, 0)
        high = (code >> 4).astype(F32)
        low = (code & 15).astype(F32)
        msg_ref[:size, :] = out_ref[...]
        msg_ref[size:, :] = jnp.concatenate([high, low], axis=0).astype(BF16)


def atom_attention(shift, pos, atoms, left, right, gain, qkv, proj, bias, tok2d, tok_rows, atom_total):
    rows, width = atoms.shape
    size = SHIFT_MAX
    chunks = rows // size
    half = WIN_K // 2
    return pl.pallas_call(
        functools.partial(atom_kernel, chunks, atom_total, tok_rows),
        grid_spec=pltpu.PrefetchScalarGridSpec(
            num_scalar_prefetch=2,
            grid=(chunks,),
            in_specs=[
                full((rows, width)),
                full((half, width)),
                full((half, width)),
                full((width,)),
                full(qkv.shape),
                full(proj.shape),
                pl.BlockSpec((AH, size, WIN_K), lambda i, *_: (0, i, 0)),
                full(tok2d.shape),
            ],
            out_specs=[
                pl.BlockSpec((size, width), lambda i, *_: (i, 0)),
                full((size + 16, width)),
            ],
            scratch_shapes=[
                pltpu.VMEM((rows, width), BF16),
                pltpu.VMEM((rows + 2 * half, width), BF16),
                pltpu.VMEM((rows + 2 * half, 2 * width), BF16),
            ],
        ),
        out_shape=[
            jax.ShapeDtypeStruct((rows, width), BF16),
            jax.ShapeDtypeStruct((size + 16, width), BF16),
        ],
        compiler_params=params(),
        cost_estimate=pl.CostEstimate(flops=8 * 10**9, bytes_accessed=6 * 10**6, transcendentals=2 * 10**6),
        name="atom_attention",
    )(shift, pos, atoms, left, right, gain, qkv, proj, bias, tok2d)


def activate(rows, weight_half):
    u = dot(rows, weight_half)
    return (u + u * jnp.tanh(u)).astype(BF16)


def pool_kernel(tok_rows, pos_ref, out_ref, weight_ref, tok_ref, sum_ref, cnt_ref):
    step = pl.program_id(0)
    size = out_ref.shape[0]
    lines = size // LANES
    base = pos_ref[0] * tok_rows
    token = lax.broadcasted_iota(jnp.int32, (tok_rows, LANES), 0)
    weight_half = (weight_ref[...].astype(F32) * 0.5).astype(BF16)
    hidden = activate(out_ref[...], weight_half)
    ones = []
    for j in range(lines):
        ids = tok_ref[pl.ds(step * lines + j, 1), :] - base
        ones.append(jnp.where(token == ids, 1.0, 0.0))
    hot = jnp.concatenate(ones, axis=1).astype(BF16)
    count = functools.reduce(jnp.add, ones)
    part = dot(hot, hidden)

    @pl.when(step == 0)
    def _():
        sum_ref[...] = part
        cnt_ref[...] = count

    @pl.when(step > 0)
    def _():
        sum_ref[...] += part
        cnt_ref[...] += count


def pool(pos, atom_out, weight, tok2d, tok_rows, part):
    rows, width = atom_out.shape
    feats = weight.shape[1] // PARTS
    size = min(1024, rows)
    return pl.pallas_call(
        functools.partial(pool_kernel, tok_rows),
        grid_spec=pltpu.PrefetchScalarGridSpec(
            num_scalar_prefetch=1,
            grid=(rows // size,),
            in_specs=[
                pl.BlockSpec((size, width), lambda i, *_: (i, 0)),
                pl.BlockSpec((width, feats), lambda i, *_: (0, part)),
                full(tok2d.shape),
            ],
            out_specs=[full((tok_rows, feats)), full((tok_rows, LANES))],
        ),
        out_shape=[
            jax.ShapeDtypeStruct((tok_rows, feats), F32),
            jax.ShapeDtypeStruct((tok_rows, LANES), F32),
        ],
        compiler_params=params(VMEM_SMALL),
        cost_estimate=pl.CostEstimate(flops=2 * 10**9, bytes_accessed=2 * 10**6, transcendentals=10**6),
        name="pool",
    )(pos, atom_out, weight, tok2d)


def finish_kernel(msg_ref, weight_ref, sum_ref, cnt_ref, repr_ref):
    tok_rows = sum_ref.shape[0]
    size = msg_ref.shape[0] - 16
    lines = size // LANES
    token = lax.broadcasted_iota(jnp.int32, (tok_rows, LANES), 0).astype(F32)
    weight_half = (weight_ref[...].astype(F32) * 0.5).astype(BF16)
    hidden = activate(msg_ref[:size, :], weight_half)
    codes = msg_ref[size:, :].astype(F32)
    ids = codes[:8] * 16.0 + codes[8:] - 1.0
    ones = [jnp.where(token == ids[8 - lines + j : 9 - lines + j], 1.0, 0.0) for j in range(lines)]
    hot = jnp.concatenate(ones, axis=1).astype(BF16)
    count = functools.reduce(jnp.add, ones) + cnt_ref[...]
    sums = sum_ref[...] + dot(hot, hidden)
    repr_ref[...] = (sums / jnp.sum(count, axis=1, keepdims=True)).astype(BF16)


def finish(msg, weight, sums, counts, part):
    rows, feats = sums.shape
    return pl.pallas_call(
        finish_kernel,
        grid=(1,),
        in_specs=[
            full(msg.shape),
            pl.BlockSpec((weight.shape[0], feats), lambda i: (0, part)),
            full(sums.shape),
            full(counts.shape),
        ],
        out_specs=full((rows, feats)),
        out_shape=jax.ShapeDtypeStruct((rows, feats), BF16),
        compiler_params=params(VMEM_SMALL),
        cost_estimate=pl.CostEstimate(flops=2 * 10**8, bytes_accessed=2 * 10**6, transcendentals=2 * 10**5),
        name="token_finish",
    )(msg, weight, sums, counts)


def query_kernel(scale, a_ref, b_ref, gain_ref, weight_ref, out_ref):
    rows = jnp.concatenate([a_ref[...].astype(F32), b_ref[...].astype(F32)], axis=1)
    normed = norm_rows(rows, gain_ref[...].reshape(1, -1)).astype(BF16)
    out_ref[...] = (dot(normed, weight_ref[...]) * scale).astype(BF16)


def project_queries(halves, gain, weight):
    rows = halves[0].shape[0]
    return pl.pallas_call(
        functools.partial(query_kernel, 1.0 / math.sqrt(weight.shape[1] // TH)),
        out_shape=jax.ShapeDtypeStruct((rows, weight.shape[1]), BF16),
        compiler_params=params(VMEM_SMALL),
        cost_estimate=pl.CostEstimate(flops=5 * 10**8, bytes_accessed=3 * 10**6, transcendentals=0),
        name="queries",
    )(*halves, gain, weight)


GROUPS = 2
ROW_TILE = 32


def pack_message(mixed, lse, heads):
    lane = lax.broadcasted_iota(jnp.int32, lse.shape, 1)
    high = lse.astype(BF16).astype(F32)
    rest = lse - high
    middle = rest.astype(BF16).astype(F32)
    low = rest - middle
    first = jnp.where(lane < heads, high, pltpu.roll(middle, heads, 1))
    second = jnp.where(lane < heads, low, 0.0)
    turned = jnp.concatenate([first, second], axis=0).T
    return jnp.concatenate([mixed.astype(BF16), turned[: 2 * heads].astype(BF16)], axis=0)


def unpack_message(msg, rows, heads):
    coded = msg[rows:].astype(F32)
    coded = jnp.concatenate([coded, jnp.zeros((LANES - 2 * heads, coded.shape[1]), F32)], axis=0).T
    first = coded[:rows]
    return msg[:rows].astype(F32), first + pltpu.roll(first, LANES - heads, 1) + coded[rows:]


def merge_parts(mixed, lse, other, lse_b, heads):
    rows, feats = mixed.shape
    width = feats // heads
    spot = lax.broadcasted_iota(jnp.int32, (rows, LANES), 1)
    lse_b = jnp.where(spot < heads, lse_b, lse)
    top = jnp.maximum(lse, lse_b)
    part = jnp.exp(lse - top)
    total = part + jnp.exp(lse_b - top)
    share = part / total
    high = share.astype(BF16)
    low = (share - high.astype(F32)).astype(BF16)
    head = lax.broadcasted_iota(jnp.int32, (LANES, feats), 0) * width
    column = lax.broadcasted_iota(jnp.int32, (LANES, feats), 1)
    spread = jnp.where((column >= head) & (column < head + width), 1.0, 0.0).astype(BF16)
    wide = dot(high, spread) + dot(low, spread)
    return other + wide * (mixed - other), top + jnp.log(total)


def attend_group(group, heads, width, half, q_ref, k_ref, v_ref, bias_hbm, scratch):
    score_s, term_s, top_s, bias_s, mix_s, sems = scratch
    rows = mix_s.shape[0]
    at = pl.multiple_of(half * rows, rows)
    pairs = heads // 2
    spot = lax.broadcasted_iota(jnp.int32, (rows, LANES), 1)

    def layout(p):
        first = 2 * p * width
        low = first // LANES * LANES
        wide = -(-(first + 2 * width) // LANES) * LANES - low
        lane = lax.broadcasted_iota(jnp.int32, (rows, wide), 1)
        first -= low
        masks = [(lane >= first + j * width) & (lane < first + (j + 1) * width) for j in range(2)]
        return slice(low, low + wide), first, masks

    def score(p):
        window, _, masks = layout(p)
        query = q_ref[pl.ds(at, rows), window].astype(F32)
        stacked = jnp.concatenate([jnp.where(m, query, 0.0).astype(BF16) for m in masks], axis=0)
        score_s[p % 2][...] = dot_nt(stacked, k_ref[:, window])

    def soften(p):
        for r in range(0, 2 * rows, ROW_TILE):
            bias = bias_s[2 * p + r // rows, r % rows : r % rows + ROW_TILE, :].astype(F32)
            scores = score_s[p % 2][r : r + ROW_TILE, :] + bias
            top = jnp.max(scores, axis=-1, keepdims=True)
            term_s[p % 2][r : r + ROW_TILE, :] = jnp.exp(scores - top).astype(BF16)
            top_s[p % 2][r : r + ROW_TILE, :] = jnp.broadcast_to(top, (ROW_TILE, LANES))

    def mix(p, lse):
        window, first, masks = layout(p)
        values = v_ref[:, window]
        column = lax.broadcasted_iota(jnp.int32, values.shape, 1)
        used = (column >= first) & (column < first + 2 * width)
        mixed = dot(term_s[p % 2][...], jnp.where(used, values.astype(F32), 1.0).astype(BF16))
        free = 0 if first >= 16 else 2 * width
        total = mixed[:, free : free + 1]
        mixed = mixed / total
        sums = top_s[p % 2][...] + jnp.log(total)
        result = mix_s[:, window]
        for j in range(2):
            result = jnp.where(masks[j], mixed[j * rows : (j + 1) * rows], result)
            lse = jnp.where(spot == 2 * p + j, sums[j * rows : (j + 1) * rows], lse)
        mix_s[:, window] = result
        return lse

    copies = bias_copies(group, heads, half, bias_hbm, bias_s, sems)
    lse = jnp.zeros((rows, LANES), F32)
    score(0)
    for p in range(pairs):
        if p + 1 < pairs:
            score(p + 1)
        copies[p].wait()
        soften(p)
        lse = mix(p, lse)
    return mix_s[...], lse


def bias_copies(group, heads, half, bias_hbm, bias_s, sems):
    rows = bias_s.shape[1]
    at = pl.multiple_of(half * rows, rows)
    return [
        pltpu.make_async_copy(
            bias_hbm.at[pl.ds(group * heads + 2 * p, 2), pl.ds(at, rows), :],
            bias_s.at[pl.ds(2 * p, 2)],
            sems.at[p],
        )
        for p in range(heads // 2)
    ]


def group_scratch(rows, keys, feats, heads):
    return [
        pltpu.VMEM((2 * rows, keys), F32),
        pltpu.VMEM((2 * rows, keys), F32),
        pltpu.VMEM((2 * rows, keys), BF16),
        pltpu.VMEM((2 * rows, keys), BF16),
        pltpu.VMEM((2 * rows, LANES), F32),
        pltpu.VMEM((2 * rows, LANES), F32),
        pltpu.VMEM((heads, rows, keys), BF16),
        pltpu.VMEM((rows, feats), F32),
        pltpu.SemaphoreType.DMA((heads // 2,)),
    ]


def scratch_of(refs):
    return refs[:2], refs[2:4], refs[4:6], refs[6], refs[7], refs[8]


def project_keys(x_ref, wk_ref, wv_ref, k_ref, v_ref):
    tile = x_ref.shape[0] // 2
    for r in range(0, x_ref.shape[0], tile):
        k_ref[r : r + tile, :] = dot(x_ref[r : r + tile, :], wk_ref[...]).astype(BF16)
        v_ref[r : r + tile, :] = dot(x_ref[r : r + tile, :], wv_ref[...]).astype(BF16)


def first_kernel(heads, width, half_ref, core_ref, q_ref, own_a, own_b, other_a, other_b, gain_ref, wk_ref, wv_ref,
                 bias_hbm, x_ref, k_ref, v_ref, msg_ref, *refs):
    scratch = scratch_of(refs)
    for copy in bias_copies(0, heads, half_ref[0], bias_hbm, scratch[3], scratch[5]):
        copy.start()
    rows = own_a.shape[0]
    core = core_ref[0]
    gain = gain_ref[...].reshape(1, -1)
    for place, parts in ((core, (own_a, own_b)), (1 - core, (other_a, other_b))):
        values = jnp.concatenate([part[...].astype(F32) for part in parts], axis=1)
        x_ref[pl.ds(pl.multiple_of(place * rows, rows), rows), :] = norm_rows(values, gain).astype(BF16)
    project_keys(x_ref, wk_ref, wv_ref, k_ref, v_ref)
    mixed, lse = attend_group(0, heads, width, half_ref[0], q_ref, k_ref, v_ref, bias_hbm, scratch)
    msg_ref[...] = pack_message(mixed, lse, heads)


def next_kernel(group, heads, width, half_ref, q_ref, x_ref, wk_ref, wv_ref, bias_hbm, k_ref, v_ref, msg_ref, *refs):
    scratch = scratch_of(refs)
    for copy in bias_copies(group, heads, half_ref[0], bias_hbm, scratch[3], scratch[5]):
        copy.start()
    project_keys(x_ref, wk_ref, wv_ref, k_ref, v_ref)
    mixed, lse = attend_group(group, heads, width, half_ref[0], q_ref, k_ref, v_ref, bias_hbm, scratch)
    msg_ref[...] = pack_message(mixed, lse, heads)


def keep_kernel(group, heads, width, half_ref, q_ref, k_ref, v_ref, near_ref, bias_hbm, o_ref, lse_ref, msg_ref, *refs):
    scratch = scratch_of(refs)
    for copy in bias_copies(group, heads, half_ref[0], bias_hbm, scratch[3], scratch[5]):
        copy.start()
    mixed, lse = attend_group(group, heads, width, half_ref[0], q_ref, k_ref, v_ref, bias_hbm, scratch)
    rows = mixed.shape[0]
    mixed, lse = merge_parts(mixed, lse, *unpack_message(near_ref[...], rows, heads), heads)
    o_ref[...] = mixed
    lse_ref[...] = lse
    msg_ref[...] = pack_message(mixed, lse, heads)


def group_call(kernel, group, half, scalars, q, arrays, weights, bias, outs, name):
    tok_rows, all_feats = q.shape
    rows, keys, feats = tok_rows // 2, bias.shape[2], all_feats // GROUPS
    heads = TH // GROUPS
    shapes = {
        "x": ((keys, all_feats), BF16),
        "kv": ((keys, feats), BF16),
        "o": ((rows, feats), F32),
        "lse": ((rows, LANES), F32),
        "msg": ((rows + 2 * heads, feats), BF16),
    }
    columns = [pl.BlockSpec((all_feats, feats), lambda i, *_, at=at: (0, at)) for at in (group, GROUPS + group)]
    return pl.pallas_call(
        functools.partial(kernel, heads, feats // heads),
        grid_spec=pltpu.PrefetchScalarGridSpec(
            num_scalar_prefetch=1 + len(scalars),
            grid=(1,),
            in_specs=[pl.BlockSpec((tok_rows, feats), lambda i, *_: (0, group))]
            + [full(array.shape) for array in arrays]
            + (columns if weights is not None else [])
            + [pl.BlockSpec(memory_space=pltpu.HBM)],
            out_specs=[full(shapes[out][0]) for out in outs],
            scratch_shapes=group_scratch(rows, keys, feats, heads),
        ),
        out_shape=[jax.ShapeDtypeStruct(*shapes[out]) for out in outs],
        compiler_params=params(VMEM_SMALL),
        cost_estimate=pl.CostEstimate(flops=4 * 10**9, bytes_accessed=4 * 10**6, transcendentals=10**6),
        name=name,
    )(half, *scalars, q, *arrays, *([weights] * 2 if weights is not None else []), bias)


def merge_kernel(heads, o_ref, lse_ref, msg_ref, out_ref, sum_ref, back_ref):
    rows = o_ref.shape[0]
    mixed, lse = merge_parts(o_ref[...], lse_ref[...], *unpack_message(msg_ref[...], rows, heads), heads)
    out_ref[...] = mixed
    sum_ref[...] = lse
    back_ref[...] = pack_message(mixed, lse, heads)


def merge(o, lse, msg):
    return pl.pallas_call(
        functools.partial(merge_kernel, TH // GROUPS),
        out_shape=[jax.ShapeDtypeStruct(a.shape, a.dtype) for a in (o, lse, msg)],
        compiler_params=params(VMEM_SMALL),
        name="merge",
    )(o, lse, msg)


def settle_kernel(heads, o_ref, lse_ref, msg_ref, out_ref):
    rows = o_ref.shape[0]
    mixed, _ = merge_parts(o_ref[...], lse_ref[...], *unpack_message(msg_ref[...], rows, heads), heads)
    out_ref[...] = mixed.astype(BF16)


def settle(o, lse, msg):
    return pl.pallas_call(
        functools.partial(settle_kernel, TH // GROUPS),
        out_shape=jax.ShapeDtypeStruct(o.shape, BF16),
        compiler_params=params(VMEM_SMALL),
        name="settle",
    )(o, lse, msg)


def output_kernel(half_ref, own_a, own_b, other_a, other_b, a_ref, b_ref, weight_ref, out_ref):
    rows, feats = own_a.shape
    for place, first, second in ((half_ref[0], own_a, own_b), (1 - half_ref[0], other_a, other_b)):
        mine = pl.ds(pl.multiple_of(place * rows, rows), rows)
        result = dot(first[...], weight_ref[:feats, :]) + dot(second[...], weight_ref[feats:, :])
        out_ref[mine, :feats] = (a_ref[mine, :].astype(F32) + result[:, :feats]).astype(BF16)
        out_ref[mine, feats:] = (b_ref[mine, :].astype(F32) + result[:, feats:]).astype(BF16)


def output_rows(half, own, other, token_repr, weight):
    rows = token_repr[0].shape[0]
    return pl.pallas_call(
        output_kernel,
        in_specs=[pl.BlockSpec(memory_space=pltpu.SMEM)] + [pl.BlockSpec(memory_space=pltpu.VMEM)] * 7,
        out_shape=jax.ShapeDtypeStruct((rows, weight.shape[1]), BF16),
        compiler_params=params(VMEM_SMALL),
        name="output_rows",
    )(half, *own, *other, *token_repr, weight)


def bits_of(count):
    return [1 << b for b in range(count.bit_length() - 1)]


def key_parts(halves):
    n_pb, n_ka = lax.axis_size("pb"), lax.axis_size("ka")
    cores = n_pb // n_ka
    chips = n_pb // cores
    shard, plane = lax.axis_index("pb"), lax.axis_index("ka")
    bits = bits_of(chips)
    core = lax.rem(shard, cores)
    away = jnp.bitwise_xor(shard // cores, plane)
    held = list(halves)
    for r in range(len(bits)):
        pairs = []
        gets = jnp.bool_(False)
        for c in range(cores):
            order = bits if c % 2 == 0 else bits[::-1]
            known = sum(order[:r])
            for k in range(n_ka):
                for j in range(chips):
                    if (j ^ k) & ~known == 0:
                        pairs.append(((j * cores + c) * n_ka + k, ((j ^ order[r]) * cores + c) * n_ka + k))
            fresh = (jnp.bitwise_and(away, ~(known + order[r])) == 0) & (jnp.bitwise_and(away, order[r]) != 0)
            gets = gets | (fresh & (core == c))
        held = [jnp.where(gets, lax.ppermute(part, ("pb", "ka"), pairs), part) for part in held]
    return held, [lax.ppermute(part, "pb", [(p, p ^ 1) for p in range(n_pb)]) for part in held]


def body(
    atoms,
    atom_gain,
    atom_qkv,
    atom_proj,
    atom_bias,
    window_shift,
    token_of_atom,
    agg_weight,
    token_gain,
    token_q,
    token_kv,
    token_o,
    pair_bias,
):
    n_pb, n_ka = lax.axis_size("pb"), lax.axis_size("ka")
    shard, plane = lax.axis_index("pb"), lax.axis_index("ka")
    rows, width = atoms.shape
    tok_rows = pair_bias.shape[1]
    half = WIN_K // 2
    up = [(i, i + 1) for i in range(n_pb - 1)]
    down = [(i + 1, i) for i in range(n_pb - 1)]
    pos = shard.astype(jnp.int32).reshape(1)
    tok2d = token_of_atom.reshape(rows // LANES, LANES)
    left = lax.ppermute(atoms[rows - half :], "pb", up)
    right = lax.ppermute(atoms[:half], "pb", down)
    atom_out, msg = atom_attention(
        window_shift, pos, atoms, left, right, atom_gain, atom_qkv, atom_proj,
        atom_bias, tok2d, tok_rows, rows * n_pb,
    )
    behind = lax.ppermute(msg, "pb", up)
    token_repr, own_keys, other_keys = [], [], []
    for part in range(PARTS):
        sums, counts = pool(pos, atom_out, agg_weight, tok2d, tok_rows, part)
        token_repr.append(finish(behind, agg_weight, sums, counts, part))
    own_keys, other_keys = key_parts(token_repr)
    queries = project_queries(token_repr, token_gain, token_q)
    parity = jnp.bitwise_and(plane ^ (plane >> 1), 1).astype(jnp.int32)
    core = lax.rem(shard, n_pb // n_ka).astype(jnp.int32)
    keep, send = parity.reshape(1), (1 - parity).reshape(1)
    swap = [(i, i ^ 1) for i in range(n_ka)]
    bits = bits_of(n_ka)[1:]

    def far(msg, bit):
        return lax.ppermute(msg, "ka", [(i, i ^ (2 * bit - 1)) for i in range(n_ka)])

    x, k, v, msg = group_call(
        first_kernel, 0, send, (core.reshape(1),), queries, (*own_keys, *other_keys, token_gain), token_kv,
        pair_bias, ("x", "kv", "kv", "msg"), "attend_first",
    )
    held, near = [(k, v)], [lax.ppermute(msg, "ka", swap)]
    for g in range(1, GROUPS):
        k, v, msg = group_call(
            functools.partial(next_kernel, g), g, send, (), queries, (x,), token_kv,
            pair_bias, ("kv", "kv", "msg"), "attend_next",
        )
        held.append((k, v))
        near.append(lax.ppermute(msg, "ka", swap))
    sums, gone = [], []
    for g in range(GROUPS):
        o, lse, msg = group_call(
            functools.partial(keep_kernel, g), g, keep, (), queries, (*held[g], near[g]), None,
            pair_bias, ("o", "lse", "msg"), "attend_keep",
        )
        sums.append((o, lse))
        gone.append(far(msg, bits[0]))
    own_mix, other_mix = [], []
    for g in range(GROUPS):
        (o, lse), got = sums[g], gone[g]
        for bit in bits[1:]:
            o, lse, msg = merge(o, lse, got)
            got = far(msg, bit)
        own_mix.append(settle(o, lse, got))
        other_mix.append(lax.ppermute(own_mix[g], "ka", swap))
    return atom_out, output_rows(keep, own_mix, other_mix, token_repr, token_o)


def solution(mesh):
    return jax.shard_map(
        body,
        mesh=mesh,
        in_specs=(
            P("pb", None),
            P(),
            P(),
            P(),
            P(None, "pb", None),
            P("pb"),
            P("pb"),
            P(),
            P(),
            P(),
            P(),
            P(),
            P(None, "pb", "ka"),
        ),
        out_specs=(P("pb", None), P("pb", None)),
        check_vma=False,
    )
```

```python
import functools
import math

import jax
import jax.numpy as jnp
from jax import lax
from jax.experimental import pallas as pl
from jax.experimental.pallas import tpu as pltpu
from jax.sharding import PartitionSpec as P

AH = 4
TH = 16
WIN_Q = 32
WIN_K = 128
SHIFT_MAX = 384
PARTS = 2
LANES = 128
F32 = jnp.float32
BF16 = jnp.bfloat16
VMEM_LIMIT = 56 * 1024 * 1024
VMEM_SMALL = 24 * 1024 * 1024


def full(shape):
    return pl.BlockSpec(shape, lambda *_: (0,) * len(shape))


def params(limit=VMEM_LIMIT):
    return pltpu.CompilerParams(vmem_limit_bytes=limit)


def norm_rows(as_float, gain):
    centre = jnp.mean(as_float, axis=-1, keepdims=True)
    spread = jnp.mean(jnp.square(as_float - centre), axis=-1, keepdims=True)
    return (as_float - centre) * lax.rsqrt(spread + 1e-05) * gain


def dot(a, b):
    return jnp.dot(a, b, preferred_element_type=F32)


def dot_nt(a, b):
    return lax.dot_general(a, b, (((1,), (1,)), ((), ())), preferred_element_type=F32)


def atom_kernel(
    chunks,
    atom_total,
    tok_rows,
    shift_ref,
    pos_ref,
    atoms_ref,
    left_ref,
    right_ref,
    gain_ref,
    qkv_ref,
    proj_ref,
    bias_ref,
    tok_ref,
    out_ref,
    msg_ref,
    q_s,
    k_s,
    v_s,
    mix_s,
):
    step = pl.program_id(0)
    rows, width = atoms_ref.shape
    size = out_ref.shape[0]
    half = WIN_K // 2
    head = width // AH
    shard = pos_ref[0]

    @pl.when(step == 0)
    def _():
        gain = gain_ref[...].reshape(1, width)

        def project(values):
            normed = norm_rows(values.astype(F32), gain).astype(BF16)
            return dot(normed, qkv_ref[...])

        def keep(res, at, count):
            k_s[pl.ds(at, count), :] = res[:, width : 2 * width].astype(BF16)
            v_s[pl.ds(at, count), :width] = res[:, 2 * width :].astype(BF16)
            v_s[pl.ds(at, count), width:] = jnp.ones((count, width), BF16)

        def one(c, carry):
            at = pl.multiple_of(c * size, size)
            res = project(atoms_ref[pl.ds(at, size), :])
            q_s[pl.ds(at, size), :] = (res[:, :width] * (1.0 / math.sqrt(head))).astype(BF16)
            keep(res, pl.multiple_of(at + half, half), size)
            return carry

        lax.fori_loop(0, chunks, one, 0, unroll=2)
        keep(project(left_ref[...]), 0, half)
        keep(project(right_ref[...]), half + rows, half)

    group = WIN_K // WIN_Q
    atoms_group = group * WIN_Q
    span = AH * WIN_Q
    lane_q = lax.broadcasted_iota(jnp.int32, (WIN_Q, width), 1)
    heads = [(lane_q >= h * head) & (lane_q < (h + 1) * head) for h in range(AH)]
    lane = lax.broadcasted_iota(jnp.int32, (span, WIN_K), 1)
    slot = lax.broadcasted_iota(jnp.int32, (1, WIN_K), 1)
    blocks = size // WIN_Q

    def region(n):
        return pl.ds(pl.multiple_of(step * size + n // group * atoms_group, atoms_group), 2 * WIN_K)

    def score(n):
        query = q_s[pl.ds(pl.multiple_of(step * size + n * WIN_Q, WIN_Q), WIN_Q), :].astype(F32)
        stacked = jnp.concatenate([jnp.where(m, query, 0.0).astype(BF16) for m in heads], axis=0)
        return dot_nt(stacked, k_s[region(n), :])

    def soften(n, scores):
        offset = n % group * WIN_Q + half + shift_ref[step * blocks + n]
        early = lane >= offset
        begin = n * WIN_Q
        bias = bias_ref[:, begin : begin + WIN_Q, :].astype(F32).reshape(span, WIN_K)
        index = slot + jnp.where(slot >= offset, 0, WIN_K)
        index = index + (step * size + n // group * atoms_group + shard * rows - half)
        shut = jnp.where((index >= 0) & (index < atom_total), 0.0, -jnp.inf)
        logits = jnp.where(early, scores[:, :WIN_K], scores[:, WIN_K:]) + (
            pltpu.roll(bias, jnp.bitwise_and(offset, WIN_K - 1), 1) + shut
        )
        terms = jnp.exp(logits - jnp.max(logits, axis=-1, keepdims=True))
        return jnp.concatenate(
            [jnp.where(early, terms, 0.0).astype(BF16), jnp.where(early, 0.0, terms).astype(BF16)], axis=1
        )

    def mix(n, weights):
        mixed = dot(weights, v_s[region(n), :])
        values, total = mixed[:WIN_Q, :width], mixed[:WIN_Q, width:]
        for h in range(1, AH):
            part = mixed[h * WIN_Q : (h + 1) * WIN_Q]
            values = jnp.where(heads[h], part[:, :width], values)
            total = jnp.where(heads[h], part[:, width:], total)
        mix_s[n * WIN_Q : (n + 1) * WIN_Q, :] = (values / total).astype(BF16)

    def project_out(g):
        local = g * atoms_group
        at = pl.multiple_of(step * size + local, atoms_group)
        own = atoms_ref[pl.ds(at, atoms_group), :].astype(F32)
        result = own + dot(mix_s[local : local + atoms_group, :], proj_ref[...])
        out_ref[local : local + atoms_group, :] = result.astype(BF16)

    ahead = score(0)
    behind = None
    for n in range(blocks):
        scores = ahead
        if n + 1 < blocks:
            ahead = score(n + 1)
        if n:
            mix(n - 1, behind)
        behind = soften(n, scores)
        if n % group == 0 and n:
            project_out(n // group - 1)
    mix(blocks - 1, behind)
    project_out(blocks // group - 1)

    @pl.when(step == chunks - 1)
    def _():
        ids = tok_ref[tok_ref.shape[0] - 8 :, :]
        code = jnp.maximum(ids - (shard + 1) * tok_rows + 1, 0)
        high = (code >> 4).astype(F32)
        low = (code & 15).astype(F32)
        msg_ref[:SHIFT_MAX, :] = out_ref[size - SHIFT_MAX :, :]
        msg_ref[SHIFT_MAX:, :] = jnp.concatenate([high, low], axis=0).astype(BF16)


def atom_attention(shift, pos, atoms, left, right, gain, qkv, proj, bias, tok2d, tok_rows, atom_total):
    rows, width = atoms.shape
    size = 2 * SHIFT_MAX
    chunks = rows // size
    half = WIN_K // 2
    return pl.pallas_call(
        functools.partial(atom_kernel, chunks, atom_total, tok_rows),
        grid_spec=pltpu.PrefetchScalarGridSpec(
            num_scalar_prefetch=2,
            grid=(chunks,),
            in_specs=[
                full((rows, width)),
                full((half, width)),
                full((half, width)),
                full((width,)),
                full(qkv.shape),
                full(proj.shape),
                pl.BlockSpec((AH, size, WIN_K), lambda i, *_: (0, i, 0)),
                full(tok2d.shape),
            ],
            out_specs=[
                pl.BlockSpec((size, width), lambda i, *_: (i, 0)),
                full((SHIFT_MAX + 16, width)),
            ],
            scratch_shapes=[
                pltpu.VMEM((rows, width), BF16),
                pltpu.VMEM((rows + 2 * half, width), BF16),
                pltpu.VMEM((rows + 2 * half, 2 * width), BF16),
                pltpu.VMEM((size, width), BF16),
            ],
        ),
        out_shape=[
            jax.ShapeDtypeStruct((rows, width), BF16),
            jax.ShapeDtypeStruct((SHIFT_MAX + 16, width), BF16),
        ],
        compiler_params=params(),
        cost_estimate=pl.CostEstimate(flops=8 * 10**9, bytes_accessed=6 * 10**6, transcendentals=2 * 10**6),
        name="atom_attention",
    )(shift, pos, atoms, left, right, gain, qkv, proj, bias, tok2d)


def activate(rows, weight_half):
    u = dot(rows, weight_half)
    return (u + u * jnp.tanh(u)).astype(BF16)


def pool_kernel(tok_rows, pos_ref, out_ref, weight_ref, tok_ref, sum_ref, cnt_ref):
    step = pl.program_id(0)
    size = out_ref.shape[0]
    lines = size // LANES
    base = pos_ref[0] * tok_rows
    token = lax.broadcasted_iota(jnp.int32, (tok_rows, LANES), 0)
    weight_half = (weight_ref[...].astype(F32) * 0.5).astype(BF16)
    hidden = activate(out_ref[...], weight_half)
    ones = []
    for j in range(lines):
        ids = tok_ref[pl.ds(step * lines + j, 1), :] - base
        ones.append(jnp.where(token == ids, 1.0, 0.0))
    hot = jnp.concatenate(ones, axis=1).astype(BF16)
    count = functools.reduce(jnp.add, ones)
    part = dot(hot, hidden)

    @pl.when(step == 0)
    def _():
        sum_ref[...] = part
        cnt_ref[...] = count

    @pl.when(step > 0)
    def _():
        sum_ref[...] += part
        cnt_ref[...] += count


def pool(pos, atom_out, weight, tok2d, tok_rows, part):
    rows, width = atom_out.shape
    feats = weight.shape[1] // PARTS
    size = min(1024, rows)
    return pl.pallas_call(
        functools.partial(pool_kernel, tok_rows),
        grid_spec=pltpu.PrefetchScalarGridSpec(
            num_scalar_prefetch=1,
            grid=(rows // size,),
            in_specs=[
                pl.BlockSpec((size, width), lambda i, *_: (i, 0)),
                pl.BlockSpec((width, feats), lambda i, *_: (0, part)),
                full(tok2d.shape),
            ],
            out_specs=[full((tok_rows, feats)), full((tok_rows, LANES))],
        ),
        out_shape=[
            jax.ShapeDtypeStruct((tok_rows, feats), F32),
            jax.ShapeDtypeStruct((tok_rows, LANES), F32),
        ],
        compiler_params=params(VMEM_SMALL),
        cost_estimate=pl.CostEstimate(flops=2 * 10**9, bytes_accessed=2 * 10**6, transcendentals=10**6),
        name="pool",
    )(pos, atom_out, weight, tok2d)


def finish_kernel(msg_ref, weight_ref, sum_ref, cnt_ref, repr_ref):
    tok_rows = sum_ref.shape[0]
    size = msg_ref.shape[0] - 16
    lines = size // LANES
    token = lax.broadcasted_iota(jnp.int32, (tok_rows, LANES), 0).astype(F32)
    weight_half = (weight_ref[...].astype(F32) * 0.5).astype(BF16)
    hidden = activate(msg_ref[:size, :], weight_half)
    codes = msg_ref[size:, :].astype(F32)
    ids = codes[:8] * 16.0 + codes[8:] - 1.0
    ones = [jnp.where(token == ids[8 - lines + j : 9 - lines + j], 1.0, 0.0) for j in range(lines)]
    hot = jnp.concatenate(ones, axis=1).astype(BF16)
    count = functools.reduce(jnp.add, ones) + cnt_ref[...]
    sums = sum_ref[...] + dot(hot, hidden)
    repr_ref[...] = (sums / jnp.sum(count, axis=1, keepdims=True)).astype(BF16)


def finish(msg, weight, sums, counts, part):
    rows, feats = sums.shape
    return pl.pallas_call(
        finish_kernel,
        grid=(1,),
        in_specs=[
            full(msg.shape),
            pl.BlockSpec((weight.shape[0], feats), lambda i: (0, part)),
            full(sums.shape),
            full(counts.shape),
        ],
        out_specs=full((rows, feats)),
        out_shape=jax.ShapeDtypeStruct((rows, feats), BF16),
        compiler_params=params(VMEM_SMALL),
        cost_estimate=pl.CostEstimate(flops=2 * 10**8, bytes_accessed=2 * 10**6, transcendentals=2 * 10**5),
        name="token_finish",
    )(msg, weight, sums, counts)


def query_kernel(scale, a_ref, b_ref, gain_ref, weight_hbm, out_ref, weight_s, sem):
    copy = pltpu.make_async_copy(weight_hbm, weight_s, sem)
    copy.start()
    rows = jnp.concatenate([a_ref[...].astype(F32), b_ref[...].astype(F32)], axis=1)
    normed = norm_rows(rows, gain_ref[...].reshape(1, -1)).astype(BF16)
    copy.wait()
    out_ref[...] = (dot(normed, weight_s[...]) * scale).astype(BF16)


def project_queries(halves, gain, weight):
    rows = halves[0].shape[0]
    return pl.pallas_call(
        functools.partial(query_kernel, 1.0 / math.sqrt(weight.shape[1] // TH)),
        in_specs=[pl.BlockSpec(memory_space=pltpu.VMEM)] * 3 + [pl.BlockSpec(memory_space=pltpu.HBM)],
        out_shape=jax.ShapeDtypeStruct((rows, weight.shape[1]), BF16),
        scratch_shapes=[pltpu.VMEM(weight.shape, BF16), pltpu.SemaphoreType.DMA],
        compiler_params=params(VMEM_SMALL),
        cost_estimate=pl.CostEstimate(flops=5 * 10**8, bytes_accessed=3 * 10**6, transcendentals=0),
        name="queries",
    )(*halves, gain, weight)


GROUPS = 2
ROW_TILE = 32


def pack_message(mixed, lse, heads):
    lane = lax.broadcasted_iota(jnp.int32, lse.shape, 1)
    high = lse.astype(BF16).astype(F32)
    rest = lse - high
    middle = rest.astype(BF16).astype(F32)
    low = rest - middle
    first = jnp.where(lane < heads, high, pltpu.roll(middle, heads, 1))
    second = jnp.where(lane < heads, low, 0.0)
    turned = jnp.concatenate([first, second], axis=0).T
    return jnp.concatenate([mixed.astype(BF16), turned[: 2 * heads].astype(BF16)], axis=0)


def unpack_message(msg, rows, heads):
    coded = msg[rows:].astype(F32)
    coded = jnp.concatenate([coded, jnp.zeros((LANES - 2 * heads, coded.shape[1]), F32)], axis=0).T
    first = coded[:rows]
    return msg[:rows].astype(F32), first + pltpu.roll(first, LANES - heads, 1) + coded[rows:]


def merge_parts(mixed, lse, other, lse_b, heads):
    rows, feats = mixed.shape
    width = feats // heads
    spot = lax.broadcasted_iota(jnp.int32, (rows, LANES), 1)
    lse_b = jnp.where(spot < heads, lse_b, lse)
    top = jnp.maximum(lse, lse_b)
    part = jnp.exp(lse - top)
    total = part + jnp.exp(lse_b - top)
    share = part / total
    high = share.astype(BF16)
    low = (share - high.astype(F32)).astype(BF16)
    head = lax.broadcasted_iota(jnp.int32, (LANES, feats), 0) * width
    column = lax.broadcasted_iota(jnp.int32, (LANES, feats), 1)
    spread = jnp.where((column >= head) & (column < head + width), 1.0, 0.0).astype(BF16)
    wide = dot(high, spread) + dot(low, spread)
    return other + wide * (mixed - other), top + jnp.log(total)


def attend_group(group, heads, width, half, q_ref, k_ref, v_ref, bias_hbm, scratch):
    score_s, term_s, top_s, bias_s, mix_s, sems = scratch
    rows = mix_s.shape[0]
    at = pl.multiple_of(half * rows, rows)
    pairs = heads // 2
    spot = lax.broadcasted_iota(jnp.int32, (rows, LANES), 1)

    def layout(p):
        first = 2 * p * width
        low = first // LANES * LANES
        wide = -(-(first + 2 * width) // LANES) * LANES - low
        lane = lax.broadcasted_iota(jnp.int32, (rows, wide), 1)
        first -= low
        masks = [(lane >= first + j * width) & (lane < first + (j + 1) * width) for j in range(2)]
        return slice(low, low + wide), first, masks

    keys = score_s[0].shape[1]
    chunk = min(256, keys)
    chunks = keys // chunk
    tiles = 2 * rows // ROW_TILE

    def stack(p):
        window, _, masks = layout(p)
        query = q_ref[pl.ds(at, rows), window].astype(F32)
        return jnp.concatenate([jnp.where(m, query, 0.0).astype(BF16) for m in masks], axis=0)

    def score(p, n, stacked):
        part = slice(n * chunk, (n + 1) * chunk)
        score_s[p % 2][:, part] = dot_nt(stacked, k_ref[part, layout(p)[0]])

    def soften(p, n):
        for r in range(n * tiles // chunks * ROW_TILE, (n + 1) * tiles // chunks * ROW_TILE, ROW_TILE):
            bias = bias_s[2 * p + r // rows, r % rows : r % rows + ROW_TILE, :].astype(F32)
            scores = score_s[p % 2][r : r + ROW_TILE, :] + bias
            top = jnp.max(scores, axis=-1, keepdims=True)
            term_s[p % 2][r : r + ROW_TILE, :] = jnp.exp(scores - top).astype(BF16)
            top_s[p % 2][r : r + ROW_TILE, :] = jnp.broadcast_to(top, (ROW_TILE, LANES))

    def mix(p, n, mixed):
        part = slice(n * chunk, (n + 1) * chunk)
        window, first, _ = layout(p)
        values = v_ref[part, window]
        column = lax.broadcasted_iota(jnp.int32, values.shape, 1)
        used = (column >= first) & (column < first + 2 * width)
        more = dot(term_s[p % 2][:, part], jnp.where(used, values.astype(F32), 1.0).astype(BF16))
        return more if mixed is None else mixed + more

    def close(p, mixed, lse):
        window, first, masks = layout(p)
        free = 0 if first >= 16 else 2 * width
        total = mixed[:, free : free + 1]
        mixed = mixed / total
        sums = top_s[p % 2][...] + jnp.log(total)
        result = mix_s[:, window]
        for j in range(2):
            result = jnp.where(masks[j], mixed[j * rows : (j + 1) * rows], result)
            lse = jnp.where(spot == 2 * p + j, sums[j * rows : (j + 1) * rows], lse)
        mix_s[:, window] = result
        return lse

    copies = bias_copies(group, heads, half, bias_hbm, bias_s, sems)
    lse = jnp.zeros((rows, LANES), F32)
    stacked = stack(0)
    for n in range(chunks):
        score(0, n, stacked)
    copies[0].wait()
    for p in range(pairs):
        if p == 1:
            for copy in copies[1:]:
                copy.wait()
        mixed = None
        if p + 1 < pairs:
            stacked = stack(p + 1)
        for n in range(chunks):
            if p + 1 < pairs:
                score(p + 1, n, stacked)
            if p:
                mixed = mix(p - 1, n, mixed)
            soften(p, n)
        if p:
            lse = close(p - 1, mixed, lse)
    mixed = None
    for n in range(chunks):
        mixed = mix(pairs - 1, n, mixed)
    lse = close(pairs - 1, mixed, lse)
    return mix_s[...], lse


def bias_copies(group, heads, half, bias_hbm, bias_s, sems):
    rows = bias_s.shape[1]
    at = pl.multiple_of(half * rows, rows)
    return [
        pltpu.make_async_copy(
            bias_hbm.at[pl.ds(group * heads + 2 * p, 2), pl.ds(at, rows), :],
            bias_s.at[pl.ds(2 * p, 2)],
            sems.at[p],
        )
        for p in range(heads // 2)
    ]


def group_scratch(rows, keys, feats, heads):
    return [
        pltpu.VMEM((2 * rows, keys), F32),
        pltpu.VMEM((2 * rows, keys), F32),
        pltpu.VMEM((2 * rows, keys), BF16),
        pltpu.VMEM((2 * rows, keys), BF16),
        pltpu.VMEM((2 * rows, LANES), F32),
        pltpu.VMEM((2 * rows, LANES), F32),
        pltpu.VMEM((heads, rows, keys), BF16),
        pltpu.VMEM((rows, feats), F32),
        pltpu.SemaphoreType.DMA((heads // 2,)),
        pltpu.VMEM((2, 2 * feats, feats), BF16),
        pltpu.SemaphoreType.DMA((2,)),
    ]


def scratch_of(refs):
    return refs[:2], refs[2:4], refs[4:6], refs[6], refs[7], refs[8]


def weight_copies(group, weight_hbm, refs):
    weight_s, sems = refs[9:11]
    feats = weight_s.shape[2]
    return [
        pltpu.make_async_copy(
            weight_hbm.at[:, pl.ds((part * GROUPS + group) * feats, feats)], weight_s.at[part], sems.at[part]
        )
        for part in range(2)
    ]


def project_keys(x_ref, weight_s, copies, k_ref, v_ref):
    tile = x_ref.shape[0] // 2
    for part, ref in enumerate((k_ref, v_ref)):
        copies[part].wait()
        for r in range(0, x_ref.shape[0], tile):
            ref[r : r + tile, :] = dot(x_ref[r : r + tile, :], weight_s[part]).astype(BF16)


def first_kernel(heads, width, half_ref, core_ref, q_ref, own_a, own_b, other_a, other_b, gain_ref, weight_hbm,
                 bias_hbm, x_ref, k_ref, v_ref, msg_ref, *refs):
    scratch = scratch_of(refs)
    weights = weight_copies(0, weight_hbm, refs)
    for copy in weights:
        copy.start()
    for copy in bias_copies(0, heads, half_ref[0], bias_hbm, scratch[3], scratch[5]):
        copy.start()
    rows = own_a.shape[0]
    core = core_ref[0]
    gain = gain_ref[...].reshape(1, -1)
    for place, parts in ((core, (own_a, own_b)), (1 - core, (other_a, other_b))):
        values = jnp.concatenate([part[...].astype(F32) for part in parts], axis=1)
        x_ref[pl.ds(pl.multiple_of(place * rows, rows), rows), :] = norm_rows(values, gain).astype(BF16)
    project_keys(x_ref, refs[9], weights, k_ref, v_ref)
    mixed, lse = attend_group(0, heads, width, half_ref[0], q_ref, k_ref, v_ref, bias_hbm, scratch)
    msg_ref[...] = pack_message(mixed, lse, heads)


def next_kernel(group, heads, width, half_ref, q_ref, x_ref, weight_hbm, bias_hbm, k_ref, v_ref, msg_ref, *refs):
    scratch = scratch_of(refs)
    weights = weight_copies(group, weight_hbm, refs)
    for copy in weights:
        copy.start()
    for copy in bias_copies(group, heads, half_ref[0], bias_hbm, scratch[3], scratch[5]):
        copy.start()
    project_keys(x_ref, refs[9], weights, k_ref, v_ref)
    mixed, lse = attend_group(group, heads, width, half_ref[0], q_ref, k_ref, v_ref, bias_hbm, scratch)
    msg_ref[...] = pack_message(mixed, lse, heads)


def keep_kernel(group, heads, width, half_ref, q_ref, k_ref, v_ref, near_ref, bias_hbm, o_ref, lse_ref, msg_ref, *refs):
    scratch = scratch_of(refs)
    for copy in bias_copies(group, heads, half_ref[0], bias_hbm, scratch[3], scratch[5]):
        copy.start()
    mixed, lse = attend_group(group, heads, width, half_ref[0], q_ref, k_ref, v_ref, bias_hbm, scratch)
    rows = mixed.shape[0]
    mixed, lse = merge_parts(mixed, lse, *unpack_message(near_ref[...], rows, heads), heads)
    o_ref[...] = mixed
    lse_ref[...] = lse
    msg_ref[...] = pack_message(mixed, lse, heads)


def group_call(kernel, group, half, scalars, q, arrays, weights, bias, outs, name):
    tok_rows, all_feats = q.shape
    rows, keys, feats = tok_rows // 2, bias.shape[2], all_feats // GROUPS
    heads = TH // GROUPS
    shapes = {
        "x": ((keys, all_feats), BF16),
        "kv": ((keys, feats), BF16),
        "o": ((rows, feats), F32),
        "lse": ((rows, LANES), F32),
        "msg": ((rows + 2 * heads, feats), BF16),
    }
    return pl.pallas_call(
        functools.partial(kernel, heads, feats // heads),
        grid_spec=pltpu.PrefetchScalarGridSpec(
            num_scalar_prefetch=1 + len(scalars),
            grid=(1,),
            in_specs=[pl.BlockSpec((tok_rows, feats), lambda i, *_: (0, group))]
            + [full(array.shape) for array in arrays]
            + [pl.BlockSpec(memory_space=pltpu.HBM)] * (1 if weights is None else 2),
            out_specs=[full(shapes[out][0]) for out in outs],
            scratch_shapes=group_scratch(rows, keys, feats, heads),
        ),
        out_shape=[jax.ShapeDtypeStruct(*shapes[out]) for out in outs],
        compiler_params=params(VMEM_SMALL),
        cost_estimate=pl.CostEstimate(flops=4 * 10**9, bytes_accessed=4 * 10**6, transcendentals=10**6),
        name=name,
    )(half, *scalars, q, *arrays, *([] if weights is None else [weights]), bias)


def merge_kernel(heads, o_ref, lse_ref, msg_ref, out_ref, sum_ref, back_ref):
    rows = o_ref.shape[0]
    mixed, lse = merge_parts(o_ref[...], lse_ref[...], *unpack_message(msg_ref[...], rows, heads), heads)
    out_ref[...] = mixed
    sum_ref[...] = lse
    back_ref[...] = pack_message(mixed, lse, heads)


def merge(o, lse, msg):
    return pl.pallas_call(
        functools.partial(merge_kernel, TH // GROUPS),
        out_shape=[jax.ShapeDtypeStruct(a.shape, a.dtype) for a in (o, lse, msg)],
        compiler_params=params(VMEM_SMALL),
        name="merge",
    )(o, lse, msg)


def settle_kernel(heads, o_ref, lse_ref, msg_ref, out_ref):
    rows = o_ref.shape[0]
    mixed, _ = merge_parts(o_ref[...], lse_ref[...], *unpack_message(msg_ref[...], rows, heads), heads)
    out_ref[...] = mixed.astype(BF16)


def settle(o, lse, msg):
    return pl.pallas_call(
        functools.partial(settle_kernel, TH // GROUPS),
        out_shape=jax.ShapeDtypeStruct(o.shape, BF16),
        compiler_params=params(VMEM_SMALL),
        name="settle",
    )(o, lse, msg)


def output_kernel(half_ref, own_a, own_b, other_a, other_b, a_ref, b_ref, weight_ref, out_ref):
    rows, feats = own_a.shape
    for place, first, second in ((half_ref[0], own_a, own_b), (1 - half_ref[0], other_a, other_b)):
        mine = pl.ds(pl.multiple_of(place * rows, rows), rows)
        result = dot(first[...], weight_ref[:feats, :]) + dot(second[...], weight_ref[feats:, :])
        out_ref[mine, :feats] = (a_ref[mine, :].astype(F32) + result[:, :feats]).astype(BF16)
        out_ref[mine, feats:] = (b_ref[mine, :].astype(F32) + result[:, feats:]).astype(BF16)


def output_rows(half, own, other, token_repr, weight):
    rows = token_repr[0].shape[0]
    return pl.pallas_call(
        output_kernel,
        in_specs=[pl.BlockSpec(memory_space=pltpu.SMEM)] + [pl.BlockSpec(memory_space=pltpu.VMEM)] * 7,
        out_shape=jax.ShapeDtypeStruct((rows, weight.shape[1]), BF16),
        compiler_params=params(VMEM_SMALL),
        name="output_rows",
    )(half, *own, *other, *token_repr, weight)


def bits_of(count):
    return [1 << b for b in range(count.bit_length() - 1)]


def key_parts(halves):
    n_pb, n_ka = lax.axis_size("pb"), lax.axis_size("ka")
    cores = n_pb // n_ka
    chips = n_pb // cores
    shard, plane = lax.axis_index("pb"), lax.axis_index("ka")
    bits = bits_of(chips)
    core = lax.rem(shard, cores)
    away = jnp.bitwise_xor(shard // cores, plane)
    held = list(halves)
    for r in range(len(bits)):
        pairs = []
        gets = jnp.bool_(False)
        for c in range(cores):
            order = bits if c % 2 == 0 else bits[::-1]
            known = sum(order[:r])
            for k in range(n_ka):
                for j in range(chips):
                    if (j ^ k) & ~known == 0:
                        pairs.append(((j * cores + c) * n_ka + k, ((j ^ order[r]) * cores + c) * n_ka + k))
            fresh = (jnp.bitwise_and(away, ~(known + order[r])) == 0) & (jnp.bitwise_and(away, order[r]) != 0)
            gets = gets | (fresh & (core == c))
        held = [jnp.where(gets, lax.ppermute(part, ("pb", "ka"), pairs), part) for part in held]
    return held, [lax.ppermute(part, "pb", [(p, p ^ 1) for p in range(n_pb)]) for part in held]


def body(
    atoms,
    atom_gain,
    atom_qkv,
    atom_proj,
    atom_bias,
    window_shift,
    token_of_atom,
    agg_weight,
    token_gain,
    token_q,
    token_kv,
    token_o,
    pair_bias,
):
    n_pb, n_ka = lax.axis_size("pb"), lax.axis_size("ka")
    shard, plane = lax.axis_index("pb"), lax.axis_index("ka")
    rows, width = atoms.shape
    tok_rows = pair_bias.shape[1]
    half = WIN_K // 2
    up = [(i, i + 1) for i in range(n_pb - 1)]
    down = [(i + 1, i) for i in range(n_pb - 1)]
    pos = shard.astype(jnp.int32).reshape(1)
    tok2d = token_of_atom.reshape(rows // LANES, LANES)
    left = lax.ppermute(atoms[rows - half :], "pb", up)
    right = lax.ppermute(atoms[:half], "pb", down)
    atom_out, msg = atom_attention(
        window_shift, pos, atoms, left, right, atom_gain, atom_qkv, atom_proj,
        atom_bias, tok2d, tok_rows, rows * n_pb,
    )
    behind = lax.ppermute(msg, "pb", up)
    token_repr, own_keys, other_keys = [], [], []
    for part in range(PARTS):
        sums, counts = pool(pos, atom_out, agg_weight, tok2d, tok_rows, part)
        token_repr.append(finish(behind, agg_weight, sums, counts, part))
    own_keys, other_keys = key_parts(token_repr)
    queries = project_queries(token_repr, token_gain, token_q)
    parity = jnp.bitwise_and(plane ^ (plane >> 1), 1).astype(jnp.int32)
    core = lax.rem(shard, n_pb // n_ka).astype(jnp.int32)
    keep, send = parity.reshape(1), (1 - parity).reshape(1)
    swap = [(i, i ^ 1) for i in range(n_ka)]
    bits = bits_of(n_ka)[1:]

    def far(msg, bit):
        return lax.ppermute(msg, "ka", [(i, i ^ (2 * bit - 1)) for i in range(n_ka)])

    x, k, v, msg = group_call(
        first_kernel, 0, send, (core.reshape(1),), queries, (*own_keys, *other_keys, token_gain), token_kv,
        pair_bias, ("x", "kv", "kv", "msg"), "attend_first",
    )
    held, near = [(k, v)], [lax.ppermute(msg, "ka", swap)]
    for g in range(1, GROUPS):
        k, v, msg = group_call(
            functools.partial(next_kernel, g), g, send, (), queries, (x,), token_kv,
            pair_bias, ("kv", "kv", "msg"), "attend_next",
        )
        held.append((k, v))
        near.append(lax.ppermute(msg, "ka", swap))
    sums, gone = [], []
    for g in range(GROUPS):
        o, lse, msg = group_call(
            functools.partial(keep_kernel, g), g, keep, (), queries, (*held[g], near[g]), None,
            pair_bias, ("o", "lse", "msg"), "attend_keep",
        )
        sums.append((o, lse))
        gone.append(far(msg, bits[0]))
    own_mix, other_mix = [], []
    for g in range(GROUPS):
        (o, lse), got = sums[g], gone[g]
        for bit in bits[1:]:
            o, lse, msg = merge(o, lse, got)
            got = far(msg, bit)
        own_mix.append(settle(o, lse, got))
        other_mix.append(lax.ppermute(own_mix[g], "ka", swap))
    return atom_out, output_rows(keep, own_mix, other_mix, token_repr, token_o)


def solution(mesh):
    return jax.shard_map(
        body,
        mesh=mesh,
        in_specs=(
            P("pb", None),
            P(),
            P(),
            P(),
            P(None, "pb", None),
            P("pb"),
            P("pb"),
            P(),
            P(),
            P(),
            P(),
            P(),
            P(None, "pb", "ka"),
        ),
        out_specs=(P("pb", None), P("pb", None)),
        check_vma=False,
    )
```

```python
import functools
import math

import jax
import jax.numpy as jnp
from jax import lax
from jax.experimental import pallas as pl
from jax.experimental.pallas import tpu as pltpu
from jax.sharding import PartitionSpec as P

AH = 4
TH = 16
WIN_Q = 32
WIN_K = 128
SHIFT_MAX = 384
PARTS = 2
LANES = 128
F32 = jnp.float32
BF16 = jnp.bfloat16
VMEM_LIMIT = 56 * 1024 * 1024
VMEM_SMALL = 24 * 1024 * 1024


def full(shape):
    return pl.BlockSpec(shape, lambda *_: (0,) * len(shape))


def params(limit=VMEM_LIMIT):
    return pltpu.CompilerParams(vmem_limit_bytes=limit)


def norm_rows(as_float, gain):
    centre = jnp.mean(as_float, axis=-1, keepdims=True)
    spread = jnp.mean(jnp.square(as_float - centre), axis=-1, keepdims=True)
    return (as_float - centre) * lax.rsqrt(spread + 1e-05) * gain


def dot(a, b):
    return jnp.dot(a, b, preferred_element_type=F32)


def atom_kernel(
    chunks,
    atom_total,
    tok_rows,
    shift_ref,
    pos_ref,
    atoms_ref,
    left_ref,
    right_ref,
    gain_ref,
    qkv_ref,
    proj_ref,
    bias_ref,
    tok_ref,
    out_ref,
    msg_ref,
    q_s,
    k_s,
    v_s,
    mix_s,
    x_s,
):
    step = pl.program_id(0)
    rows, width = atoms_ref.shape
    size = out_ref.shape[0]
    half = WIN_K // 2
    head = width // AH
    shard = pos_ref[0]

    @pl.when(step == 0)
    def _():
        gain = gain_ref[...].reshape(1, width)
        x_s[:half, :] = left_ref[...]
        x_s[half : half + rows, :] = atoms_ref[...]
        x_s[half + rows :, :] = right_ref[...]
        total = rows + 2 * half
        tile = 5 * WIN_K if total % (5 * WIN_K) == 0 else WIN_K

        def one(c, carry):
            at = pl.ds(pl.multiple_of(c * tile, tile), tile)
            normed = norm_rows(x_s[at, :].astype(F32), gain).astype(BF16)
            res = dot(normed, qkv_ref[...])
            q_s[at, :] = (res[:, :width] * (1.0 / math.sqrt(head))).astype(BF16)
            k_s[:, at] = res[:, width : 2 * width].T.astype(BF16)
            v_s[at, :width] = res[:, 2 * width :].astype(BF16)
            v_s[at, width:] = jnp.ones((tile, width), BF16)
            return carry

        lax.fori_loop(0, total // tile, one, 0)

    group = WIN_K // WIN_Q
    atoms_group = group * WIN_Q
    span = AH * WIN_Q
    lane_q = lax.broadcasted_iota(jnp.int32, (WIN_Q, width), 1)
    heads = [(lane_q >= h * head) & (lane_q < (h + 1) * head) for h in range(AH)]
    lane = lax.broadcasted_iota(jnp.int32, (span, WIN_K), 1)
    slot = lax.broadcasted_iota(jnp.int32, (1, WIN_K), 1)
    blocks = size // WIN_Q

    def region(n):
        return pl.ds(pl.multiple_of(step * size + n // group * atoms_group, atoms_group), 2 * WIN_K)

    def score(n):
        query = q_s[pl.ds(pl.multiple_of(step * size + n * WIN_Q + half, WIN_Q), WIN_Q), :].astype(F32)
        stacked = jnp.concatenate([jnp.where(m, query, 0.0).astype(BF16) for m in heads], axis=0)
        return dot(stacked, k_s[:, region(n)])

    def soften(n, scores):
        offset = n % group * WIN_Q + half + shift_ref[step * blocks + n]
        early = lane >= offset
        begin = n * WIN_Q
        bias = bias_ref[:, begin : begin + WIN_Q, :].astype(F32).reshape(span, WIN_K)
        index = slot + jnp.where(slot >= offset, 0, WIN_K)
        index = index + (step * size + n // group * atoms_group + shard * rows - half)
        shut = jnp.where((index >= 0) & (index < atom_total), 0.0, -jnp.inf)
        logits = jnp.where(early, scores[:, :WIN_K], scores[:, WIN_K:]) + (
            pltpu.roll(bias, jnp.bitwise_and(offset, WIN_K - 1), 1) + shut
        )
        terms = jnp.exp(logits - jnp.max(logits, axis=-1, keepdims=True))
        return jnp.concatenate(
            [jnp.where(early, terms, 0.0).astype(BF16), jnp.where(early, 0.0, terms).astype(BF16)], axis=1
        )

    def mix(n, weights):
        mixed = dot(weights, v_s[region(n), :])
        values, total = mixed[:WIN_Q, :width], mixed[:WIN_Q, width:]
        for h in range(1, AH):
            part = mixed[h * WIN_Q : (h + 1) * WIN_Q]
            values = jnp.where(heads[h], part[:, :width], values)
            total = jnp.where(heads[h], part[:, width:], total)
        mix_s[n * WIN_Q : (n + 1) * WIN_Q, :] = (values / total).astype(BF16)

    def project_out(g):
        local = g * atoms_group
        at = pl.multiple_of(step * size + local, atoms_group)
        own = atoms_ref[pl.ds(at, atoms_group), :].astype(F32)
        result = own + dot(mix_s[local : local + atoms_group, :], proj_ref[...])
        out_ref[local : local + atoms_group, :] = result.astype(BF16)

    ahead = score(0)
    behind = None
    for n in range(blocks):
        scores = ahead
        if n + 1 < blocks:
            ahead = score(n + 1)
        if n:
            mix(n - 1, behind)
        behind = soften(n, scores)
        if n % group == 0 and n:
            project_out(n // group - 1)
    mix(blocks - 1, behind)
    project_out(blocks // group - 1)

    @pl.when(step == chunks - 1)
    def _():
        ids = tok_ref[tok_ref.shape[0] - 8 :, :]
        code = jnp.maximum(ids - (shard + 1) * tok_rows + 1, 0)
        high = (code >> 4).astype(F32)
        low = (code & 15).astype(F32)
        msg_ref[:SHIFT_MAX, :] = out_ref[size - SHIFT_MAX :, :]
        msg_ref[SHIFT_MAX:, :] = jnp.concatenate([high, low], axis=0).astype(BF16)


def atom_attention(shift, pos, atoms, left, right, gain, qkv, proj, bias, tok2d, tok_rows, atom_total):
    rows, width = atoms.shape
    size = 2 * SHIFT_MAX
    chunks = rows // size
    half = WIN_K // 2
    return pl.pallas_call(
        functools.partial(atom_kernel, chunks, atom_total, tok_rows),
        grid_spec=pltpu.PrefetchScalarGridSpec(
            num_scalar_prefetch=2,
            grid=(chunks,),
            in_specs=[
                full((rows, width)),
                full((half, width)),
                full((half, width)),
                full((width,)),
                full(qkv.shape),
                full(proj.shape),
                pl.BlockSpec((AH, size, WIN_K), lambda i, *_: (0, i, 0)),
                full(tok2d.shape),
            ],
            out_specs=[
                pl.BlockSpec((size, width), lambda i, *_: (i, 0)),
                full((SHIFT_MAX + 16, width)),
            ],
            scratch_shapes=[
                pltpu.VMEM((rows + 2 * half, width), BF16),
                pltpu.VMEM((width, rows + 2 * half), BF16),
                pltpu.VMEM((rows + 2 * half, 2 * width), BF16),
                pltpu.VMEM((size, width), BF16),
                pltpu.VMEM((rows + 2 * half, width), BF16),
            ],
        ),
        out_shape=[
            jax.ShapeDtypeStruct((rows, width), BF16),
            jax.ShapeDtypeStruct((SHIFT_MAX + 16, width), BF16),
        ],
        compiler_params=params(),
        cost_estimate=pl.CostEstimate(flops=8 * 10**9, bytes_accessed=6 * 10**6, transcendentals=2 * 10**6),
        name="atom_attention",
    )(shift, pos, atoms, left, right, gain, qkv, proj, bias, tok2d)


def activate(rows, weight_half):
    u = dot(rows, weight_half)
    return (u + u * jnp.tanh(u)).astype(BF16)


def pool_kernel(tok_rows, pos_ref, out_ref, weight_ref, tok_ref, sum_ref, cnt_ref):
    step = pl.program_id(0)
    size = out_ref.shape[0]
    lines = size // LANES
    base = pos_ref[0] * tok_rows
    token = lax.broadcasted_iota(jnp.int32, (tok_rows, LANES), 0)
    weight_half = (weight_ref[...].astype(F32) * 0.5).astype(BF16)
    hidden = activate(out_ref[...], weight_half)
    ones = []
    for j in range(lines):
        ids = tok_ref[pl.ds(step * lines + j, 1), :] - base
        ones.append(jnp.where(token == ids, 1.0, 0.0))
    hot = jnp.concatenate(ones, axis=1).astype(BF16)
    count = functools.reduce(jnp.add, ones)
    part = dot(hot, hidden)

    @pl.when(step == 0)
    def _():
        sum_ref[...] = part
        cnt_ref[...] = count

    @pl.when(step > 0)
    def _():
        sum_ref[...] += part
        cnt_ref[...] += count


def pool(pos, atom_out, weight, tok2d, tok_rows, part):
    rows, width = atom_out.shape
    feats = weight.shape[1] // PARTS
    size = min(1024, rows)
    return pl.pallas_call(
        functools.partial(pool_kernel, tok_rows),
        grid_spec=pltpu.PrefetchScalarGridSpec(
            num_scalar_prefetch=1,
            grid=(rows // size,),
            in_specs=[
                pl.BlockSpec((size, width), lambda i, *_: (i, 0)),
                pl.BlockSpec((width, feats), lambda i, *_: (0, part)),
                full(tok2d.shape),
            ],
            out_specs=[full((tok_rows, feats)), full((tok_rows, LANES))],
        ),
        out_shape=[
            jax.ShapeDtypeStruct((tok_rows, feats), F32),
            jax.ShapeDtypeStruct((tok_rows, LANES), F32),
        ],
        compiler_params=params(VMEM_SMALL),
        cost_estimate=pl.CostEstimate(flops=2 * 10**9, bytes_accessed=2 * 10**6, transcendentals=10**6),
        name="pool",
    )(pos, atom_out, weight, tok2d)


def finish_kernel(msg_ref, weight_ref, sum_ref, cnt_ref, repr_ref):
    tok_rows = sum_ref.shape[0]
    size = msg_ref.shape[0] - 16
    lines = size // LANES
    token = lax.broadcasted_iota(jnp.int32, (tok_rows, LANES), 0).astype(F32)
    weight_half = (weight_ref[...].astype(F32) * 0.5).astype(BF16)
    hidden = activate(msg_ref[:size, :], weight_half)
    codes = msg_ref[size:, :].astype(F32)
    ids = codes[:8] * 16.0 + codes[8:] - 1.0
    ones = [jnp.where(token == ids[8 - lines + j : 9 - lines + j], 1.0, 0.0) for j in range(lines)]
    hot = jnp.concatenate(ones, axis=1).astype(BF16)
    count = functools.reduce(jnp.add, ones) + cnt_ref[...]
    sums = sum_ref[...] + dot(hot, hidden)
    repr_ref[...] = (sums / jnp.sum(count, axis=1, keepdims=True)).astype(BF16)


def finish(msg, weight, sums, counts, part):
    rows, feats = sums.shape
    return pl.pallas_call(
        finish_kernel,
        grid=(1,),
        in_specs=[
            full(msg.shape),
            pl.BlockSpec((weight.shape[0], feats), lambda i: (0, part)),
            full(sums.shape),
            full(counts.shape),
        ],
        out_specs=full((rows, feats)),
        out_shape=jax.ShapeDtypeStruct((rows, feats), BF16),
        compiler_params=params(VMEM_SMALL),
        cost_estimate=pl.CostEstimate(flops=2 * 10**8, bytes_accessed=2 * 10**6, transcendentals=2 * 10**5),
        name="token_finish",
    )(msg, weight, sums, counts)


def query_kernel(scale, a_ref, b_ref, gain_ref, weight_hbm, out_ref, weight_s, sem):
    copy = pltpu.make_async_copy(weight_hbm, weight_s, sem)
    copy.start()
    rows = jnp.concatenate([a_ref[...].astype(F32), b_ref[...].astype(F32)], axis=1)
    normed = norm_rows(rows, gain_ref[...].reshape(1, -1)).astype(BF16)
    copy.wait()
    out_ref[...] = (dot(normed, weight_s[...]) * scale).astype(BF16)


def project_queries(halves, gain, weight):
    rows = halves[0].shape[0]
    return pl.pallas_call(
        functools.partial(query_kernel, 1.0 / math.sqrt(weight.shape[1] // TH)),
        in_specs=[pl.BlockSpec(memory_space=pltpu.VMEM)] * 3 + [pl.BlockSpec(memory_space=pltpu.HBM)],
        out_shape=jax.ShapeDtypeStruct((rows, weight.shape[1]), BF16),
        scratch_shapes=[pltpu.VMEM(weight.shape, BF16), pltpu.SemaphoreType.DMA],
        compiler_params=params(VMEM_SMALL),
        cost_estimate=pl.CostEstimate(flops=5 * 10**8, bytes_accessed=3 * 10**6, transcendentals=0),
        name="queries",
    )(*halves, gain, weight)


GROUPS = 2
ROW_TILE = 32


def pack_message(mixed, lse, heads):
    lane = lax.broadcasted_iota(jnp.int32, lse.shape, 1)
    high = lse.astype(BF16).astype(F32)
    rest = lse - high
    middle = rest.astype(BF16).astype(F32)
    low = rest - middle
    first = jnp.where(lane < heads, high, pltpu.roll(middle, heads, 1))
    second = jnp.where(lane < heads, low, 0.0)
    turned = jnp.concatenate([first, second], axis=0).T
    return jnp.concatenate([mixed.astype(BF16), turned[: 2 * heads].astype(BF16)], axis=0)


def unpack_message(msg, rows, heads):
    coded = msg[rows:].astype(F32)
    coded = jnp.concatenate([coded, jnp.zeros((LANES - 2 * heads, coded.shape[1]), F32)], axis=0).T
    first = coded[:rows]
    return msg[:rows].astype(F32), first + pltpu.roll(first, LANES - heads, 1) + coded[rows:]


def merge_parts(mixed, lse, other, lse_b, heads):
    rows, feats = mixed.shape
    width = feats // heads
    spot = lax.broadcasted_iota(jnp.int32, (rows, LANES), 1)
    lse_b = jnp.where(spot < heads, lse_b, lse)
    top = jnp.maximum(lse, lse_b)
    part = jnp.exp(lse - top)
    total = part + jnp.exp(lse_b - top)
    share = part / total
    high = share.astype(BF16)
    low = (share - high.astype(F32)).astype(BF16)
    head = lax.broadcasted_iota(jnp.int32, (LANES, feats), 0) * width
    column = lax.broadcasted_iota(jnp.int32, (LANES, feats), 1)
    spread = jnp.where((column >= head) & (column < head + width), 1.0, 0.0).astype(BF16)
    wide = dot(high, spread) + dot(low, spread)
    return other + wide * (mixed - other), top + jnp.log(total)


def attend_group(group, heads, width, half, q_ref, k_ref, v_ref, bias_hbm, scratch):
    score_s, term_s, top_s, bias_s, mix_s, sems = scratch
    rows = mix_s.shape[0]
    at = pl.multiple_of(half * rows, rows)
    pairs = heads // 2
    spot = lax.broadcasted_iota(jnp.int32, (rows, LANES), 1)

    def layout(p):
        first = 2 * p * width
        low = first // LANES * LANES
        wide = -(-(first + 2 * width) // LANES) * LANES - low
        lane = lax.broadcasted_iota(jnp.int32, (rows, wide), 1)
        first -= low
        masks = [(lane >= first + j * width) & (lane < first + (j + 1) * width) for j in range(2)]
        return slice(low, low + wide), first, masks

    keys = score_s[0].shape[1]
    chunk = min(256, keys)
    chunks = keys // chunk
    tiles = 2 * rows // ROW_TILE

    def stack(p):
        window, _, masks = layout(p)
        query = q_ref[pl.ds(at, rows), window].astype(F32)
        return jnp.concatenate([jnp.where(m, query, 0.0).astype(BF16) for m in masks], axis=0)

    def score(p, n, stacked):
        part = slice(n * chunk, (n + 1) * chunk)
        score_s[p % 2][:, part] = dot(stacked, k_ref[layout(p)[0], part])

    def soften(p, n):
        for r in range(n * tiles // chunks * ROW_TILE, (n + 1) * tiles // chunks * ROW_TILE, ROW_TILE):
            bias = bias_s[2 * p + r // rows, r % rows : r % rows + ROW_TILE, :].astype(F32)
            scores = score_s[p % 2][r : r + ROW_TILE, :] + bias
            top = jnp.max(scores, axis=-1, keepdims=True)
            term_s[p % 2][r : r + ROW_TILE, :] = jnp.exp(scores - top).astype(BF16)
            top_s[p % 2][r : r + ROW_TILE, :] = jnp.broadcast_to(top, (ROW_TILE, LANES))

    def mix(p, n, mixed):
        part = slice(n * chunk, (n + 1) * chunk)
        window, first, _ = layout(p)
        values = v_ref[part, window]
        column = lax.broadcasted_iota(jnp.int32, values.shape, 1)
        used = (column >= first) & (column < first + 2 * width)
        more = dot(term_s[p % 2][:, part], jnp.where(used, values.astype(F32), 1.0).astype(BF16))
        return more if mixed is None else mixed + more

    def close(p, mixed, lse):
        window, first, masks = layout(p)
        free = 0 if first >= 16 else 2 * width
        total = mixed[:, free : free + 1]
        mixed = mixed / total
        sums = top_s[p % 2][...] + jnp.log(total)
        result = mix_s[:, window]
        for j in range(2):
            result = jnp.where(masks[j], mixed[j * rows : (j + 1) * rows], result)
            lse = jnp.where(spot == 2 * p + j, sums[j * rows : (j + 1) * rows], lse)
        mix_s[:, window] = result
        return lse

    copies = bias_copies(group, heads, half, bias_hbm, bias_s, sems)
    lse = jnp.zeros((rows, LANES), F32)
    stacked = stack(0)
    for n in range(chunks):
        score(0, n, stacked)
    copies[0].wait()
    for p in range(pairs):
        if p == 1:
            for copy in copies[1:]:
                copy.wait()
        mixed = None
        if p + 1 < pairs:
            stacked = stack(p + 1)
        for n in range(chunks):
            if p + 1 < pairs:
                score(p + 1, n, stacked)
            if p:
                mixed = mix(p - 1, n, mixed)
            soften(p, n)
        if p:
            lse = close(p - 1, mixed, lse)
    mixed = None
    for n in range(chunks):
        mixed = mix(pairs - 1, n, mixed)
    lse = close(pairs - 1, mixed, lse)
    return mix_s[...], lse


def bias_copies(group, heads, half, bias_hbm, bias_s, sems):
    rows = bias_s.shape[1]
    at = pl.multiple_of(half * rows, rows)
    return [
        pltpu.make_async_copy(
            bias_hbm.at[pl.ds(group * heads + 2 * p, 2), pl.ds(at, rows), :],
            bias_s.at[pl.ds(2 * p, 2)],
            sems.at[p],
        )
        for p in range(heads // 2)
    ]


def group_scratch(rows, keys, feats, heads):
    return [
        pltpu.VMEM((2 * rows, keys), F32),
        pltpu.VMEM((2 * rows, keys), F32),
        pltpu.VMEM((2 * rows, keys), BF16),
        pltpu.VMEM((2 * rows, keys), BF16),
        pltpu.VMEM((2 * rows, LANES), F32),
        pltpu.VMEM((2 * rows, LANES), F32),
        pltpu.VMEM((heads, rows, keys), BF16),
        pltpu.VMEM((rows, feats), F32),
        pltpu.SemaphoreType.DMA((heads // 2,)),
        pltpu.VMEM((2, 2 * feats, feats), BF16),
        pltpu.SemaphoreType.DMA((2,)),
    ]


def scratch_of(refs):
    return refs[:2], refs[2:4], refs[4:6], refs[6], refs[7], refs[8]


def weight_copies(group, weight_hbm, refs):
    weight_s, sems = refs[9:11]
    feats = weight_s.shape[2]
    return [
        pltpu.make_async_copy(
            weight_hbm.at[:, pl.ds((part * GROUPS + group) * feats, feats)], weight_s.at[part], sems.at[part]
        )
        for part in range(2)
    ]


def project_keys(x_ref, weight_s, copies, k_ref, v_ref):
    tile = x_ref.shape[0] // 2
    copies[0].wait()
    for r in range(0, x_ref.shape[0], tile):
        k_ref[:, r : r + tile] = dot(x_ref[r : r + tile, :], weight_s[0]).T.astype(BF16)
    copies[1].wait()
    for r in range(0, x_ref.shape[0], tile):
        v_ref[r : r + tile, :] = dot(x_ref[r : r + tile, :], weight_s[1]).astype(BF16)


def first_kernel(heads, width, half_ref, core_ref, q_ref, own_a, own_b, other_a, other_b, gain_ref, weight_hbm,
                 bias_hbm, x_ref, k_ref, v_ref, msg_ref, *refs):
    scratch = scratch_of(refs)
    weights = weight_copies(0, weight_hbm, refs)
    for copy in weights:
        copy.start()
    for copy in bias_copies(0, heads, half_ref[0], bias_hbm, scratch[3], scratch[5]):
        copy.start()
    rows = own_a.shape[0]
    core = core_ref[0]
    gain = gain_ref[...].reshape(1, -1)
    for place, parts in ((core, (own_a, own_b)), (1 - core, (other_a, other_b))):
        values = jnp.concatenate([part[...].astype(F32) for part in parts], axis=1)
        x_ref[pl.ds(pl.multiple_of(place * rows, rows), rows), :] = norm_rows(values, gain).astype(BF16)
    project_keys(x_ref, refs[9], weights, k_ref, v_ref)
    mixed, lse = attend_group(0, heads, width, half_ref[0], q_ref, k_ref, v_ref, bias_hbm, scratch)
    msg_ref[...] = pack_message(mixed, lse, heads)


def next_kernel(group, heads, width, half_ref, q_ref, x_ref, weight_hbm, bias_hbm, k_ref, v_ref, msg_ref, *refs):
    scratch = scratch_of(refs)
    weights = weight_copies(group, weight_hbm, refs)
    for copy in weights:
        copy.start()
    for copy in bias_copies(group, heads, half_ref[0], bias_hbm, scratch[3], scratch[5]):
        copy.start()
    project_keys(x_ref, refs[9], weights, k_ref, v_ref)
    mixed, lse = attend_group(group, heads, width, half_ref[0], q_ref, k_ref, v_ref, bias_hbm, scratch)
    msg_ref[...] = pack_message(mixed, lse, heads)


def keep_kernel(group, heads, width, half_ref, q_ref, k_ref, v_ref, near_ref, bias_hbm, o_ref, lse_ref, msg_ref, *refs):
    scratch = scratch_of(refs)
    for copy in bias_copies(group, heads, half_ref[0], bias_hbm, scratch[3], scratch[5]):
        copy.start()
    mixed, lse = attend_group(group, heads, width, half_ref[0], q_ref, k_ref, v_ref, bias_hbm, scratch)
    rows = mixed.shape[0]
    mixed, lse = merge_parts(mixed, lse, *unpack_message(near_ref[...], rows, heads), heads)
    o_ref[...] = mixed
    lse_ref[...] = lse
    msg_ref[...] = pack_message(mixed, lse, heads)


def group_call(kernel, group, half, scalars, q, arrays, weights, bias, outs, name):
    tok_rows, all_feats = q.shape
    rows, keys, feats = tok_rows // 2, bias.shape[2], all_feats // GROUPS
    heads = TH // GROUPS
    shapes = {
        "x": ((keys, all_feats), BF16),
        "k": ((feats, keys), BF16),
        "v": ((keys, feats), BF16),
        "o": ((rows, feats), F32),
        "lse": ((rows, LANES), F32),
        "msg": ((rows + 2 * heads, feats), BF16),
    }
    return pl.pallas_call(
        functools.partial(kernel, heads, feats // heads),
        grid_spec=pltpu.PrefetchScalarGridSpec(
            num_scalar_prefetch=1 + len(scalars),
            grid=(1,),
            in_specs=[pl.BlockSpec((tok_rows, feats), lambda i, *_: (0, group))]
            + [full(array.shape) for array in arrays]
            + [pl.BlockSpec(memory_space=pltpu.HBM)] * (1 if weights is None else 2),
            out_specs=[full(shapes[out][0]) for out in outs],
            scratch_shapes=group_scratch(rows, keys, feats, heads),
        ),
        out_shape=[jax.ShapeDtypeStruct(*shapes[out]) for out in outs],
        compiler_params=params(),
        cost_estimate=pl.CostEstimate(flops=4 * 10**9, bytes_accessed=4 * 10**6, transcendentals=10**6),
        name=name,
    )(half, *scalars, q, *arrays, *([] if weights is None else [weights]), bias)


def merge_kernel(heads, o_ref, lse_ref, msg_ref, out_ref, sum_ref, back_ref):
    rows = o_ref.shape[0]
    mixed, lse = merge_parts(o_ref[...], lse_ref[...], *unpack_message(msg_ref[...], rows, heads), heads)
    out_ref[...] = mixed
    sum_ref[...] = lse
    back_ref[...] = pack_message(mixed, lse, heads)


def merge(o, lse, msg):
    return pl.pallas_call(
        functools.partial(merge_kernel, TH // GROUPS),
        out_shape=[jax.ShapeDtypeStruct(a.shape, a.dtype) for a in (o, lse, msg)],
        compiler_params=params(VMEM_SMALL),
        name="merge",
    )(o, lse, msg)


def settle_kernel(heads, o_ref, lse_ref, msg_ref, out_ref):
    rows = o_ref.shape[0]
    mixed, _ = merge_parts(o_ref[...], lse_ref[...], *unpack_message(msg_ref[...], rows, heads), heads)
    out_ref[...] = mixed.astype(BF16)


def settle(o, lse, msg):
    return pl.pallas_call(
        functools.partial(settle_kernel, TH // GROUPS),
        out_shape=jax.ShapeDtypeStruct(o.shape, BF16),
        compiler_params=params(VMEM_SMALL),
        name="settle",
    )(o, lse, msg)


def output_kernel(half_ref, own_a, own_b, other_a, other_b, a_ref, b_ref, weight_ref, out_ref):
    rows, feats = own_a.shape
    for place, first, second in ((half_ref[0], own_a, own_b), (1 - half_ref[0], other_a, other_b)):
        mine = pl.ds(pl.multiple_of(place * rows, rows), rows)
        result = dot(first[...], weight_ref[:feats, :]) + dot(second[...], weight_ref[feats:, :])
        out_ref[mine, :feats] = (a_ref[mine, :].astype(F32) + result[:, :feats]).astype(BF16)
        out_ref[mine, feats:] = (b_ref[mine, :].astype(F32) + result[:, feats:]).astype(BF16)


def output_rows(half, own, other, token_repr, weight):
    rows = token_repr[0].shape[0]
    return pl.pallas_call(
        output_kernel,
        in_specs=[pl.BlockSpec(memory_space=pltpu.SMEM)] + [pl.BlockSpec(memory_space=pltpu.VMEM)] * 7,
        out_shape=jax.ShapeDtypeStruct((rows, weight.shape[1]), BF16),
        compiler_params=params(VMEM_SMALL),
        name="output_rows",
    )(half, *own, *other, *token_repr, weight)


def bits_of(count):
    return [1 << b for b in range(count.bit_length() - 1)]


def key_parts(halves):
    n_pb, n_ka = lax.axis_size("pb"), lax.axis_size("ka")
    cores = n_pb // n_ka
    chips = n_pb // cores
    shard, plane = lax.axis_index("pb"), lax.axis_index("ka")
    bits = bits_of(chips)
    core = lax.rem(shard, cores)
    away = jnp.bitwise_xor(shard // cores, plane)
    held = list(halves)
    for r in range(len(bits)):
        pairs = []
        gets = jnp.bool_(False)
        for c in range(cores):
            order = bits if c % 2 == 0 else bits[::-1]
            known = sum(order[:r])
            for k in range(n_ka):
                for j in range(chips):
                    if (j ^ k) & ~known == 0:
                        pairs.append(((j * cores + c) * n_ka + k, ((j ^ order[r]) * cores + c) * n_ka + k))
            fresh = (jnp.bitwise_and(away, ~(known + order[r])) == 0) & (jnp.bitwise_and(away, order[r]) != 0)
            gets = gets | (fresh & (core == c))
        held = [jnp.where(gets, lax.ppermute(part, ("pb", "ka"), pairs), part) for part in held]
    return held, [lax.ppermute(part, "pb", [(p, p ^ 1) for p in range(n_pb)]) for part in held]


def body(
    atoms,
    atom_gain,
    atom_qkv,
    atom_proj,
    atom_bias,
    window_shift,
    token_of_atom,
    agg_weight,
    token_gain,
    token_q,
    token_kv,
    token_o,
    pair_bias,
):
    n_pb, n_ka = lax.axis_size("pb"), lax.axis_size("ka")
    shard, plane = lax.axis_index("pb"), lax.axis_index("ka")
    rows, width = atoms.shape
    tok_rows = pair_bias.shape[1]
    half = WIN_K // 2
    up = [(i, i + 1) for i in range(n_pb - 1)]
    down = [(i + 1, i) for i in range(n_pb - 1)]
    pos = shard.astype(jnp.int32).reshape(1)
    tok2d = token_of_atom.reshape(rows // LANES, LANES)
    left = lax.ppermute(atoms[rows - half :], "pb", up)
    right = lax.ppermute(atoms[:half], "pb", down)
    atom_out, msg = atom_attention(
        window_shift, pos, atoms, left, right, atom_gain, atom_qkv, atom_proj,
        atom_bias, tok2d, tok_rows, rows * n_pb,
    )
    behind = lax.ppermute(msg, "pb", up)
    token_repr, own_keys, other_keys = [], [], []
    for part in range(PARTS):
        sums, counts = pool(pos, atom_out, agg_weight, tok2d, tok_rows, part)
        token_repr.append(finish(behind, agg_weight, sums, counts, part))
    own_keys, other_keys = key_parts(token_repr)
    queries = project_queries(token_repr, token_gain, token_q)
    parity = jnp.bitwise_and(plane ^ (plane >> 1), 1).astype(jnp.int32)
    core = lax.rem(shard, n_pb // n_ka).astype(jnp.int32)
    keep, send = parity.reshape(1), (1 - parity).reshape(1)
    swap = [(i, i ^ 1) for i in range(n_ka)]
    bits = bits_of(n_ka)[1:]

    def far(msg, bit):
        return lax.ppermute(msg, "ka", [(i, i ^ (2 * bit - 1)) for i in range(n_ka)])

    x, k, v, msg = group_call(
        first_kernel, 0, send, (core.reshape(1),), queries, (*own_keys, *other_keys, token_gain), token_kv,
        pair_bias, ("x", "k", "v", "msg"), "attend_first",
    )
    held, near = [(k, v)], [lax.ppermute(msg, "ka", swap)]
    for g in range(1, GROUPS):
        k, v, msg = group_call(
            functools.partial(next_kernel, g), g, send, (), queries, (x,), token_kv,
            pair_bias, ("k", "v", "msg"), "attend_next",
        )
        held.append((k, v))
        near.append(lax.ppermute(msg, "ka", swap))
    sums, gone = [], []
    for g in range(GROUPS):
        o, lse, msg = group_call(
            functools.partial(keep_kernel, g), g, keep, (), queries, (*held[g], near[g]), None,
            pair_bias, ("o", "lse", "msg"), "attend_keep",
        )
        sums.append((o, lse))
        gone.append(far(msg, bits[0]))
    own_mix, other_mix = [], []
    for g in range(GROUPS):
        (o, lse), got = sums[g], gone[g]
        for bit in bits[1:]:
            o, lse, msg = merge(o, lse, got)
            got = far(msg, bit)
        own_mix.append(settle(o, lse, got))
        other_mix.append(lax.ppermute(own_mix[g], "ka", swap))
    return atom_out, output_rows(keep, own_mix, other_mix, token_repr, token_o)


def solution(mesh):
    return jax.shard_map(
        body,
        mesh=mesh,
        in_specs=(
            P("pb", None),
            P(),
            P(),
            P(),
            P(None, "pb", None),
            P("pb"),
            P("pb"),
            P(),
            P(),
            P(),
            P(),
            P(),
            P(None, "pb", "ka"),
        ),
        out_specs=(P("pb", None), P("pb", None)),
        check_vma=False,
    )
```

```python
import functools
import math

import jax
import jax.numpy as jnp
from jax import lax
from jax.experimental import pallas as pl
from jax.experimental.pallas import tpu as pltpu
from jax.sharding import PartitionSpec as P

AH = 4
TH = 16
WIN_Q = 32
WIN_K = 128
SHIFT_MAX = 384
PARTS = 2
LANES = 128
F32 = jnp.float32
BF16 = jnp.bfloat16
VMEM_LIMIT = 56 * 1024 * 1024
VMEM_SMALL = 24 * 1024 * 1024


def full(shape):
    return pl.BlockSpec(shape, lambda *_: (0,) * len(shape))


def params(limit=VMEM_LIMIT):
    return pltpu.CompilerParams(vmem_limit_bytes=limit)


def norm_rows(as_float, gain):
    centre = jnp.mean(as_float, axis=-1, keepdims=True)
    spread = jnp.mean(jnp.square(as_float - centre), axis=-1, keepdims=True)
    return (as_float - centre) * lax.rsqrt(spread + 1e-05) * gain


def dot(a, b):
    return jnp.dot(a, b, preferred_element_type=F32)


def atom_kernel(
    chunks,
    atom_total,
    tok_rows,
    shift_ref,
    pos_ref,
    atoms_ref,
    left_ref,
    right_ref,
    gain_ref,
    qkv_ref,
    proj_ref,
    bias_ref,
    tok_ref,
    out_ref,
    msg_ref,
    q_s,
    k_s,
    v_s,
    x_s,
):
    step = pl.program_id(0)
    rows, width = atoms_ref.shape
    size = out_ref.shape[0]
    half = WIN_K // 2
    head = width // AH
    shard = pos_ref[0]

    @pl.when(step == 0)
    def _():
        gain = gain_ref[...].reshape(1, width)
        x_s[:half, :] = left_ref[...]
        x_s[half : half + rows, :] = atoms_ref[...]
        x_s[half + rows :, :] = right_ref[...]
        total = rows + 2 * half
        tile = 5 * WIN_K if total % (5 * WIN_K) == 0 else WIN_K

        def one(c, carry):
            at = pl.ds(pl.multiple_of(c * tile, tile), tile)
            normed = norm_rows(x_s[at, :].astype(F32), gain).astype(BF16)
            res = dot(normed, qkv_ref[...])
            q_s[at, :] = (res[:, :width] * (1.0 / math.sqrt(head))).astype(BF16)
            k_s[:, at] = res[:, width : 2 * width].T.astype(BF16)
            v_s[at, :width] = res[:, 2 * width :].astype(BF16)
            v_s[at, width:] = jnp.ones((tile, width), BF16)
            return carry

        lax.fori_loop(0, total // tile, one, 0, unroll=True)

    group = WIN_K // WIN_Q
    atoms_group = group * WIN_Q
    span = AH * WIN_Q
    lane_q = lax.broadcasted_iota(jnp.int32, (WIN_Q, width), 1)
    heads = [(lane_q >= h * head) & (lane_q < (h + 1) * head) for h in range(AH)]
    lane = lax.broadcasted_iota(jnp.int32, (span, WIN_K), 1)
    slot = lax.broadcasted_iota(jnp.int32, (1, WIN_K), 1)
    blocks = size // WIN_Q

    def region(n):
        return pl.ds(pl.multiple_of(step * size + n // group * atoms_group, atoms_group), 2 * WIN_K)

    def score(g):
        query = q_s[pl.ds(pl.multiple_of(step * size + g * atoms_group + half, half), atoms_group), :].astype(F32)
        stacked = [
            jnp.where(m, query[i * WIN_Q : (i + 1) * WIN_Q], 0.0).astype(BF16) for i in range(group) for m in heads
        ]
        return dot(jnp.concatenate(stacked, axis=0), k_s[:, region(g * group)])

    def soften(n, scores):
        offset = n % group * WIN_Q + half + shift_ref[step * blocks + n]
        early = lane >= offset
        begin = n * WIN_Q
        bias = bias_ref[:, begin : begin + WIN_Q, :].astype(F32).reshape(span, WIN_K)
        index = slot + jnp.where(slot >= offset, 0, WIN_K)
        index = index + (step * size + n // group * atoms_group + shard * rows - half)
        shut = jnp.where((index >= 0) & (index < atom_total), 0.0, -jnp.inf)
        logits = jnp.where(early, scores[:, :WIN_K], scores[:, WIN_K:]) + (
            pltpu.roll(bias, jnp.bitwise_and(offset, WIN_K - 1), 1) + shut
        )
        terms = jnp.exp(logits - jnp.max(logits, axis=-1, keepdims=True))
        return jnp.concatenate(
            [jnp.where(early, terms, 0.0).astype(BF16), jnp.where(early, 0.0, terms).astype(BF16)], axis=1
        )

    def mix(g, weights):
        mixed = dot(jnp.concatenate(weights, axis=0), v_s[region(g * group), :])
        merged = []
        for i in range(group):
            parts = [mixed[(i * AH + h) * WIN_Q : (i * AH + h + 1) * WIN_Q] for h in range(AH)]
            values, total = parts[0][:, :width], parts[0][:, width:]
            for h in range(1, AH):
                values = jnp.where(heads[h], parts[h][:, :width], values)
                total = jnp.where(heads[h], parts[h][:, width:], total)
            merged.append((values / total).astype(BF16))
        local = g * atoms_group
        at = pl.multiple_of(step * size + local, atoms_group)
        own = atoms_ref[pl.ds(at, atoms_group), :].astype(F32)
        result = own + dot(jnp.concatenate(merged, axis=0), proj_ref[...])
        out_ref[local : local + atoms_group, :] = result.astype(BF16)

    groups = blocks // group
    ahead = score(0)
    behind = None
    for g in range(groups):
        scores = ahead
        if g + 1 < groups:
            ahead = score(g + 1)
        if g:
            mix(g - 1, behind)
        behind = [soften(g * group + i, scores[i * span : (i + 1) * span]) for i in range(group)]
    mix(groups - 1, behind)

    @pl.when(step == chunks - 1)
    def _():
        ids = tok_ref[tok_ref.shape[0] - 8 :, :]
        code = jnp.maximum(ids - (shard + 1) * tok_rows + 1, 0)
        high = (code >> 4).astype(F32)
        low = (code & 15).astype(F32)
        msg_ref[:SHIFT_MAX, :] = out_ref[size - SHIFT_MAX :, :]
        msg_ref[SHIFT_MAX:, :] = jnp.concatenate([high, low], axis=0).astype(BF16)


def atom_attention(shift, pos, atoms, left, right, gain, qkv, proj, bias, tok2d, tok_rows, atom_total):
    rows, width = atoms.shape
    size = 2 * SHIFT_MAX
    chunks = rows // size
    half = WIN_K // 2
    return pl.pallas_call(
        functools.partial(atom_kernel, chunks, atom_total, tok_rows),
        grid_spec=pltpu.PrefetchScalarGridSpec(
            num_scalar_prefetch=2,
            grid=(chunks,),
            in_specs=[
                full((rows, width)),
                full((half, width)),
                full((half, width)),
                full((width,)),
                full(qkv.shape),
                full(proj.shape),
                pl.BlockSpec((AH, size, WIN_K), lambda i, *_: (0, i, 0)),
                full(tok2d.shape),
            ],
            out_specs=[
                pl.BlockSpec((size, width), lambda i, *_: (i, 0)),
                full((SHIFT_MAX + 16, width)),
            ],
            scratch_shapes=[
                pltpu.VMEM((rows + 2 * half, width), BF16),
                pltpu.VMEM((width, rows + 2 * half), BF16),
                pltpu.VMEM((rows + 2 * half, 2 * width), BF16),
                pltpu.VMEM((rows + 2 * half, width), BF16),
            ],
        ),
        out_shape=[
            jax.ShapeDtypeStruct((rows, width), BF16),
            jax.ShapeDtypeStruct((SHIFT_MAX + 16, width), BF16),
        ],
        compiler_params=params(),
        cost_estimate=pl.CostEstimate(flops=8 * 10**9, bytes_accessed=6 * 10**6, transcendentals=2 * 10**6),
        name="atom_attention",
    )(shift, pos, atoms, left, right, gain, qkv, proj, bias, tok2d)


def activate(rows, weight_half):
    u = dot(rows, weight_half)
    return (u + u * jnp.tanh(u)).astype(BF16)


def pool_kernel(tok_rows, pos_ref, out_ref, weight_ref, tok_ref, sum_ref, cnt_ref):
    step = pl.program_id(0)
    size = out_ref.shape[0]
    lines = size // LANES
    base = pos_ref[0] * tok_rows
    token = lax.broadcasted_iota(jnp.int32, (tok_rows, LANES), 0)
    weight_half = (weight_ref[...].astype(F32) * 0.5).astype(BF16)
    hidden = activate(out_ref[...], weight_half)
    ones = []
    for j in range(lines):
        ids = tok_ref[pl.ds(step * lines + j, 1), :] - base
        ones.append(jnp.where(token == ids, 1.0, 0.0))
    hot = jnp.concatenate(ones, axis=1).astype(BF16)
    count = functools.reduce(jnp.add, ones)
    more = dot(hot, hidden)

    @pl.when(step == 0)
    def _():
        sum_ref[...] = more
        cnt_ref[...] = count

    @pl.when(step > 0)
    def _():
        sum_ref[...] += more
        cnt_ref[...] += count


def pool(pos, atom_out, weight, tok2d, tok_rows, part):
    rows, width = atom_out.shape
    feats = weight.shape[1] // PARTS
    size = min(1024, rows)
    return pl.pallas_call(
        functools.partial(pool_kernel, tok_rows),
        grid_spec=pltpu.PrefetchScalarGridSpec(
            num_scalar_prefetch=1,
            grid=(rows // size,),
            in_specs=[
                pl.BlockSpec((size, width), lambda i, *_: (i, 0)),
                pl.BlockSpec((width, feats), lambda i, *_: (0, part)),
                full(tok2d.shape),
            ],
            out_specs=[full((tok_rows, feats)), full((tok_rows, LANES))],
        ),
        out_shape=[
            jax.ShapeDtypeStruct((tok_rows, feats), F32),
            jax.ShapeDtypeStruct((tok_rows, LANES), F32),
        ],
        compiler_params=params(VMEM_SMALL),
        cost_estimate=pl.CostEstimate(flops=2 * 10**9, bytes_accessed=2 * 10**6, transcendentals=10**6),
        name="pool",
    )(pos, atom_out, weight, tok2d)


def finish_kernel(msg_ref, weight_ref, sum_ref, cnt_ref, repr_ref):
    tok_rows = sum_ref.shape[0]
    size = msg_ref.shape[0] - 16
    lines = size // LANES
    token = lax.broadcasted_iota(jnp.int32, (tok_rows, LANES), 0).astype(F32)
    weight_half = (weight_ref[...].astype(F32) * 0.5).astype(BF16)
    hidden = activate(msg_ref[:size, :], weight_half)
    codes = msg_ref[size:, :].astype(F32)
    ids = codes[:8] * 16.0 + codes[8:] - 1.0
    ones = [jnp.where(token == ids[8 - lines + j : 9 - lines + j], 1.0, 0.0) for j in range(lines)]
    hot = jnp.concatenate(ones, axis=1).astype(BF16)
    count = functools.reduce(jnp.add, ones) + cnt_ref[...]
    sums = sum_ref[...] + dot(hot, hidden)
    repr_ref[...] = (sums / jnp.sum(count, axis=1, keepdims=True)).astype(BF16)


def finish(msg, weight, sums, counts, part):
    rows, feats = sums.shape
    return pl.pallas_call(
        finish_kernel,
        grid=(1,),
        in_specs=[
            full(msg.shape),
            pl.BlockSpec((weight.shape[0], feats), lambda i: (0, part)),
            full(sums.shape),
            full(counts.shape),
        ],
        out_specs=full((rows, feats)),
        out_shape=jax.ShapeDtypeStruct((rows, feats), BF16),
        compiler_params=params(VMEM_SMALL),
        cost_estimate=pl.CostEstimate(flops=2 * 10**8, bytes_accessed=2 * 10**6, transcendentals=2 * 10**5),
        name="token_finish",
    )(msg, weight, sums, counts)


def query_kernel(scale, a_ref, b_ref, gain_ref, weight_hbm, out_ref, weight_s, sem):
    copy = pltpu.make_async_copy(weight_hbm, weight_s, sem)
    copy.start()
    rows = jnp.concatenate([a_ref[...].astype(F32), b_ref[...].astype(F32)], axis=1)
    normed = norm_rows(rows, gain_ref[...].reshape(1, -1)).astype(BF16)
    copy.wait()
    out_ref[...] = (dot(normed, weight_s[...]) * scale).astype(BF16)


def project_queries(halves, gain, weight):
    rows = halves[0].shape[0]
    return pl.pallas_call(
        functools.partial(query_kernel, 1.0 / math.sqrt(weight.shape[1] // TH)),
        in_specs=[pl.BlockSpec(memory_space=pltpu.VMEM)] * 3 + [pl.BlockSpec(memory_space=pl.ANY)],
        out_shape=jax.ShapeDtypeStruct((rows, weight.shape[1]), BF16),
        scratch_shapes=[pltpu.VMEM(weight.shape, BF16), pltpu.SemaphoreType.DMA],
        compiler_params=params(VMEM_SMALL),
        cost_estimate=pl.CostEstimate(flops=5 * 10**8, bytes_accessed=3 * 10**6, transcendentals=0),
        name="queries",
    )(*halves, gain, weight)


GROUPS = 2
ROW_TILE = 32


def pack_message(mixed, lse, heads):
    lane = lax.broadcasted_iota(jnp.int32, lse.shape, 1)
    high = lse.astype(BF16).astype(F32)
    rest = lse - high
    middle = rest.astype(BF16).astype(F32)
    low = rest - middle
    first = jnp.where(lane < heads, high, pltpu.roll(middle, heads, 1))
    second = jnp.where(lane < heads, low, 0.0)
    turned = jnp.concatenate([first, second], axis=0).T
    return jnp.concatenate([mixed.astype(BF16), turned[: 2 * heads].astype(BF16)], axis=0)


def unpack_message(msg, rows, heads):
    coded = msg[rows:].astype(F32)
    coded = jnp.concatenate([coded, jnp.zeros((LANES - 2 * heads, coded.shape[1]), F32)], axis=0).T
    first = coded[:rows]
    return msg[:rows].astype(F32), first + pltpu.roll(first, LANES - heads, 1) + coded[rows:]


def merge_parts(mixed, lse, other, lse_b, heads):
    rows, feats = mixed.shape
    width = feats // heads
    spot = lax.broadcasted_iota(jnp.int32, (rows, LANES), 1)
    lse_b = jnp.where(spot < heads, lse_b, lse)
    top = jnp.maximum(lse, lse_b)
    part = jnp.exp(lse - top)
    total = part + jnp.exp(lse_b - top)
    share = part / total
    high = share.astype(BF16)
    low = (share - high.astype(F32)).astype(BF16)
    head = lax.broadcasted_iota(jnp.int32, (LANES, feats), 0) * width
    column = lax.broadcasted_iota(jnp.int32, (LANES, feats), 1)
    spread = jnp.where((column >= head) & (column < head + width), 1.0, 0.0).astype(BF16)
    wide = dot(high, spread) + dot(low, spread)
    return other + wide * (mixed - other), top + jnp.log(total)


def attend_group(group, heads, width, half, q_ref, k_ref, v_ref, bias_ref, scratch):
    score_s, term_s, top_s, mix_s = scratch
    rows = mix_s.shape[0]
    at = pl.multiple_of(half * rows, rows)
    pairs = heads // 2
    spot = lax.broadcasted_iota(jnp.int32, (rows, LANES), 1)

    def layout(p):
        first = 2 * p * width
        low = first // LANES * LANES
        wide = -(-(first + 2 * width) // LANES) * LANES - low
        lane = lax.broadcasted_iota(jnp.int32, (rows, wide), 1)
        first -= low
        masks = [(lane >= first + j * width) & (lane < first + (j + 1) * width) for j in range(2)]
        return slice(low, low + wide), first, masks

    keys = score_s[0].shape[1]
    chunk = min(256, keys)
    chunks = keys // chunk
    tiles = 2 * rows // ROW_TILE

    def stack(p):
        window, _, masks = layout(p)
        query = q_ref[pl.ds(at, rows), window].astype(F32)
        return jnp.concatenate([jnp.where(m, query, 0.0).astype(BF16) for m in masks], axis=0)

    def score(p, n, stacked):
        part = slice(n * chunk, (n + 1) * chunk)
        score_s[p % 2][:, part] = dot(stacked, k_ref[layout(p)[0], part])

    def soften(p, n):
        for r in range(n * tiles // chunks * ROW_TILE, (n + 1) * tiles // chunks * ROW_TILE, ROW_TILE):
            line = pl.multiple_of(at + r % rows, ROW_TILE)
            bias = bias_ref[group * heads + 2 * p + r // rows, pl.ds(line, ROW_TILE), :].astype(F32)
            scores = score_s[p % 2][r : r + ROW_TILE, :] + bias
            top = jnp.max(scores, axis=-1, keepdims=True)
            term_s[p % 2][r : r + ROW_TILE, :] = jnp.exp(scores - top).astype(BF16)
            top_s[p % 2][r : r + ROW_TILE, :] = jnp.broadcast_to(top, (ROW_TILE, LANES))

    def mix(p, n, mixed):
        part = slice(n * chunk, (n + 1) * chunk)
        window, first, _ = layout(p)
        values = v_ref[part, window]
        column = lax.broadcasted_iota(jnp.int32, values.shape, 1)
        used = (column >= first) & (column < first + 2 * width)
        more = dot(term_s[p % 2][:, part], jnp.where(used, values.astype(F32), 1.0).astype(BF16))
        return more if mixed is None else mixed + more

    def close(p, mixed, lse):
        window, first, masks = layout(p)
        free = 0 if first >= 16 else 2 * width
        total = mixed[:, free : free + 1]
        mixed = mixed / total
        sums = top_s[p % 2][...] + jnp.log(total)
        result = mix_s[:, window]
        for j in range(2):
            result = jnp.where(masks[j], mixed[j * rows : (j + 1) * rows], result)
            lse = jnp.where(spot == 2 * p + j, sums[j * rows : (j + 1) * rows], lse)
        mix_s[:, window] = result
        return lse

    lse = jnp.zeros((rows, LANES), F32)
    stacked = stack(0)
    for n in range(chunks):
        score(0, n, stacked)
    for p in range(pairs):
        mixed = None
        if p + 1 < pairs:
            stacked = stack(p + 1)
        for n in range(chunks):
            if p + 1 < pairs:
                score(p + 1, n, stacked)
            if p:
                mixed = mix(p - 1, n, mixed)
            soften(p, n)
        if p:
            lse = close(p - 1, mixed, lse)
    mixed = None
    for n in range(chunks):
        mixed = mix(pairs - 1, n, mixed)
    lse = close(pairs - 1, mixed, lse)
    return mix_s[...], lse


def group_scratch(rows, keys, feats, heads):
    return [
        pltpu.VMEM((2 * rows, keys), F32),
        pltpu.VMEM((2 * rows, keys), F32),
        pltpu.VMEM((2 * rows, keys), BF16),
        pltpu.VMEM((2 * rows, keys), BF16),
        pltpu.VMEM((2 * rows, LANES), F32),
        pltpu.VMEM((2 * rows, LANES), F32),
        pltpu.VMEM((rows, feats), F32),
        pltpu.VMEM((2, 2 * feats, feats), BF16),
        pltpu.SemaphoreType.DMA((2,)),
    ]


def scratch_of(refs):
    return refs[:2], refs[2:4], refs[4:6], refs[6]


def weight_copies(group, weight_hbm, refs):
    weight_s, sems = refs[7:9]
    feats = weight_s.shape[2]
    return [
        pltpu.make_async_copy(
            weight_hbm.at[:, pl.ds((part * GROUPS + group) * feats, feats)], weight_s.at[part], sems.at[part]
        )
        for part in range(2)
    ]


def project_keys(x_ref, weight_s, copies, k_ref, v_ref):
    tile = x_ref.shape[0] // 2
    copies[0].wait()
    for r in range(0, x_ref.shape[0], tile):
        k_ref[:, r : r + tile] = dot(x_ref[r : r + tile, :], weight_s[0]).T.astype(BF16)
    copies[1].wait()
    for r in range(0, x_ref.shape[0], tile):
        v_ref[r : r + tile, :] = dot(x_ref[r : r + tile, :], weight_s[1]).astype(BF16)


def first_kernel(heads, width, half_ref, core_ref, q_ref, own_a, own_b, other_a, other_b, gain_ref, weight_hbm,
                 bias_ref, x_ref, k_ref, v_ref, msg_ref, *refs):
    scratch = scratch_of(refs)
    weights = weight_copies(0, weight_hbm, refs)
    for copy in weights:
        copy.start()
    rows = own_a.shape[0]
    core = core_ref[0]
    gain = gain_ref[...].reshape(1, -1)
    for place, parts in ((core, (own_a, own_b)), (1 - core, (other_a, other_b))):
        values = jnp.concatenate([part[...].astype(F32) for part in parts], axis=1)
        x_ref[pl.ds(pl.multiple_of(place * rows, rows), rows), :] = norm_rows(values, gain).astype(BF16)
    project_keys(x_ref, refs[7], weights, k_ref, v_ref)
    mixed, lse = attend_group(0, heads, width, half_ref[0], q_ref, k_ref, v_ref, bias_ref, scratch)
    msg_ref[...] = pack_message(mixed, lse, heads)


def next_kernel(group, heads, width, half_ref, q_ref, x_ref, weight_hbm, bias_ref, k_ref, v_ref, msg_ref, *refs):
    scratch = scratch_of(refs)
    weights = weight_copies(group, weight_hbm, refs)
    for copy in weights:
        copy.start()
    project_keys(x_ref, refs[7], weights, k_ref, v_ref)
    mixed, lse = attend_group(group, heads, width, half_ref[0], q_ref, k_ref, v_ref, bias_ref, scratch)
    msg_ref[...] = pack_message(mixed, lse, heads)


def keep_kernel(group, heads, width, half_ref, q_ref, k_ref, v_ref, near_ref, bias_ref, o_ref, lse_ref, msg_ref, *refs):
    scratch = scratch_of(refs)
    mixed, lse = attend_group(group, heads, width, half_ref[0], q_ref, k_ref, v_ref, bias_ref, scratch)
    rows = mixed.shape[0]
    mixed, lse = merge_parts(mixed, lse, *unpack_message(near_ref[...], rows, heads), heads)
    o_ref[...] = mixed
    lse_ref[...] = lse
    msg_ref[...] = pack_message(mixed, lse, heads)


def group_call(kernel, group, half, scalars, q, arrays, weights, bias, outs, name):
    tok_rows, all_feats = q.shape
    rows, keys, feats = tok_rows // 2, bias.shape[2], all_feats // GROUPS
    heads = TH // GROUPS
    shapes = {
        "x": ((keys, all_feats), BF16),
        "k": ((feats, keys), BF16),
        "v": ((keys, feats), BF16),
        "o": ((rows, feats), F32),
        "lse": ((rows, LANES), F32),
        "msg": ((rows + 2 * heads, feats), BF16),
    }
    return pl.pallas_call(
        functools.partial(kernel, heads, feats // heads),
        grid_spec=pltpu.PrefetchScalarGridSpec(
            num_scalar_prefetch=1 + len(scalars),
            grid=(1,),
            in_specs=[pl.BlockSpec((tok_rows, feats), lambda i, *_: (0, group))]
            + [full(array.shape) for array in arrays]
            + [pl.BlockSpec(memory_space=pl.ANY)] * (0 if weights is None else 1)
            + [pl.BlockSpec(memory_space=pltpu.VMEM)],
            out_specs=[full(shapes[out][0]) for out in outs],
            scratch_shapes=group_scratch(rows, keys, feats, heads),
        ),
        out_shape=[jax.ShapeDtypeStruct(*shapes[out]) for out in outs],
        compiler_params=params(VMEM_SMALL),
        cost_estimate=pl.CostEstimate(flops=4 * 10**9, bytes_accessed=4 * 10**6, transcendentals=10**6),
        name=name,
    )(half, *scalars, q, *arrays, *([] if weights is None else [weights]), bias)


def merge_kernel(heads, o_ref, lse_ref, msg_ref, out_ref, sum_ref, back_ref):
    rows = o_ref.shape[0]
    mixed, lse = merge_parts(o_ref[...], lse_ref[...], *unpack_message(msg_ref[...], rows, heads), heads)
    out_ref[...] = mixed
    sum_ref[...] = lse
    back_ref[...] = pack_message(mixed, lse, heads)


def merge(o, lse, msg):
    return pl.pallas_call(
        functools.partial(merge_kernel, TH // GROUPS),
        out_shape=[jax.ShapeDtypeStruct(a.shape, a.dtype) for a in (o, lse, msg)],
        compiler_params=params(VMEM_SMALL),
        name="merge",
    )(o, lse, msg)


def settle_kernel(heads, o_ref, lse_ref, msg_ref, out_ref):
    rows = o_ref.shape[0]
    mixed, _ = merge_parts(o_ref[...], lse_ref[...], *unpack_message(msg_ref[...], rows, heads), heads)
    out_ref[...] = mixed.astype(BF16)


def settle(o, lse, msg):
    return pl.pallas_call(
        functools.partial(settle_kernel, TH // GROUPS),
        out_shape=jax.ShapeDtypeStruct(o.shape, BF16),
        compiler_params=params(VMEM_SMALL),
        name="settle",
    )(o, lse, msg)


def output_kernel(half_ref, own_a, own_b, other_a, other_b, a_ref, b_ref, weight_ref, out_ref):
    rows, feats = own_a.shape
    for place, first, second in ((half_ref[0], own_a, own_b), (1 - half_ref[0], other_a, other_b)):
        mine = pl.ds(pl.multiple_of(place * rows, rows), rows)
        result = dot(first[...], weight_ref[:feats, :]) + dot(second[...], weight_ref[feats:, :])
        out_ref[mine, :feats] = (a_ref[mine, :].astype(F32) + result[:, :feats]).astype(BF16)
        out_ref[mine, feats:] = (b_ref[mine, :].astype(F32) + result[:, feats:]).astype(BF16)


def output_rows(half, own, other, token_repr, weight):
    rows = token_repr[0].shape[0]
    return pl.pallas_call(
        output_kernel,
        in_specs=[pl.BlockSpec(memory_space=pltpu.SMEM)] + [pl.BlockSpec(memory_space=pltpu.VMEM)] * 7,
        out_shape=jax.ShapeDtypeStruct((rows, weight.shape[1]), BF16),
        compiler_params=params(VMEM_SMALL),
        name="output_rows",
    )(half, *own, *other, *token_repr, weight)


def bits_of(count):
    return [1 << b for b in range(count.bit_length() - 1)]


def key_parts(halves):
    n_pb, n_ka = lax.axis_size("pb"), lax.axis_size("ka")
    cores = n_pb // n_ka
    chips = n_pb // cores
    shard, plane = lax.axis_index("pb"), lax.axis_index("ka")
    bits = bits_of(chips)
    core = lax.rem(shard, cores)
    away = jnp.bitwise_xor(shard // cores, plane)
    held = list(halves)
    for r in range(len(bits)):
        pairs = []
        gets = jnp.bool_(False)
        for c in range(cores):
            order = bits if c % 2 == 0 else bits[::-1]
            known = sum(order[:r])
            for k in range(n_ka):
                for j in range(chips):
                    if (j ^ k) & ~known == 0:
                        pairs.append(((j * cores + c) * n_ka + k, ((j ^ order[r]) * cores + c) * n_ka + k))
            fresh = (jnp.bitwise_and(away, ~(known + order[r])) == 0) & (jnp.bitwise_and(away, order[r]) != 0)
            gets = gets | (fresh & (core == c))
        held = [jnp.where(gets, lax.ppermute(part, ("pb", "ka"), pairs), part) for part in held]
    return held, [lax.ppermute(part, "pb", [(p, p ^ 1) for p in range(n_pb)]) for part in held]


def body(
    atoms,
    atom_gain,
    atom_qkv,
    atom_proj,
    atom_bias,
    window_shift,
    token_of_atom,
    agg_weight,
    token_gain,
    token_q,
    token_kv,
    token_o,
    pair_bias,
):
    n_pb, n_ka = lax.axis_size("pb"), lax.axis_size("ka")
    shard, plane = lax.axis_index("pb"), lax.axis_index("ka")
    rows, width = atoms.shape
    tok_rows = pair_bias.shape[1]
    half = WIN_K // 2
    up = [(i, i + 1) for i in range(n_pb - 1)]
    down = [(i + 1, i) for i in range(n_pb - 1)]
    pos = shard.astype(jnp.int32).reshape(1)
    tok2d = token_of_atom.reshape(rows // LANES, LANES)
    left = lax.ppermute(atoms[rows - half :], "pb", up)
    right = lax.ppermute(atoms[:half], "pb", down)
    atom_out, msg = atom_attention(
        window_shift, pos, atoms, left, right, atom_gain, atom_qkv, atom_proj,
        atom_bias, tok2d, tok_rows, rows * n_pb,
    )
    behind = lax.ppermute(msg, "pb", up)
    token_repr = []
    for part in range(PARTS):
        sums, counts = pool(pos, atom_out, agg_weight, tok2d, tok_rows, part)
        token_repr.append(finish(behind, agg_weight, sums, counts, part))
    late_bias, token_repr[0] = lax.optimization_barrier((pair_bias, token_repr[0]))
    own_keys, other_keys = key_parts(token_repr)
    queries = project_queries(token_repr, token_gain, token_q)
    parity = jnp.bitwise_and(plane ^ (plane >> 1), 1).astype(jnp.int32)
    core = lax.rem(shard, n_pb // n_ka).astype(jnp.int32)
    keep, send = parity.reshape(1), (1 - parity).reshape(1)
    swap = [(i, i ^ 1) for i in range(n_ka)]
    bits = bits_of(n_ka)[1:]

    def far(msg, bit):
        return lax.ppermute(msg, "ka", [(i, i ^ (2 * bit - 1)) for i in range(n_ka)])

    x, k, v, msg = group_call(
        first_kernel, 0, send, (core.reshape(1),), queries, (*own_keys, *other_keys, token_gain), token_kv,
        late_bias, ("x", "k", "v", "msg"), "attend_first",
    )
    held, near = [(k, v)], [lax.ppermute(msg, "ka", swap)]
    for g in range(1, GROUPS):
        k, v, msg = group_call(
            functools.partial(next_kernel, g), g, send, (), queries, (x,), token_kv,
            late_bias, ("k", "v", "msg"), "attend_next",
        )
        held.append((k, v))
        near.append(lax.ppermute(msg, "ka", swap))
    sums, gone = [], []
    for g in range(GROUPS):
        o, lse, msg = group_call(
            functools.partial(keep_kernel, g), g, keep, (), queries, (*held[g], near[g]), None,
            late_bias, ("o", "lse", "msg"), "attend_keep",
        )
        sums.append((o, lse))
        gone.append(far(msg, bits[0]))
    own_mix, other_mix = [], []
    for g in range(GROUPS):
        (o, lse), got = sums[g], gone[g]
        for bit in bits[1:]:
            o, lse, msg = merge(o, lse, got)
            got = far(msg, bit)
        own_mix.append(settle(o, lse, got))
        other_mix.append(lax.ppermute(own_mix[g], "ka", swap))
    return atom_out, output_rows(keep, own_mix, other_mix, token_repr, token_o)


def solution(mesh):
    return jax.shard_map(
        body,
        mesh=mesh,
        in_specs=(
            P("pb", None),
            P(),
            P(),
            P(),
            P(None, "pb", None),
            P("pb"),
            P("pb"),
            P(),
            P(),
            P(),
            P(),
            P(),
            P(None, "pb", "ka"),
        ),
        out_specs=(P("pb", None), P("pb", None)),
        check_vma=False,
    )
```

```python
import functools
import math

import jax
import jax.numpy as jnp
from jax import lax
from jax.experimental import pallas as pl
from jax.experimental.pallas import tpu as pltpu
from jax.sharding import PartitionSpec as P

AH = 4
TH = 16
WIN_Q = 32
WIN_K = 128
SHIFT_MAX = 384
PARTS = 2
LANES = 128
F32 = jnp.float32
BF16 = jnp.bfloat16
VMEM_LIMIT = 56 * 1024 * 1024
VMEM_SMALL = 24 * 1024 * 1024


def full(shape):
    return pl.BlockSpec(shape, lambda *_: (0,) * len(shape))


def params(limit=VMEM_LIMIT):
    return pltpu.CompilerParams(vmem_limit_bytes=limit)


def norm_rows(as_float, gain):
    centre = jnp.mean(as_float, axis=-1, keepdims=True)
    spread = jnp.mean(jnp.square(as_float - centre), axis=-1, keepdims=True)
    return (as_float - centre) * lax.rsqrt(spread + 1e-05) * gain


def dot(a, b):
    return jnp.dot(a, b, preferred_element_type=F32)


def atom_kernel(
    chunks,
    atom_total,
    tok_rows,
    shift_ref,
    pos_ref,
    atoms_ref,
    left_ref,
    right_ref,
    gain_ref,
    qkv_ref,
    proj_ref,
    bias_ref,
    tok_ref,
    out_ref,
    near_ref,
    msg_ref,
    q_s,
    k_s,
    v_s,
    x_s,
):
    step = pl.program_id(0)
    rows, width = atoms_ref.shape
    size = out_ref.shape[0]
    half = WIN_K // 2
    head = width // AH
    shard = pos_ref[0]

    @pl.when(step == 0)
    def _():
        gain = gain_ref[...].reshape(1, width)
        x_s[:half, :] = left_ref[...]
        x_s[half : half + rows, :] = atoms_ref[...]
        x_s[half + rows :, :] = right_ref[...]
        total = rows + 2 * half
        tile = 5 * WIN_K if total % (5 * WIN_K) == 0 else WIN_K

        def one(c, carry):
            at = pl.ds(pl.multiple_of(c * tile, tile), tile)
            normed = norm_rows(x_s[at, :].astype(F32), gain).astype(BF16)
            res = dot(normed, qkv_ref[...])
            q_s[at, :] = (res[:, :width] * (1.0 / math.sqrt(head))).astype(BF16)
            k_s[:, at] = res[:, width : 2 * width].T.astype(BF16)
            v_s[at, :width] = res[:, 2 * width :].astype(BF16)
            v_s[at, width:] = jnp.ones((tile, width), BF16)
            return carry

        lax.fori_loop(0, total // tile, one, 0, unroll=True)

    group = WIN_K // WIN_Q
    atoms_group = group * WIN_Q
    span = AH * WIN_Q
    lane_q = lax.broadcasted_iota(jnp.int32, (WIN_Q, width), 1)
    heads = [(lane_q >= h * head) & (lane_q < (h + 1) * head) for h in range(AH)]
    lane = lax.broadcasted_iota(jnp.int32, (span, WIN_K), 1)
    slot = lax.broadcasted_iota(jnp.int32, (1, WIN_K), 1)
    blocks = size // WIN_Q

    def region(n):
        return pl.ds(pl.multiple_of(step * size + n // group * atoms_group, atoms_group), 2 * WIN_K)

    def score(g):
        query = q_s[pl.ds(pl.multiple_of(step * size + g * atoms_group + half, half), atoms_group), :].astype(F32)
        stacked = [
            jnp.where(m, query[i * WIN_Q : (i + 1) * WIN_Q], 0.0).astype(BF16) for i in range(group) for m in heads
        ]
        return dot(jnp.concatenate(stacked, axis=0), k_s[:, region(g * group)])

    def soften(n, scores):
        offset = n % group * WIN_Q + half + shift_ref[step * blocks + n]
        early = lane >= offset
        begin = n * WIN_Q
        bias = bias_ref[:, begin : begin + WIN_Q, :].astype(F32).reshape(span, WIN_K)
        index = slot + jnp.where(slot >= offset, 0, WIN_K)
        index = index + (step * size + n // group * atoms_group + shard * rows - half)
        shut = jnp.where((index >= 0) & (index < atom_total), 0.0, -jnp.inf)
        logits = jnp.where(early, scores[:, :WIN_K], scores[:, WIN_K:]) + (
            pltpu.roll(bias, jnp.bitwise_and(offset, WIN_K - 1), 1) + shut
        )
        terms = jnp.exp(logits - jnp.max(logits, axis=-1, keepdims=True))
        return jnp.concatenate(
            [jnp.where(early, terms, 0.0).astype(BF16), jnp.where(early, 0.0, terms).astype(BF16)], axis=1
        )

    def mix(g, weights):
        mixed = dot(jnp.concatenate(weights, axis=0), v_s[region(g * group), :])
        merged = []
        for i in range(group):
            parts = [mixed[(i * AH + h) * WIN_Q : (i * AH + h + 1) * WIN_Q] for h in range(AH)]
            values, total = parts[0][:, :width], parts[0][:, width:]
            for h in range(1, AH):
                values = jnp.where(heads[h], parts[h][:, :width], values)
                total = jnp.where(heads[h], parts[h][:, width:], total)
            merged.append((values / total).astype(BF16))
        local = g * atoms_group
        at = pl.multiple_of(step * size + local, atoms_group)
        own = atoms_ref[pl.ds(at, atoms_group), :].astype(F32)
        result = own + dot(jnp.concatenate(merged, axis=0), proj_ref[...])
        out_ref[local : local + atoms_group, :] = result.astype(BF16)
        near_ref[local : local + atoms_group, :] = result.astype(BF16)

    groups = blocks // group
    ahead = score(0)
    behind = None
    for g in range(groups):
        scores = ahead
        if g + 1 < groups:
            ahead = score(g + 1)
        if g:
            mix(g - 1, behind)
        behind = [soften(g * group + i, scores[i * span : (i + 1) * span]) for i in range(group)]
    mix(groups - 1, behind)

    @pl.when(step == chunks - 1)
    def _():
        ids = tok_ref[tok_ref.shape[0] - 8 :, :]
        code = jnp.maximum(ids - (shard + 1) * tok_rows + 1, 0)
        high = (code >> 4).astype(F32)
        low = (code & 15).astype(F32)
        msg_ref[:SHIFT_MAX, :] = out_ref[size - SHIFT_MAX :, :]
        msg_ref[SHIFT_MAX:, :] = jnp.concatenate([high, low], axis=0).astype(BF16)


def atom_attention(shift, pos, atoms, left, right, gain, qkv, proj, bias, tok2d, tok_rows, atom_total):
    rows, width = atoms.shape
    size = 2 * SHIFT_MAX
    chunks = rows // size
    half = WIN_K // 2
    return pl.pallas_call(
        functools.partial(atom_kernel, chunks, atom_total, tok_rows),
        grid_spec=pltpu.PrefetchScalarGridSpec(
            num_scalar_prefetch=2,
            grid=(chunks,),
            in_specs=[
                full((rows, width)),
                full((half, width)),
                full((half, width)),
                full((width,)),
                full(qkv.shape),
                full(proj.shape),
                pl.BlockSpec((AH, size, WIN_K), lambda i, *_: (0, i, 0)),
                full(tok2d.shape),
            ],
            out_specs=[
                pl.BlockSpec((size, width), lambda i, *_: (i, 0)),
                pl.BlockSpec((size, width), lambda i, *_: (i, 0)),
                full((SHIFT_MAX + 16, width)),
            ],
            scratch_shapes=[
                pltpu.VMEM((rows + 2 * half, width), BF16),
                pltpu.VMEM((width, rows + 2 * half), BF16),
                pltpu.VMEM((rows + 2 * half, 2 * width), BF16),
                pltpu.VMEM((rows + 2 * half, width), BF16),
            ],
        ),
        out_shape=[
            jax.ShapeDtypeStruct((rows, width), BF16),
            jax.ShapeDtypeStruct((rows, width), BF16),
            jax.ShapeDtypeStruct((SHIFT_MAX + 16, width), BF16),
        ],
        compiler_params=params(),
        cost_estimate=pl.CostEstimate(flops=8 * 10**9, bytes_accessed=6 * 10**6, transcendentals=2 * 10**6),
        name="atom_attention",
    )(shift, pos, atoms, left, right, gain, qkv, proj, bias, tok2d)


def activate(rows, weight_half):
    u = dot(rows, weight_half)
    return (u + u * jnp.tanh(u)).astype(BF16)


def pool_kernel(tok_rows, pos_ref, out_ref, weight_ref, tok_ref, sum_ref, cnt_ref):
    step = pl.program_id(0)
    size = out_ref.shape[0]
    lines = size // LANES
    base = pos_ref[0] * tok_rows
    token = lax.broadcasted_iota(jnp.int32, (tok_rows, LANES), 0)
    weight_half = (weight_ref[...].astype(F32) * 0.5).astype(BF16)
    hidden = activate(out_ref[...], weight_half)
    ones = []
    for j in range(lines):
        ids = tok_ref[pl.ds(step * lines + j, 1), :] - base
        ones.append(jnp.where(token == ids, 1.0, 0.0))
    hot = jnp.concatenate(ones, axis=1).astype(BF16)
    count = functools.reduce(jnp.add, ones)
    more = dot(hot, hidden)

    @pl.when(step == 0)
    def _():
        sum_ref[...] = more
        cnt_ref[...] = count

    @pl.when(step > 0)
    def _():
        sum_ref[...] += more
        cnt_ref[...] += count


def pool(pos, atom_out, weight, tok2d, tok_rows, part):
    rows, width = atom_out.shape
    feats = weight.shape[1] // PARTS
    size = min(1024, rows)
    return pl.pallas_call(
        functools.partial(pool_kernel, tok_rows),
        grid_spec=pltpu.PrefetchScalarGridSpec(
            num_scalar_prefetch=1,
            grid=(rows // size,),
            in_specs=[
                pl.BlockSpec((size, width), lambda i, *_: (i, 0)),
                pl.BlockSpec((width, feats), lambda i, *_: (0, part)),
                full(tok2d.shape),
            ],
            out_specs=[full((tok_rows, feats)), full((tok_rows, LANES))],
        ),
        out_shape=[
            jax.ShapeDtypeStruct((tok_rows, feats), F32),
            jax.ShapeDtypeStruct((tok_rows, LANES), F32),
        ],
        compiler_params=params(VMEM_SMALL),
        cost_estimate=pl.CostEstimate(flops=2 * 10**9, bytes_accessed=2 * 10**6, transcendentals=10**6),
        name="pool",
    )(pos, atom_out, weight, tok2d)


def finish_kernel(msg_ref, weight_ref, sum_ref, cnt_ref, repr_ref):
    tok_rows = sum_ref.shape[0]
    size = msg_ref.shape[0] - 16
    lines = size // LANES
    token = lax.broadcasted_iota(jnp.int32, (tok_rows, LANES), 0).astype(F32)
    weight_half = (weight_ref[...].astype(F32) * 0.5).astype(BF16)
    hidden = activate(msg_ref[:size, :], weight_half)
    codes = msg_ref[size:, :].astype(F32)
    ids = codes[:8] * 16.0 + codes[8:] - 1.0
    ones = [jnp.where(token == ids[8 - lines + j : 9 - lines + j], 1.0, 0.0) for j in range(lines)]
    hot = jnp.concatenate(ones, axis=1).astype(BF16)
    count = functools.reduce(jnp.add, ones) + cnt_ref[...]
    sums = sum_ref[...] + dot(hot, hidden)
    repr_ref[...] = (sums / jnp.sum(count, axis=1, keepdims=True)).astype(BF16)


def finish(msg, weight, sums, counts, part):
    rows, feats = sums.shape
    return pl.pallas_call(
        finish_kernel,
        grid=(1,),
        in_specs=[
            full(msg.shape),
            pl.BlockSpec((weight.shape[0], feats), lambda i: (0, part)),
            full(sums.shape),
            full(counts.shape),
        ],
        out_specs=full((rows, feats)),
        out_shape=jax.ShapeDtypeStruct((rows, feats), BF16),
        compiler_params=params(VMEM_SMALL),
        cost_estimate=pl.CostEstimate(flops=2 * 10**8, bytes_accessed=2 * 10**6, transcendentals=2 * 10**5),
        name="token_finish",
    )(msg, weight, sums, counts)


def query_kernel(scale, a_ref, b_ref, gain_ref, weight_hbm, out_ref, weight_s, sem):
    copy = pltpu.make_async_copy(weight_hbm, weight_s, sem)
    copy.start()
    rows = jnp.concatenate([a_ref[...].astype(F32), b_ref[...].astype(F32)], axis=1)
    normed = norm_rows(rows, gain_ref[...].reshape(1, -1)).astype(BF16)
    copy.wait()
    out_ref[...] = (dot(normed, weight_s[...]) * scale).astype(BF16)


def project_queries(halves, gain, weight):
    rows = halves[0].shape[0]
    return pl.pallas_call(
        functools.partial(query_kernel, 1.0 / math.sqrt(weight.shape[1] // TH)),
        in_specs=[pl.BlockSpec(memory_space=pltpu.VMEM)] * 3 + [pl.BlockSpec(memory_space=pl.ANY)],
        out_shape=jax.ShapeDtypeStruct((rows, weight.shape[1]), BF16),
        scratch_shapes=[pltpu.VMEM(weight.shape, BF16), pltpu.SemaphoreType.DMA],
        compiler_params=params(VMEM_SMALL),
        cost_estimate=pl.CostEstimate(flops=5 * 10**8, bytes_accessed=3 * 10**6, transcendentals=0),
        name="queries",
    )(*halves, gain, weight)


GROUPS = 2
ROW_TILE = 32


def pack_message(mixed, lse, heads):
    lane = lax.broadcasted_iota(jnp.int32, lse.shape, 1)
    high = lse.astype(BF16).astype(F32)
    rest = lse - high
    middle = rest.astype(BF16).astype(F32)
    low = rest - middle
    first = jnp.where(lane < heads, high, pltpu.roll(middle, heads, 1))
    second = jnp.where(lane < heads, low, 0.0)
    turned = jnp.concatenate([first, second], axis=0).T
    return jnp.concatenate([mixed.astype(BF16), turned[: 2 * heads].astype(BF16)], axis=0)


def unpack_message(msg, rows, heads):
    coded = msg[rows:].astype(F32)
    coded = jnp.concatenate([coded, jnp.zeros((LANES - 2 * heads, coded.shape[1]), F32)], axis=0).T
    first = coded[:rows]
    return msg[:rows].astype(F32), first + pltpu.roll(first, LANES - heads, 1) + coded[rows:]


def merge_parts(mixed, lse, other, lse_b, heads):
    rows, feats = mixed.shape
    width = feats // heads
    spot = lax.broadcasted_iota(jnp.int32, (rows, LANES), 1)
    lse_b = jnp.where(spot < heads, lse_b, lse)
    top = jnp.maximum(lse, lse_b)
    part = jnp.exp(lse - top)
    total = part + jnp.exp(lse_b - top)
    share = part / total
    high = share.astype(BF16)
    low = (share - high.astype(F32)).astype(BF16)
    head = lax.broadcasted_iota(jnp.int32, (LANES, feats), 0) * width
    column = lax.broadcasted_iota(jnp.int32, (LANES, feats), 1)
    spread = jnp.where((column >= head) & (column < head + width), 1.0, 0.0).astype(BF16)
    wide = dot(high, spread) + dot(low, spread)
    return other + wide * (mixed - other), top + jnp.log(total)


def attend_group(group, heads, width, half, q_ref, k_ref, v_ref, bias_ref, scratch):
    score_s, term_s, top_s, mix_s = scratch
    rows = mix_s.shape[0]
    at = pl.multiple_of(half * rows, rows)
    pairs = heads // 2
    spot = lax.broadcasted_iota(jnp.int32, (rows, LANES), 1)

    def layout(p):
        first = 2 * p * width
        low = first // LANES * LANES
        wide = -(-(first + 2 * width) // LANES) * LANES - low
        lane = lax.broadcasted_iota(jnp.int32, (rows, wide), 1)
        first -= low
        masks = [(lane >= first + j * width) & (lane < first + (j + 1) * width) for j in range(2)]
        return slice(low, low + wide), first, masks

    keys = score_s[0].shape[1]
    chunk = min(256, keys)
    chunks = keys // chunk
    tiles = 2 * rows // ROW_TILE

    def stack(p):
        window, _, masks = layout(p)
        query = q_ref[pl.ds(at, rows), window].astype(F32)
        return jnp.concatenate([jnp.where(m, query, 0.0).astype(BF16) for m in masks], axis=0)

    def score(p, n, stacked):
        part = slice(n * chunk, (n + 1) * chunk)
        score_s[p % 2][:, part] = dot(stacked, k_ref[layout(p)[0], part])

    def soften(p, n):
        for r in range(n * tiles // chunks * ROW_TILE, (n + 1) * tiles // chunks * ROW_TILE, ROW_TILE):
            bias = bias_ref[group * heads + 2 * p + r // rows, r % rows : r % rows + ROW_TILE, :].astype(F32)
            scores = score_s[p % 2][r : r + ROW_TILE, :] + bias
            top = jnp.max(scores, axis=-1, keepdims=True)
            term_s[p % 2][r : r + ROW_TILE, :] = jnp.exp(scores - top).astype(BF16)
            top_s[p % 2][r : r + ROW_TILE, :] = jnp.broadcast_to(top, (ROW_TILE, LANES))

    def mix(p, n, mixed):
        part = slice(n * chunk, (n + 1) * chunk)
        window, first, _ = layout(p)
        values = v_ref[part, window]
        column = lax.broadcasted_iota(jnp.int32, values.shape, 1)
        used = (column >= first) & (column < first + 2 * width)
        more = dot(term_s[p % 2][:, part], jnp.where(used, values.astype(F32), 1.0).astype(BF16))
        return more if mixed is None else mixed + more

    def close(p, mixed, lse):
        window, first, masks = layout(p)
        free = 0 if first >= 16 else 2 * width
        total = mixed[:, free : free + 1]
        mixed = mixed / total
        sums = top_s[p % 2][...] + jnp.log(total)
        result = mix_s[:, window]
        for j in range(2):
            result = jnp.where(masks[j], mixed[j * rows : (j + 1) * rows], result)
            lse = jnp.where(spot == 2 * p + j, sums[j * rows : (j + 1) * rows], lse)
        mix_s[:, window] = result
        return lse

    lse = jnp.zeros((rows, LANES), F32)
    stacked = stack(0)
    for n in range(chunks):
        score(0, n, stacked)
    for p in range(pairs):
        mixed = None
        if p + 1 < pairs:
            stacked = stack(p + 1)
        for n in range(chunks):
            if p + 1 < pairs:
                score(p + 1, n, stacked)
            if p:
                mixed = mix(p - 1, n, mixed)
            soften(p, n)
        if p:
            lse = close(p - 1, mixed, lse)
    mixed = None
    for n in range(chunks):
        mixed = mix(pairs - 1, n, mixed)
    lse = close(pairs - 1, mixed, lse)
    return mix_s[...], lse


def group_scratch(rows, keys, feats, heads):
    return [
        pltpu.VMEM((2 * rows, keys), F32),
        pltpu.VMEM((2 * rows, keys), F32),
        pltpu.VMEM((2 * rows, keys), BF16),
        pltpu.VMEM((2 * rows, keys), BF16),
        pltpu.VMEM((2 * rows, LANES), F32),
        pltpu.VMEM((2 * rows, LANES), F32),
        pltpu.VMEM((rows, feats), F32),
        pltpu.VMEM((2, 2 * feats, feats), BF16),
        pltpu.SemaphoreType.DMA((2,)),
    ]


def scratch_of(refs):
    return refs[:2], refs[2:4], refs[4:6], refs[6]


def weight_copies(group, weight_hbm, refs):
    weight_s, sems = refs[7:9]
    feats = weight_s.shape[2]
    return [
        pltpu.make_async_copy(
            weight_hbm.at[:, pl.ds((part * GROUPS + group) * feats, feats)], weight_s.at[part], sems.at[part]
        )
        for part in range(2)
    ]


def project_keys(x_ref, weight_s, copies, k_ref, v_ref):
    tile = x_ref.shape[0] // 2
    copies[0].wait()
    for r in range(0, x_ref.shape[0], tile):
        k_ref[:, r : r + tile] = dot(x_ref[r : r + tile, :], weight_s[0]).T.astype(BF16)
    copies[1].wait()
    for r in range(0, x_ref.shape[0], tile):
        v_ref[r : r + tile, :] = dot(x_ref[r : r + tile, :], weight_s[1]).astype(BF16)


def first_kernel(heads, width, half_ref, core_ref, q_ref, own_a, own_b, other_a, other_b, gain_ref, weight_hbm,
                 bias_ref, x_ref, k_ref, v_ref, msg_ref, *refs):
    scratch = scratch_of(refs)
    weights = weight_copies(0, weight_hbm, refs)
    for copy in weights:
        copy.start()
    rows = own_a.shape[0]
    core = core_ref[0]
    gain = gain_ref[...].reshape(1, -1)
    for place, parts in ((core, (own_a, own_b)), (1 - core, (other_a, other_b))):
        values = jnp.concatenate([part[...].astype(F32) for part in parts], axis=1)
        x_ref[pl.ds(pl.multiple_of(place * rows, rows), rows), :] = norm_rows(values, gain).astype(BF16)
    project_keys(x_ref, refs[7], weights, k_ref, v_ref)
    mixed, lse = attend_group(0, heads, width, half_ref[0], q_ref, k_ref, v_ref, bias_ref, scratch)
    msg_ref[...] = pack_message(mixed, lse, heads)


def next_kernel(group, heads, width, half_ref, q_ref, x_ref, weight_hbm, bias_ref, k_ref, v_ref, msg_ref, *refs):
    scratch = scratch_of(refs)
    weights = weight_copies(group, weight_hbm, refs)
    for copy in weights:
        copy.start()
    project_keys(x_ref, refs[7], weights, k_ref, v_ref)
    mixed, lse = attend_group(group, heads, width, half_ref[0], q_ref, k_ref, v_ref, bias_ref, scratch)
    msg_ref[...] = pack_message(mixed, lse, heads)


def keep_kernel(group, heads, width, half_ref, q_ref, k_ref, v_ref, near_ref, bias_ref, o_ref, lse_ref, msg_ref, *refs):
    scratch = scratch_of(refs)
    mixed, lse = attend_group(group, heads, width, half_ref[0], q_ref, k_ref, v_ref, bias_ref, scratch)
    rows = mixed.shape[0]
    mixed, lse = merge_parts(mixed, lse, *unpack_message(near_ref[...], rows, heads), heads)
    o_ref[...] = mixed
    lse_ref[...] = lse
    msg_ref[...] = pack_message(mixed, lse, heads)


def group_call(kernel, group, half, scalars, q, arrays, weights, bias, outs, name):
    tok_rows, all_feats = q.shape
    rows, keys, feats = tok_rows // 2, bias.shape[2], all_feats // GROUPS
    heads = TH // GROUPS
    shapes = {
        "x": ((keys, all_feats), BF16),
        "k": ((feats, keys), BF16),
        "v": ((keys, feats), BF16),
        "o": ((rows, feats), F32),
        "lse": ((rows, LANES), F32),
        "msg": ((rows + 2 * heads, feats), BF16),
    }
    return pl.pallas_call(
        functools.partial(kernel, heads, feats // heads),
        grid_spec=pltpu.PrefetchScalarGridSpec(
            num_scalar_prefetch=1 + len(scalars),
            grid=(1,),
            in_specs=[pl.BlockSpec((tok_rows, feats), lambda i, *_: (0, group))]
            + [full(array.shape) for array in arrays]
            + [pl.BlockSpec(memory_space=pl.ANY)] * (0 if weights is None else 1)
            + [pl.BlockSpec(memory_space=pltpu.VMEM)],
            out_specs=[full(shapes[out][0]) for out in outs],
            scratch_shapes=group_scratch(rows, keys, feats, heads),
        ),
        out_shape=[jax.ShapeDtypeStruct(*shapes[out]) for out in outs],
        compiler_params=params(VMEM_SMALL),
        cost_estimate=pl.CostEstimate(flops=4 * 10**9, bytes_accessed=4 * 10**6, transcendentals=10**6),
        name=name,
    )(half, *scalars, q, *arrays, *([] if weights is None else [weights]), bias)


def merge_kernel(heads, o_ref, lse_ref, msg_ref, out_ref, sum_ref, back_ref):
    rows = o_ref.shape[0]
    mixed, lse = merge_parts(o_ref[...], lse_ref[...], *unpack_message(msg_ref[...], rows, heads), heads)
    out_ref[...] = mixed
    sum_ref[...] = lse
    back_ref[...] = pack_message(mixed, lse, heads)


def merge(o, lse, msg):
    return pl.pallas_call(
        functools.partial(merge_kernel, TH // GROUPS),
        out_shape=[jax.ShapeDtypeStruct(a.shape, a.dtype) for a in (o, lse, msg)],
        compiler_params=params(VMEM_SMALL),
        name="merge",
    )(o, lse, msg)


def settle_kernel(heads, o_ref, lse_ref, msg_ref, out_ref):
    rows = o_ref.shape[0]
    mixed, _ = merge_parts(o_ref[...], lse_ref[...], *unpack_message(msg_ref[...], rows, heads), heads)
    out_ref[...] = mixed.astype(BF16)


def settle(o, lse, msg):
    return pl.pallas_call(
        functools.partial(settle_kernel, TH // GROUPS),
        out_shape=jax.ShapeDtypeStruct(o.shape, BF16),
        compiler_params=params(VMEM_SMALL),
        name="settle",
    )(o, lse, msg)


def output_kernel(half_ref, own_a, own_b, other_a, other_b, a_ref, b_ref, weight_ref, out_ref):
    rows, feats = own_a.shape
    for place, first, second in ((half_ref[0], own_a, own_b), (1 - half_ref[0], other_a, other_b)):
        mine = pl.ds(pl.multiple_of(place * rows, rows), rows)
        result = dot(first[...], weight_ref[:feats, :]) + dot(second[...], weight_ref[feats:, :])
        out_ref[mine, :feats] = (a_ref[mine, :].astype(F32) + result[:, :feats]).astype(BF16)
        out_ref[mine, feats:] = (b_ref[mine, :].astype(F32) + result[:, feats:]).astype(BF16)


def output_rows(half, own, other, token_repr, weight):
    rows = token_repr[0].shape[0]
    return pl.pallas_call(
        output_kernel,
        in_specs=[pl.BlockSpec(memory_space=pltpu.SMEM)] + [pl.BlockSpec(memory_space=pltpu.VMEM)] * 7,
        out_shape=jax.ShapeDtypeStruct((rows, weight.shape[1]), BF16),
        compiler_params=params(VMEM_SMALL),
        name="output_rows",
    )(half, *own, *other, *token_repr, weight)


def bits_of(count):
    return [1 << b for b in range(count.bit_length() - 1)]


def key_parts(halves):
    n_pb, n_ka = lax.axis_size("pb"), lax.axis_size("ka")
    cores = n_pb // n_ka
    chips = n_pb // cores
    shard, plane = lax.axis_index("pb"), lax.axis_index("ka")
    bits = bits_of(chips)
    core = lax.rem(shard, cores)
    away = jnp.bitwise_xor(shard // cores, plane)
    held = list(halves)
    for r in range(len(bits)):
        pairs = []
        gets = jnp.bool_(False)
        for c in range(cores):
            order = bits if c % 2 == 0 else bits[::-1]
            known = sum(order[:r])
            for k in range(n_ka):
                for j in range(chips):
                    if (j ^ k) & ~known == 0:
                        pairs.append(((j * cores + c) * n_ka + k, ((j ^ order[r]) * cores + c) * n_ka + k))
            fresh = (jnp.bitwise_and(away, ~(known + order[r])) == 0) & (jnp.bitwise_and(away, order[r]) != 0)
            gets = gets | (fresh & (core == c))
        held = [jnp.where(gets, lax.ppermute(part, ("pb", "ka"), pairs), part) for part in held]
    return held


def body(
    atoms,
    atom_gain,
    atom_qkv,
    atom_proj,
    atom_bias,
    window_shift,
    token_of_atom,
    agg_weight,
    token_gain,
    token_q,
    token_kv,
    token_o,
    pair_bias,
):
    n_pb, n_ka = lax.axis_size("pb"), lax.axis_size("ka")
    shard, plane = lax.axis_index("pb"), lax.axis_index("ka")
    rows, width = atoms.shape
    tok_rows = pair_bias.shape[1]
    half = WIN_K // 2
    up = [(i, i + 1) for i in range(n_pb - 1)]
    down = [(i + 1, i) for i in range(n_pb - 1)]
    pos = shard.astype(jnp.int32).reshape(1)
    tok2d = token_of_atom.reshape(rows // LANES, LANES)
    left = lax.ppermute(atoms[rows - half :], "pb", up)
    right = lax.ppermute(atoms[:half], "pb", down)
    atom_out, near_out, msg = atom_attention(
        window_shift, pos, atoms, left, right, atom_gain, atom_qkv, atom_proj,
        atom_bias, tok2d, tok_rows, rows * n_pb,
    )
    behind = lax.ppermute(msg, "pb", up)
    token_repr = []
    for part in range(PARTS):
        sums, counts = pool(pos, near_out, agg_weight, tok2d, tok_rows, part)
        token_repr.append(finish(behind, agg_weight, sums, counts, part))
    late_bias, token_repr[0] = lax.optimization_barrier((pair_bias, token_repr[0]))
    parity = jnp.bitwise_and(plane ^ (plane >> 1), 1).astype(jnp.int32)
    core = lax.rem(shard, n_pb // n_ka).astype(jnp.int32)
    keep, send = parity.reshape(1), (1 - parity).reshape(1)
    share = tok_rows // 2
    send_bias = lax.dynamic_slice_in_dim(late_bias, (1 - parity) * share, share, axis=1)
    queries = project_queries(token_repr, token_gain, token_q)
    own_keys = key_parts(token_repr)
    own_keys[0], queries, send_bias = lax.optimization_barrier((own_keys[0], queries, send_bias))
    cores = [(p, p ^ 1) for p in range(n_pb)]
    other_keys = [lax.ppermute(own_keys[0], "pb", cores)]
    late_bias, own_keys[1] = lax.optimization_barrier((late_bias, own_keys[1]))
    other_keys.append(lax.ppermute(own_keys[1], "pb", cores))
    late_bias, send_bias = lax.optimization_barrier((late_bias, send_bias))
    keep_bias = lax.dynamic_slice_in_dim(late_bias, parity * share, share, axis=1)
    swap = [(i, i ^ 1) for i in range(n_ka)]
    bits = bits_of(n_ka)[1:]

    def far(msg, bit):
        return lax.ppermute(msg, "ka", [(i, i ^ (2 * bit - 1)) for i in range(n_ka)])

    x, k, v, msg = group_call(
        first_kernel, 0, send, (core.reshape(1),), queries, (*own_keys, *other_keys, token_gain), token_kv,
        send_bias, ("x", "k", "v", "msg"), "attend_first",
    )
    held, near = [(k, v)], [lax.ppermute(msg, "ka", swap)]
    for g in range(1, GROUPS):
        k, v, msg = group_call(
            functools.partial(next_kernel, g), g, send, (), queries, (x,), token_kv,
            send_bias, ("k", "v", "msg"), "attend_next",
        )
        held.append((k, v))
        near.append(lax.ppermute(msg, "ka", swap))
    sums, gone = [], []
    for g in range(GROUPS):
        o, lse, msg = group_call(
            functools.partial(keep_kernel, g), g, keep, (), queries, (*held[g], near[g]), None,
            keep_bias, ("o", "lse", "msg"), "attend_keep",
        )
        sums.append((o, lse))
        gone.append(far(msg, bits[0]))
    own_mix, other_mix = [], []
    for g in range(GROUPS):
        (o, lse), got = sums[g], gone[g]
        for bit in bits[1:]:
            o, lse, msg = merge(o, lse, got)
            got = far(msg, bit)
        own_mix.append(settle(o, lse, got))
        other_mix.append(lax.ppermute(own_mix[g], "ka", swap))
    return atom_out, output_rows(keep, own_mix, other_mix, token_repr, token_o)


def solution(mesh):
    return jax.shard_map(
        body,
        mesh=mesh,
        in_specs=(
            P("pb", None),
            P(),
            P(),
            P(),
            P(None, "pb", None),
            P("pb"),
            P("pb"),
            P(),
            P(),
            P(),
            P(),
            P(),
            P(None, "pb", "ka"),
        ),
        out_specs=(P("pb", None), P("pb", None)),
        check_vma=False,
    )
```

```python
import functools
import math

import jax
import jax.numpy as jnp
from jax import lax
from jax.experimental import pallas as pl
from jax.experimental.pallas import tpu as pltpu
from jax.sharding import PartitionSpec as P

AH = 4
TH = 16
WIN_Q = 32
WIN_K = 128
SHIFT_MAX = 384
PARTS = 2
LANES = 128
F32 = jnp.float32
BF16 = jnp.bfloat16
VMEM_LIMIT = 56 * 1024 * 1024
VMEM_SMALL = 24 * 1024 * 1024


def full(shape):
    return pl.BlockSpec(shape, lambda *_: (0,) * len(shape))


def params(limit=VMEM_LIMIT):
    return pltpu.CompilerParams(vmem_limit_bytes=limit)


def norm_rows(as_float, gain):
    centre = jnp.mean(as_float, axis=-1, keepdims=True)
    spread = jnp.mean(jnp.square(as_float - centre), axis=-1, keepdims=True)
    return (as_float - centre) * lax.rsqrt(spread + 1e-05) * gain


def dot(a, b):
    return jnp.dot(a, b, preferred_element_type=F32)


def atom_kernel(
    chunks,
    atom_total,
    tok_rows,
    shift_ref,
    pos_ref,
    atoms_ref,
    left_ref,
    right_ref,
    gain_ref,
    qkv_ref,
    proj_ref,
    bias_ref,
    tok_ref,
    out_ref,
    msg_ref,
    q_s,
    k_s,
    v_s,
    x_s,
):
    step = pl.program_id(0)
    rows, width = atoms_ref.shape
    size = out_ref.shape[0]
    half = WIN_K // 2
    head = width // AH
    shard = pos_ref[0]

    @pl.when(step == 0)
    def _():
        gain = gain_ref[...].reshape(1, width)
        x_s[:half, :] = left_ref[...]
        x_s[half : half + rows, :] = atoms_ref[...]
        x_s[half + rows :, :] = right_ref[...]
        total = rows + 2 * half
        tile = 5 * WIN_K if total % (5 * WIN_K) == 0 else WIN_K

        def one(c, carry):
            at = pl.ds(pl.multiple_of(c * tile, tile), tile)
            normed = norm_rows(x_s[at, :].astype(F32), gain).astype(BF16)
            res = dot(normed, qkv_ref[...])
            q_s[at, :] = (res[:, :width] * (1.0 / math.sqrt(head))).astype(BF16)
            k_s[:, at] = res[:, width : 2 * width].T.astype(BF16)
            v_s[at, :width] = res[:, 2 * width :].astype(BF16)
            v_s[at, width:] = jnp.ones((tile, width), BF16)
            return carry

        lax.fori_loop(0, total // tile, one, 0, unroll=True)

    group = WIN_K // WIN_Q
    atoms_group = group * WIN_Q
    span = AH * WIN_Q
    lane_q = lax.broadcasted_iota(jnp.int32, (WIN_Q, width), 1)
    heads = [(lane_q >= h * head) & (lane_q < (h + 1) * head) for h in range(AH)]
    lane = lax.broadcasted_iota(jnp.int32, (span, WIN_K), 1)
    slot = lax.broadcasted_iota(jnp.int32, (1, WIN_K), 1)
    blocks = size // WIN_Q

    def region(n):
        return pl.ds(pl.multiple_of(step * size + n // group * atoms_group, atoms_group), 2 * WIN_K)

    def score(g):
        query = q_s[pl.ds(pl.multiple_of(step * size + g * atoms_group + half, half), atoms_group), :].astype(F32)
        stacked = [
            jnp.where(m, query[i * WIN_Q : (i + 1) * WIN_Q], 0.0).astype(BF16) for i in range(group) for m in heads
        ]
        return dot(jnp.concatenate(stacked, axis=0), k_s[:, region(g * group)])

    def soften(n, scores):
        offset = n % group * WIN_Q + half + shift_ref[step * blocks + n]
        early = lane >= offset
        begin = n * WIN_Q
        bias = bias_ref[:, begin : begin + WIN_Q, :].astype(F32).reshape(span, WIN_K)
        index = slot + jnp.where(slot >= offset, 0, WIN_K)
        index = index + (step * size + n // group * atoms_group + shard * rows - half)
        shut = jnp.where((index >= 0) & (index < atom_total), 0.0, -jnp.inf)
        logits = jnp.where(early, scores[:, :WIN_K], scores[:, WIN_K:]) + (
            pltpu.roll(bias, jnp.bitwise_and(offset, WIN_K - 1), 1) + shut
        )
        terms = jnp.exp(logits - jnp.max(logits, axis=-1, keepdims=True))
        return jnp.concatenate(
            [jnp.where(early, terms, 0.0).astype(BF16), jnp.where(early, 0.0, terms).astype(BF16)], axis=1
        )

    def mix(g, weights):
        mixed = dot(jnp.concatenate(weights, axis=0), v_s[region(g * group), :])
        merged = []
        for i in range(group):
            parts = [mixed[(i * AH + h) * WIN_Q : (i * AH + h + 1) * WIN_Q] for h in range(AH)]
            values, total = parts[0][:, :width], parts[0][:, width:]
            for h in range(1, AH):
                values = jnp.where(heads[h], parts[h][:, :width], values)
                total = jnp.where(heads[h], parts[h][:, width:], total)
            merged.append((values / total).astype(BF16))
        local = g * atoms_group
        at = pl.multiple_of(step * size + local, atoms_group)
        own = atoms_ref[pl.ds(at, atoms_group), :].astype(F32)
        result = own + dot(jnp.concatenate(merged, axis=0), proj_ref[...])
        out_ref[local : local + atoms_group, :] = result.astype(BF16)

    groups = blocks // group
    ahead = score(0)
    behind = None
    for g in range(groups):
        scores = ahead
        if g + 1 < groups:
            ahead = score(g + 1)
        if g:
            mix(g - 1, behind)
        behind = [soften(g * group + i, scores[i * span : (i + 1) * span]) for i in range(group)]
    mix(groups - 1, behind)

    @pl.when(step == chunks - 1)
    def _():
        ids = tok_ref[tok_ref.shape[0] - 8 :, :]
        code = jnp.maximum(ids - (shard + 1) * tok_rows + 1, 0)
        high = (code >> 4).astype(F32)
        low = (code & 15).astype(F32)
        msg_ref[:SHIFT_MAX, :] = out_ref[size - SHIFT_MAX :, :]
        msg_ref[SHIFT_MAX:, :] = jnp.concatenate([high, low], axis=0).astype(BF16)


def atom_attention(shift, pos, atoms, left, right, gain, qkv, proj, bias, tok2d, tok_rows, atom_total):
    rows, width = atoms.shape
    size = 2 * SHIFT_MAX
    chunks = rows // size
    half = WIN_K // 2
    return pl.pallas_call(
        functools.partial(atom_kernel, chunks, atom_total, tok_rows),
        grid_spec=pltpu.PrefetchScalarGridSpec(
            num_scalar_prefetch=2,
            grid=(chunks,),
            in_specs=[
                full((rows, width)),
                full((half, width)),
                full((half, width)),
                full((width,)),
                full(qkv.shape),
                full(proj.shape),
                pl.BlockSpec((AH, size, WIN_K), lambda i, *_: (0, i, 0)),
                full(tok2d.shape),
            ],
            out_specs=[
                pl.BlockSpec((size, width), lambda i, *_: (i, 0)),
                full((SHIFT_MAX + 16, width)),
            ],
            scratch_shapes=[
                pltpu.VMEM((rows + 2 * half, width), BF16),
                pltpu.VMEM((width, rows + 2 * half), BF16),
                pltpu.VMEM((rows + 2 * half, 2 * width), BF16),
                pltpu.VMEM((rows + 2 * half, width), BF16),
            ],
        ),
        out_shape=[
            jax.ShapeDtypeStruct((rows, width), BF16),
            jax.ShapeDtypeStruct((SHIFT_MAX + 16, width), BF16),
        ],
        compiler_params=params(),
        cost_estimate=pl.CostEstimate(flops=8 * 10**9, bytes_accessed=6 * 10**6, transcendentals=2 * 10**6),
        name="atom_attention",
    )(shift, pos, atoms, left, right, gain, qkv, proj, bias, tok2d)


def activate(rows, weight_half):
    u = dot(rows, weight_half)
    return (u + u * jnp.tanh(u)).astype(BF16)


def pool_kernel(tok_rows, pos_ref, out_ref, weight_ref, tok_ref, sum_ref, cnt_ref):
    step = pl.program_id(0)
    size = out_ref.shape[0]
    lines = size // LANES
    base = pos_ref[0] * tok_rows
    token = lax.broadcasted_iota(jnp.int32, (tok_rows, LANES), 0)
    weight_half = (weight_ref[...].astype(F32) * 0.5).astype(BF16)
    hidden = activate(out_ref[...], weight_half)
    ones = []
    for j in range(lines):
        ids = tok_ref[pl.ds(step * lines + j, 1), :] - base
        ones.append(jnp.where(token == ids, 1.0, 0.0))
    hot = jnp.concatenate(ones, axis=1).astype(BF16)
    count = functools.reduce(jnp.add, ones)
    more = dot(hot, hidden)

    @pl.when(step == 0)
    def _():
        sum_ref[...] = more
        cnt_ref[...] = count

    @pl.when(step > 0)
    def _():
        sum_ref[...] += more
        cnt_ref[...] += count


def pool(pos, atom_out, weight, tok2d, tok_rows, part):
    rows, width = atom_out.shape
    feats = weight.shape[1] // PARTS
    size = min(1024, rows)
    return pl.pallas_call(
        functools.partial(pool_kernel, tok_rows),
        grid_spec=pltpu.PrefetchScalarGridSpec(
            num_scalar_prefetch=1,
            grid=(rows // size,),
            in_specs=[
                pl.BlockSpec((size, width), lambda i, *_: (i, 0)),
                pl.BlockSpec((width, feats), lambda i, *_: (0, part)),
                full(tok2d.shape),
            ],
            out_specs=[full((tok_rows, feats)), full((tok_rows, LANES))],
        ),
        out_shape=[
            jax.ShapeDtypeStruct((tok_rows, feats), F32),
            jax.ShapeDtypeStruct((tok_rows, LANES), F32),
        ],
        compiler_params=params(VMEM_SMALL),
        cost_estimate=pl.CostEstimate(flops=2 * 10**9, bytes_accessed=2 * 10**6, transcendentals=10**6),
        name="pool",
    )(pos, atom_out, weight, tok2d)


def finish_kernel(msg_ref, weight_ref, sum_ref, cnt_ref, repr_ref):
    tok_rows = sum_ref.shape[0]
    size = msg_ref.shape[0] - 16
    lines = size // LANES
    token = lax.broadcasted_iota(jnp.int32, (tok_rows, LANES), 0).astype(F32)
    weight_half = (weight_ref[...].astype(F32) * 0.5).astype(BF16)
    hidden = activate(msg_ref[:size, :], weight_half)
    codes = msg_ref[size:, :].astype(F32)
    ids = codes[:8] * 16.0 + codes[8:] - 1.0
    ones = [jnp.where(token == ids[8 - lines + j : 9 - lines + j], 1.0, 0.0) for j in range(lines)]
    hot = jnp.concatenate(ones, axis=1).astype(BF16)
    count = functools.reduce(jnp.add, ones) + cnt_ref[...]
    sums = sum_ref[...] + dot(hot, hidden)
    repr_ref[...] = (sums / jnp.sum(count, axis=1, keepdims=True)).astype(BF16)


def finish(msg, weight, sums, counts, part):
    rows, feats = sums.shape
    return pl.pallas_call(
        finish_kernel,
        grid=(1,),
        in_specs=[
            full(msg.shape),
            pl.BlockSpec((weight.shape[0], feats), lambda i: (0, part)),
            full(sums.shape),
            full(counts.shape),
        ],
        out_specs=full((rows, feats)),
        out_shape=jax.ShapeDtypeStruct((rows, feats), BF16),
        compiler_params=params(VMEM_SMALL),
        cost_estimate=pl.CostEstimate(flops=2 * 10**8, bytes_accessed=2 * 10**6, transcendentals=2 * 10**5),
        name="token_finish",
    )(msg, weight, sums, counts)


def query_kernel(scale, a_ref, b_ref, gain_ref, weight_ref, bias_ref, kv_ref, out_ref, bias_out, kv_out):
    del bias_ref, kv_ref, bias_out, kv_out
    rows = jnp.concatenate([a_ref[...].astype(F32), b_ref[...].astype(F32)], axis=1)
    normed = norm_rows(rows, gain_ref[...].reshape(1, -1)).astype(BF16)
    out_ref[...] = (dot(normed, weight_ref[...]) * scale).astype(BF16)


def project_queries(halves, gain, weight, bias, kv):
    rows = halves[0].shape[0]
    return pl.pallas_call(
        functools.partial(query_kernel, 1.0 / math.sqrt(weight.shape[1] // TH)),
        in_specs=[pl.BlockSpec(memory_space=pltpu.VMEM)] * 6,
        out_specs=[pl.BlockSpec(memory_space=pltpu.VMEM)] * 3,
        out_shape=[
            jax.ShapeDtypeStruct((rows, weight.shape[1]), BF16),
            jax.ShapeDtypeStruct(bias.shape, bias.dtype),
            jax.ShapeDtypeStruct(kv.shape, kv.dtype),
        ],
        input_output_aliases={4: 1, 5: 2},
        compiler_params=params(VMEM_SMALL),
        cost_estimate=pl.CostEstimate(flops=5 * 10**8, bytes_accessed=3 * 10**6, transcendentals=0),
        name="queries",
    )(*halves, gain, weight, bias, kv)


GROUPS = 2
ROW_TILE = 32


def pack_message(mixed, lse, heads):
    lane = lax.broadcasted_iota(jnp.int32, lse.shape, 1)
    high = lse.astype(BF16).astype(F32)
    rest = lse - high
    middle = rest.astype(BF16).astype(F32)
    low = rest - middle
    first = jnp.where(lane < heads, high, pltpu.roll(middle, heads, 1))
    second = jnp.where(lane < heads, low, 0.0)
    turned = jnp.concatenate([first, second], axis=0).T
    return jnp.concatenate([mixed.astype(BF16), turned[: 2 * heads].astype(BF16)], axis=0)


def unpack_message(msg, rows, heads):
    coded = msg[rows:].astype(F32)
    coded = jnp.concatenate([coded, jnp.zeros((LANES - 2 * heads, coded.shape[1]), F32)], axis=0).T
    first = coded[:rows]
    return msg[:rows].astype(F32), first + pltpu.roll(first, LANES - heads, 1) + coded[rows:]


def merge_parts(mixed, lse, other, lse_b, heads):
    rows, feats = mixed.shape
    width = feats // heads
    spot = lax.broadcasted_iota(jnp.int32, (rows, LANES), 1)
    lse_b = jnp.where(spot < heads, lse_b, lse)
    top = jnp.maximum(lse, lse_b)
    part = jnp.exp(lse - top)
    total = part + jnp.exp(lse_b - top)
    share = part / total
    high = share.astype(BF16)
    low = (share - high.astype(F32)).astype(BF16)
    head = lax.broadcasted_iota(jnp.int32, (LANES, feats), 0) * width
    column = lax.broadcasted_iota(jnp.int32, (LANES, feats), 1)
    spread = jnp.where((column >= head) & (column < head + width), 1.0, 0.0).astype(BF16)
    wide = dot(high, spread) + dot(low, spread)
    return other + wide * (mixed - other), top + jnp.log(total)


def attend_group(group, heads, width, half, q_ref, k_ref, v_ref, bias_ref, scratch):
    score_s, term_s, top_s, mix_s = scratch
    rows = mix_s.shape[0]
    at = pl.multiple_of(half * rows, rows)
    pairs = heads // 2
    spot = lax.broadcasted_iota(jnp.int32, (rows, LANES), 1)

    def layout(p):
        first = 2 * p * width
        low = first // LANES * LANES
        wide = -(-(first + 2 * width) // LANES) * LANES - low
        lane = lax.broadcasted_iota(jnp.int32, (rows, wide), 1)
        first -= low
        masks = [(lane >= first + j * width) & (lane < first + (j + 1) * width) for j in range(2)]
        return slice(low, low + wide), first, masks

    keys = score_s[0].shape[1]
    chunk = min(256, keys)
    chunks = keys // chunk
    tiles = 2 * rows // ROW_TILE

    def stack(p):
        window, _, masks = layout(p)
        query = q_ref[pl.ds(at, rows), window].astype(F32)
        return jnp.concatenate([jnp.where(m, query, 0.0).astype(BF16) for m in masks], axis=0)

    def score(p, n, stacked):
        part = slice(n * chunk, (n + 1) * chunk)
        score_s[p % 2][:, part] = dot(stacked, k_ref[layout(p)[0], part])

    def soften(p, n):
        for r in range(n * tiles // chunks * ROW_TILE, (n + 1) * tiles // chunks * ROW_TILE, ROW_TILE):
            line = pl.multiple_of(at + r % rows, ROW_TILE)
            bias = bias_ref[group * heads + 2 * p + r // rows, pl.ds(line, ROW_TILE), :].astype(F32)
            scores = score_s[p % 2][r : r + ROW_TILE, :] + bias
            top = jnp.max(scores, axis=-1, keepdims=True)
            term_s[p % 2][r : r + ROW_TILE, :] = jnp.exp(scores - top).astype(BF16)
            top_s[p % 2][r : r + ROW_TILE, :] = jnp.broadcast_to(top, (ROW_TILE, LANES))

    def mix(p, n, mixed):
        part = slice(n * chunk, (n + 1) * chunk)
        window, first, _ = layout(p)
        values = v_ref[part, window]
        column = lax.broadcasted_iota(jnp.int32, values.shape, 1)
        used = (column >= first) & (column < first + 2 * width)
        more = dot(term_s[p % 2][:, part], jnp.where(used, values.astype(F32), 1.0).astype(BF16))
        return more if mixed is None else mixed + more

    def close(p, mixed, lse):
        window, first, masks = layout(p)
        free = 0 if first >= 16 else 2 * width
        total = mixed[:, free : free + 1]
        mixed = mixed / total
        sums = top_s[p % 2][...] + jnp.log(total)
        result = mix_s[:, window]
        for j in range(2):
            result = jnp.where(masks[j], mixed[j * rows : (j + 1) * rows], result)
            lse = jnp.where(spot == 2 * p + j, sums[j * rows : (j + 1) * rows], lse)
        mix_s[:, window] = result
        return lse

    lse = jnp.zeros((rows, LANES), F32)
    stacked = stack(0)
    for n in range(chunks):
        score(0, n, stacked)
    for p in range(pairs):
        mixed = None
        if p + 1 < pairs:
            stacked = stack(p + 1)
        for n in range(chunks):
            if p + 1 < pairs:
                score(p + 1, n, stacked)
            if p:
                mixed = mix(p - 1, n, mixed)
            soften(p, n)
        if p:
            lse = close(p - 1, mixed, lse)
    mixed = None
    for n in range(chunks):
        mixed = mix(pairs - 1, n, mixed)
    lse = close(pairs - 1, mixed, lse)
    return mix_s[...], lse


def group_scratch(rows, keys, feats, heads):
    return [
        pltpu.VMEM((2 * rows, keys), F32),
        pltpu.VMEM((2 * rows, keys), F32),
        pltpu.VMEM((2 * rows, keys), BF16),
        pltpu.VMEM((2 * rows, keys), BF16),
        pltpu.VMEM((2 * rows, LANES), F32),
        pltpu.VMEM((2 * rows, LANES), F32),
        pltpu.VMEM((rows, feats), F32),
    ]


def scratch_of(refs):
    return refs[:2], refs[2:4], refs[4:6], refs[6]


def project_keys(group, x_ref, weight_ref, k_ref, v_ref):
    tile = x_ref.shape[0] // 2
    feats = v_ref.shape[1]
    for r in range(0, x_ref.shape[0], tile):
        rows = x_ref[r : r + tile, :]
        k_ref[:, r : r + tile] = dot(rows, weight_ref[:, group * feats : (group + 1) * feats]).T.astype(BF16)
        at = (GROUPS + group) * feats
        v_ref[r : r + tile, :] = dot(rows, weight_ref[:, at : at + feats]).astype(BF16)


def first_kernel(heads, width, half_ref, core_ref, q_ref, own_a, own_b, other_a, other_b, gain_ref, weight_ref,
                 bias_ref, x_ref, k_ref, v_ref, msg_ref, kv_out, bias_out, *refs):
    scratch = scratch_of(refs)
    rows = own_a.shape[0]
    core = core_ref[0]
    gain = gain_ref[...].reshape(1, -1)
    for place, parts in ((core, (own_a, own_b)), (1 - core, (other_a, other_b))):
        values = jnp.concatenate([part[...].astype(F32) for part in parts], axis=1)
        x_ref[pl.ds(pl.multiple_of(place * rows, rows), rows), :] = norm_rows(values, gain).astype(BF16)
    project_keys(0, x_ref, weight_ref, k_ref, v_ref)
    mixed, lse = attend_group(0, heads, width, half_ref[0], q_ref, k_ref, v_ref, bias_ref, scratch)
    msg_ref[...] = pack_message(mixed, lse, heads)


def next_kernel(group, heads, width, half_ref, q_ref, x_ref, weight_ref, bias_ref, k_ref, v_ref, msg_ref, kv_out, bias_out, *refs):
    scratch = scratch_of(refs)
    project_keys(group, x_ref, weight_ref, k_ref, v_ref)
    mixed, lse = attend_group(group, heads, width, half_ref[0], q_ref, k_ref, v_ref, bias_ref, scratch)
    msg_ref[...] = pack_message(mixed, lse, heads)


def keep_kernel(group, heads, width, half_ref, q_ref, k_ref, v_ref, near_ref, bias_ref, o_ref, lse_ref, msg_ref, bias_out, *refs):
    scratch = scratch_of(refs)
    mixed, lse = attend_group(group, heads, width, half_ref[0], q_ref, k_ref, v_ref, bias_ref, scratch)
    rows = mixed.shape[0]
    mixed, lse = merge_parts(mixed, lse, *unpack_message(near_ref[...], rows, heads), heads)
    o_ref[...] = mixed
    lse_ref[...] = lse
    msg_ref[...] = pack_message(mixed, lse, heads)


def group_call(kernel, group, half, scalars, q, arrays, weights, bias, outs, name):
    tok_rows, all_feats = q.shape
    rows, keys, feats = tok_rows // 2, bias.shape[2], all_feats // GROUPS
    heads = TH // GROUPS
    shapes = {
        "x": ((keys, all_feats), BF16),
        "k": ((feats, keys), BF16),
        "v": ((keys, feats), BF16),
        "o": ((rows, feats), F32),
        "lse": ((rows, LANES), F32),
        "msg": ((rows + 2 * heads, feats), BF16),
    }
    held = ([] if weights is None else [weights]) + [bias]
    before = 2 + len(scalars) + len(arrays)
    return pl.pallas_call(
        functools.partial(kernel, heads, feats // heads),
        grid_spec=pltpu.PrefetchScalarGridSpec(
            num_scalar_prefetch=1 + len(scalars),
            grid=(1,),
            in_specs=[pl.BlockSpec((tok_rows, feats), lambda i, *_: (0, group))]
            + [full(array.shape) for array in arrays]
            + [pl.BlockSpec(memory_space=pltpu.VMEM)] * len(held),
            out_specs=[full(shapes[out][0]) for out in outs]
            + [pl.BlockSpec(memory_space=pltpu.VMEM)] * len(held),
            scratch_shapes=group_scratch(rows, keys, feats, heads),
        ),
        out_shape=[jax.ShapeDtypeStruct(*shapes[out]) for out in outs]
        + [jax.ShapeDtypeStruct(array.shape, array.dtype) for array in held],
        input_output_aliases={before + i: len(outs) + i for i in range(len(held))},
        compiler_params=params(VMEM_SMALL),
        cost_estimate=pl.CostEstimate(flops=4 * 10**9, bytes_accessed=4 * 10**6, transcendentals=10**6),
        name=name,
    )(half, *scalars, q, *arrays, *held)


def merge_kernel(heads, o_ref, lse_ref, msg_ref, out_ref, sum_ref, back_ref):
    rows = o_ref.shape[0]
    mixed, lse = merge_parts(o_ref[...], lse_ref[...], *unpack_message(msg_ref[...], rows, heads), heads)
    out_ref[...] = mixed
    sum_ref[...] = lse
    back_ref[...] = pack_message(mixed, lse, heads)


def merge(o, lse, msg):
    return pl.pallas_call(
        functools.partial(merge_kernel, TH // GROUPS),
        out_shape=[jax.ShapeDtypeStruct(a.shape, a.dtype) for a in (o, lse, msg)],
        compiler_params=params(VMEM_SMALL),
        name="merge",
    )(o, lse, msg)


def settle_kernel(heads, o_ref, lse_ref, msg_ref, out_ref):
    rows = o_ref.shape[0]
    mixed, _ = merge_parts(o_ref[...], lse_ref[...], *unpack_message(msg_ref[...], rows, heads), heads)
    out_ref[...] = mixed.astype(BF16)


def settle(o, lse, msg):
    return pl.pallas_call(
        functools.partial(settle_kernel, TH // GROUPS),
        out_shape=jax.ShapeDtypeStruct(o.shape, BF16),
        compiler_params=params(VMEM_SMALL),
        name="settle",
    )(o, lse, msg)


def output_kernel(half_ref, own_a, own_b, other_a, other_b, a_ref, b_ref, weight_ref, out_ref):
    rows, feats = own_a.shape
    for place, first, second in ((half_ref[0], own_a, own_b), (1 - half_ref[0], other_a, other_b)):
        mine = pl.ds(pl.multiple_of(place * rows, rows), rows)
        result = dot(first[...], weight_ref[:feats, :]) + dot(second[...], weight_ref[feats:, :])
        out_ref[mine, :feats] = (a_ref[mine, :].astype(F32) + result[:, :feats]).astype(BF16)
        out_ref[mine, feats:] = (b_ref[mine, :].astype(F32) + result[:, feats:]).astype(BF16)


def output_rows(half, own, other, token_repr, weight):
    rows = token_repr[0].shape[0]
    return pl.pallas_call(
        output_kernel,
        in_specs=[pl.BlockSpec(memory_space=pltpu.SMEM)] + [pl.BlockSpec(memory_space=pltpu.VMEM)] * 7,
        out_shape=jax.ShapeDtypeStruct((rows, weight.shape[1]), BF16),
        compiler_params=params(VMEM_SMALL),
        name="output_rows",
    )(half, *own, *other, *token_repr, weight)


def bits_of(count):
    return [1 << b for b in range(count.bit_length() - 1)]


def key_parts(halves):
    n_pb, n_ka = lax.axis_size("pb"), lax.axis_size("ka")
    cores = n_pb // n_ka
    chips = n_pb // cores
    shard, plane = lax.axis_index("pb"), lax.axis_index("ka")
    bits = bits_of(chips)
    core = lax.rem(shard, cores)
    away = jnp.bitwise_xor(shard // cores, plane)
    held = list(halves)
    for r in range(len(bits)):
        pairs = []
        gets = jnp.bool_(False)
        for c in range(cores):
            order = bits if c % 2 == 0 else bits[::-1]
            known = sum(order[:r])
            for k in range(n_ka):
                for j in range(chips):
                    if (j ^ k) & ~known == 0:
                        pairs.append(((j * cores + c) * n_ka + k, ((j ^ order[r]) * cores + c) * n_ka + k))
            fresh = (jnp.bitwise_and(away, ~(known + order[r])) == 0) & (jnp.bitwise_and(away, order[r]) != 0)
            gets = gets | (fresh & (core == c))
        held = [jnp.where(gets, lax.ppermute(part, ("pb", "ka"), pairs), part) for part in held]
    return held


def body(
    atoms,
    atom_gain,
    atom_qkv,
    atom_proj,
    atom_bias,
    window_shift,
    token_of_atom,
    agg_weight,
    token_gain,
    token_q,
    token_kv,
    token_o,
    pair_bias,
):
    n_pb, n_ka = lax.axis_size("pb"), lax.axis_size("ka")
    shard, plane = lax.axis_index("pb"), lax.axis_index("ka")
    rows, width = atoms.shape
    tok_rows = pair_bias.shape[1]
    half = WIN_K // 2
    up = [(i, i + 1) for i in range(n_pb - 1)]
    down = [(i + 1, i) for i in range(n_pb - 1)]
    pos = shard.astype(jnp.int32).reshape(1)
    tok2d = token_of_atom.reshape(rows // LANES, LANES)
    left = lax.ppermute(atoms[rows - half :], "pb", up)
    right = lax.ppermute(atoms[:half], "pb", down)
    atom_out, msg = atom_attention(
        window_shift, pos, atoms, left, right, atom_gain, atom_qkv, atom_proj,
        atom_bias, tok2d, tok_rows, rows * n_pb,
    )
    behind = lax.ppermute(msg, "pb", up)
    token_repr = []
    for part in range(PARTS):
        sums, counts = pool(pos, atom_out, agg_weight, tok2d, tok_rows, part)
        token_repr.append(finish(behind, agg_weight, sums, counts, part))
    parity = jnp.bitwise_and(plane ^ (plane >> 1), 1).astype(jnp.int32)
    core = lax.rem(shard, n_pb // n_ka).astype(jnp.int32)
    keep, send = parity.reshape(1), (1 - parity).reshape(1)
    late_bias, late_kv, token_repr[0] = lax.optimization_barrier((pair_bias, token_kv, token_repr[0]))
    queries, bias, kv = project_queries(token_repr, token_gain, token_q, late_bias, late_kv)
    own_keys = key_parts(token_repr)
    own_keys[0], queries = lax.optimization_barrier((own_keys[0], queries))
    other_keys = [lax.ppermute(part, "pb", [(p, p ^ 1) for p in range(n_pb)]) for part in own_keys]
    swap = [(i, i ^ 1) for i in range(n_ka)]
    bits = bits_of(n_ka)[1:]

    def far(msg, bit):
        return lax.ppermute(msg, "ka", [(i, i ^ (2 * bit - 1)) for i in range(n_ka)])

    x, k, v, msg, kv, bias = group_call(
        first_kernel, 0, send, (core.reshape(1),), queries, (*own_keys, *other_keys, token_gain), kv,
        bias, ("x", "k", "v", "msg"), "attend_first",
    )
    held, near = [(k, v)], [lax.ppermute(msg, "ka", swap)]
    for g in range(1, GROUPS):
        k, v, msg, kv, bias = group_call(
            functools.partial(next_kernel, g), g, send, (), queries, (x,), kv,
            bias, ("k", "v", "msg"), "attend_next",
        )
        held.append((k, v))
        near.append(lax.ppermute(msg, "ka", swap))
    sums, gone = [], []
    for g in range(GROUPS):
        o, lse, msg, bias = group_call(
            functools.partial(keep_kernel, g), g, keep, (), queries, (*held[g], near[g]), None,
            bias, ("o", "lse", "msg"), "attend_keep",
        )
        sums.append((o, lse))
        gone.append(far(msg, bits[0]))
    own_mix, other_mix = [], []
    for g in range(GROUPS):
        (o, lse), got = sums[g], gone[g]
        for bit in bits[1:]:
            o, lse, msg = merge(o, lse, got)
            got = far(msg, bit)
        own_mix.append(settle(o, lse, got))
        other_mix.append(lax.ppermute(own_mix[g], "ka", swap))
    return atom_out, output_rows(keep, own_mix, other_mix, token_repr, token_o)


def solution(mesh):
    return jax.shard_map(
        body,
        mesh=mesh,
        in_specs=(
            P("pb", None),
            P(),
            P(),
            P(),
            P(None, "pb", None),
            P("pb"),
            P("pb"),
            P(),
            P(),
            P(),
            P(),
            P(),
            P(None, "pb", "ka"),
        ),
        out_specs=(P("pb", None), P("pb", None)),
        check_vma=False,
    )
```

```python
import functools
import math

import jax
import jax.numpy as jnp
from jax import lax
from jax.experimental import pallas as pl
from jax.experimental.pallas import tpu as pltpu
from jax.sharding import PartitionSpec as P

AH = 4
TH = 16
WIN_Q = 32
WIN_K = 128
SHIFT_MAX = 384
PARTS = 2
LANES = 128
F32 = jnp.float32
BF16 = jnp.bfloat16
VMEM_LIMIT = 56 * 1024 * 1024
VMEM_SMALL = 24 * 1024 * 1024


def full(shape):
    return pl.BlockSpec(shape, lambda *_: (0,) * len(shape))


def params(limit=VMEM_LIMIT):
    return pltpu.CompilerParams(vmem_limit_bytes=limit)


def norm_rows(as_float, gain):
    centre = jnp.mean(as_float, axis=-1, keepdims=True)
    spread = jnp.mean(jnp.square(as_float - centre), axis=-1, keepdims=True)
    return (as_float - centre) * lax.rsqrt(spread + 1e-05) * gain


def dot(a, b):
    return jnp.dot(a, b, preferred_element_type=F32)


def atom_kernel(
    chunks,
    atom_total,
    tok_rows,
    shift_ref,
    pos_ref,
    atoms_ref,
    left_ref,
    right_ref,
    gain_ref,
    qkv_ref,
    proj_ref,
    bias_ref,
    tok_ref,
    out_ref,
    msg_ref,
    q_s,
    k_s,
    v_s,
    x_s,
):
    step = pl.program_id(0)
    rows, width = atoms_ref.shape
    size = out_ref.shape[0]
    half = WIN_K // 2
    head = width // AH
    shard = pos_ref[0]

    @pl.when(step == 0)
    def _():
        gain = gain_ref[...].reshape(1, width)
        x_s[:half, :] = left_ref[...]
        x_s[half : half + rows, :] = atoms_ref[...]
        x_s[half + rows :, :] = right_ref[...]
        total = rows + 2 * half
        tile = 5 * WIN_K if total % (5 * WIN_K) == 0 else WIN_K

        def one(c, carry):
            at = pl.ds(pl.multiple_of(c * tile, tile), tile)
            normed = norm_rows(x_s[at, :].astype(F32), gain).astype(BF16)
            res = dot(normed, qkv_ref[...])
            q_s[at, :] = (res[:, :width] * (1.0 / math.sqrt(head))).astype(BF16)
            k_s[:, at] = res[:, width : 2 * width].T.astype(BF16)
            v_s[at, :width] = res[:, 2 * width :].astype(BF16)
            v_s[at, width:] = jnp.ones((tile, width), BF16)
            return carry

        lax.fori_loop(0, total // tile, one, 0, unroll=True)

    group = WIN_K // WIN_Q
    atoms_group = group * WIN_Q
    span = AH * WIN_Q
    lane_q = lax.broadcasted_iota(jnp.int32, (WIN_Q, width), 1)
    heads = [(lane_q >= h * head) & (lane_q < (h + 1) * head) for h in range(AH)]
    lane = lax.broadcasted_iota(jnp.int32, (span, WIN_K), 1)
    slot = lax.broadcasted_iota(jnp.int32, (1, WIN_K), 1)
    blocks = size // WIN_Q

    def region(n):
        return pl.ds(pl.multiple_of(step * size + n // group * atoms_group, atoms_group), 2 * WIN_K)

    def score(g):
        query = q_s[pl.ds(pl.multiple_of(step * size + g * atoms_group + half, half), atoms_group), :].astype(F32)
        stacked = [
            jnp.where(m, query[i * WIN_Q : (i + 1) * WIN_Q], 0.0).astype(BF16) for i in range(group) for m in heads
        ]
        return dot(jnp.concatenate(stacked, axis=0), k_s[:, region(g * group)])

    def soften(n, scores):
        offset = n % group * WIN_Q + half + shift_ref[step * blocks + n]
        early = lane >= offset
        begin = n * WIN_Q
        bias = bias_ref[:, begin : begin + WIN_Q, :].astype(F32).reshape(span, WIN_K)
        index = slot + jnp.where(slot >= offset, 0, WIN_K)
        index = index + (step * size + n // group * atoms_group + shard * rows - half)
        shut = jnp.where((index >= 0) & (index < atom_total), 0.0, -jnp.inf)
        logits = jnp.where(early, scores[:, :WIN_K], scores[:, WIN_K:]) + (
            pltpu.roll(bias, jnp.bitwise_and(offset, WIN_K - 1), 1) + shut
        )
        terms = jnp.exp(logits - jnp.max(logits, axis=-1, keepdims=True))
        return jnp.concatenate(
            [jnp.where(early, terms, 0.0).astype(BF16), jnp.where(early, 0.0, terms).astype(BF16)], axis=1
        )

    def mix(g, weights):
        mixed = dot(jnp.concatenate(weights, axis=0), v_s[region(g * group), :])
        merged = []
        for i in range(group):
            parts = [mixed[(i * AH + h) * WIN_Q : (i * AH + h + 1) * WIN_Q] for h in range(AH)]
            values, total = parts[0][:, :width], parts[0][:, width:]
            for h in range(1, AH):
                values = jnp.where(heads[h], parts[h][:, :width], values)
                total = jnp.where(heads[h], parts[h][:, width:], total)
            merged.append((values / total).astype(BF16))
        local = g * atoms_group
        at = pl.multiple_of(step * size + local, atoms_group)
        own = atoms_ref[pl.ds(at, atoms_group), :].astype(F32)
        result = own + dot(jnp.concatenate(merged, axis=0), proj_ref[...])
        out_ref[local : local + atoms_group, :] = result.astype(BF16)

    groups = blocks // group
    ahead = score(0)
    behind = None
    for g in range(groups):
        scores = ahead
        if g + 1 < groups:
            ahead = score(g + 1)
        if g:
            mix(g - 1, behind)
        behind = [soften(g * group + i, scores[i * span : (i + 1) * span]) for i in range(group)]
    mix(groups - 1, behind)

    @pl.when(step == chunks - 1)
    def _():
        ids = tok_ref[tok_ref.shape[0] - 8 :, :]
        code = jnp.maximum(ids - (shard + 1) * tok_rows + 1, 0)
        high = (code >> 4).astype(F32)
        low = (code & 15).astype(F32)
        msg_ref[:SHIFT_MAX, :] = out_ref[size - SHIFT_MAX :, :]
        msg_ref[SHIFT_MAX:, :] = jnp.concatenate([high, low], axis=0).astype(BF16)


def atom_attention(shift, pos, atoms, left, right, gain, qkv, proj, bias, tok2d, tok_rows, atom_total):
    rows, width = atoms.shape
    size = 2 * SHIFT_MAX
    chunks = rows // size
    half = WIN_K // 2
    return pl.pallas_call(
        functools.partial(atom_kernel, chunks, atom_total, tok_rows),
        grid_spec=pltpu.PrefetchScalarGridSpec(
            num_scalar_prefetch=2,
            grid=(chunks,),
            in_specs=[
                full((rows, width)),
                full((half, width)),
                full((half, width)),
                full((width,)),
                full(qkv.shape),
                full(proj.shape),
                pl.BlockSpec((AH, size, WIN_K), lambda i, *_: (0, i, 0)),
                full(tok2d.shape),
            ],
            out_specs=[
                pl.BlockSpec((size, width), lambda i, *_: (i, 0)),
                full((SHIFT_MAX + 16, width)),
            ],
            scratch_shapes=[
                pltpu.VMEM((rows + 2 * half, width), BF16),
                pltpu.VMEM((width, rows + 2 * half), BF16),
                pltpu.VMEM((rows + 2 * half, 2 * width), BF16),
                pltpu.VMEM((rows + 2 * half, width), BF16),
            ],
        ),
        out_shape=[
            jax.ShapeDtypeStruct((rows, width), BF16),
            jax.ShapeDtypeStruct((SHIFT_MAX + 16, width), BF16),
        ],
        compiler_params=params(),
        cost_estimate=pl.CostEstimate(flops=8 * 10**9, bytes_accessed=6 * 10**6, transcendentals=2 * 10**6),
        name="atom_attention",
    )(shift, pos, atoms, left, right, gain, qkv, proj, bias, tok2d)


def activate(rows, weight_half):
    u = dot(rows, weight_half)
    return (u + u * jnp.tanh(u)).astype(BF16)


def pool_kernel(tok_rows, pos_ref, out_ref, weight_ref, tok_ref, sum_ref, cnt_ref):
    step = pl.program_id(0)
    size = out_ref.shape[0]
    lines = size // LANES
    base = pos_ref[0] * tok_rows
    token = lax.broadcasted_iota(jnp.int32, (tok_rows, LANES), 0)
    weight_half = (weight_ref[...].astype(F32) * 0.5).astype(BF16)
    hidden = activate(out_ref[...], weight_half)
    ones = []
    for j in range(lines):
        ids = tok_ref[pl.ds(step * lines + j, 1), :] - base
        ones.append(jnp.where(token == ids, 1.0, 0.0))
    hot = jnp.concatenate(ones, axis=1).astype(BF16)
    count = functools.reduce(jnp.add, ones)
    more = dot(hot, hidden)

    @pl.when(step == 0)
    def _():
        sum_ref[...] = more
        cnt_ref[...] = count

    @pl.when(step > 0)
    def _():
        sum_ref[...] += more
        cnt_ref[...] += count


def pool(pos, atom_out, weight, tok2d, tok_rows, part):
    rows, width = atom_out.shape
    feats = weight.shape[1] // PARTS
    size = min(1024, rows)
    return pl.pallas_call(
        functools.partial(pool_kernel, tok_rows),
        grid_spec=pltpu.PrefetchScalarGridSpec(
            num_scalar_prefetch=1,
            grid=(rows // size,),
            in_specs=[
                pl.BlockSpec((size, width), lambda i, *_: (i, 0)),
                pl.BlockSpec((width, feats), lambda i, *_: (0, part)),
                full(tok2d.shape),
            ],
            out_specs=[full((tok_rows, feats)), full((tok_rows, LANES))],
        ),
        out_shape=[
            jax.ShapeDtypeStruct((tok_rows, feats), F32),
            jax.ShapeDtypeStruct((tok_rows, LANES), F32),
        ],
        compiler_params=params(VMEM_SMALL),
        cost_estimate=pl.CostEstimate(flops=2 * 10**9, bytes_accessed=2 * 10**6, transcendentals=10**6),
        name="pool",
    )(pos, atom_out, weight, tok2d)


def finish_kernel(msg_ref, weight_ref, sum_ref, cnt_ref, repr_ref):
    tok_rows = sum_ref.shape[0]
    size = msg_ref.shape[0] - 16
    lines = size // LANES
    token = lax.broadcasted_iota(jnp.int32, (tok_rows, LANES), 0).astype(F32)
    weight_half = (weight_ref[...].astype(F32) * 0.5).astype(BF16)
    hidden = activate(msg_ref[:size, :], weight_half)
    codes = msg_ref[size:, :].astype(F32)
    ids = codes[:8] * 16.0 + codes[8:] - 1.0
    ones = [jnp.where(token == ids[8 - lines + j : 9 - lines + j], 1.0, 0.0) for j in range(lines)]
    hot = jnp.concatenate(ones, axis=1).astype(BF16)
    count = functools.reduce(jnp.add, ones) + cnt_ref[...]
    sums = sum_ref[...] + dot(hot, hidden)
    repr_ref[...] = (sums / jnp.sum(count, axis=1, keepdims=True)).astype(BF16)


def finish(msg, weight, sums, counts, part):
    rows, feats = sums.shape
    return pl.pallas_call(
        finish_kernel,
        grid=(1,),
        in_specs=[
            full(msg.shape),
            pl.BlockSpec((weight.shape[0], feats), lambda i: (0, part)),
            full(sums.shape),
            full(counts.shape),
        ],
        out_specs=full((rows, feats)),
        out_shape=jax.ShapeDtypeStruct((rows, feats), BF16),
        compiler_params=params(VMEM_SMALL),
        cost_estimate=pl.CostEstimate(flops=2 * 10**8, bytes_accessed=2 * 10**6, transcendentals=2 * 10**5),
        name="token_finish",
    )(msg, weight, sums, counts)


def query_kernel(scale, a_ref, b_ref, gain_ref, weight_hbm, out_ref, weight_s, sem):
    copy = pltpu.make_async_copy(weight_hbm, weight_s, sem)
    copy.start()
    rows = jnp.concatenate([a_ref[...].astype(F32), b_ref[...].astype(F32)], axis=1)
    normed = norm_rows(rows, gain_ref[...].reshape(1, -1)).astype(BF16)
    copy.wait()
    out_ref[...] = (dot(normed, weight_s[...]) * scale).astype(BF16)


def project_queries(halves, gain, weight):
    rows = halves[0].shape[0]
    return pl.pallas_call(
        functools.partial(query_kernel, 1.0 / math.sqrt(weight.shape[1] // TH)),
        in_specs=[pl.BlockSpec(memory_space=pltpu.VMEM)] * 3 + [pl.BlockSpec(memory_space=pl.ANY)],
        out_shape=jax.ShapeDtypeStruct((rows, weight.shape[1]), BF16),
        scratch_shapes=[pltpu.VMEM(weight.shape, BF16), pltpu.SemaphoreType.DMA],
        compiler_params=params(VMEM_SMALL),
        cost_estimate=pl.CostEstimate(flops=5 * 10**8, bytes_accessed=3 * 10**6, transcendentals=0),
        name="queries",
    )(*halves, gain, weight)


GROUPS = 2
ROW_TILE = 32


def pack_message(mixed, lse, heads):
    lane = lax.broadcasted_iota(jnp.int32, lse.shape, 1)
    high = lse.astype(BF16).astype(F32)
    rest = lse - high
    middle = rest.astype(BF16).astype(F32)
    low = rest - middle
    first = jnp.where(lane < heads, high, pltpu.roll(middle, heads, 1))
    second = jnp.where(lane < heads, low, 0.0)
    turned = jnp.concatenate([first, second], axis=0).T
    return jnp.concatenate([mixed.astype(BF16), turned[: 2 * heads].astype(BF16)], axis=0)


def unpack_message(msg, rows, heads):
    coded = msg[rows:].astype(F32)
    coded = jnp.concatenate([coded, jnp.zeros((LANES - 2 * heads, coded.shape[1]), F32)], axis=0).T
    first = coded[:rows]
    return msg[:rows].astype(F32), first + pltpu.roll(first, LANES - heads, 1) + coded[rows:]


def merge_parts(mixed, lse, other, lse_b, heads):
    rows, feats = mixed.shape
    width = feats // heads
    spot = lax.broadcasted_iota(jnp.int32, (rows, LANES), 1)
    lse_b = jnp.where(spot < heads, lse_b, lse)
    top = jnp.maximum(lse, lse_b)
    part = jnp.exp(lse - top)
    total = part + jnp.exp(lse_b - top)
    share = part / total
    high = share.astype(BF16)
    low = (share - high.astype(F32)).astype(BF16)
    head = lax.broadcasted_iota(jnp.int32, (LANES, feats), 0) * width
    column = lax.broadcasted_iota(jnp.int32, (LANES, feats), 1)
    spread = jnp.where((column >= head) & (column < head + width), 1.0, 0.0).astype(BF16)
    wide = dot(high, spread) + dot(low, spread)
    return other + wide * (mixed - other), top + jnp.log(total)


def attend_group(group, heads, width, half, q_ref, k_ref, v_ref, bias_ref, scratch):
    score_s, term_s, top_s, mix_s = scratch
    rows = mix_s.shape[0]
    at = pl.multiple_of(half * rows, rows)
    pairs = heads // 2
    spot = lax.broadcasted_iota(jnp.int32, (rows, LANES), 1)

    def layout(p):
        first = 2 * p * width
        low = first // LANES * LANES
        wide = -(-(first + 2 * width) // LANES) * LANES - low
        lane = lax.broadcasted_iota(jnp.int32, (rows, wide), 1)
        first -= low
        masks = [(lane >= first + j * width) & (lane < first + (j + 1) * width) for j in range(2)]
        return slice(low, low + wide), first, masks

    keys = score_s[0].shape[1]
    chunk = min(256, keys)
    chunks = keys // chunk
    tiles = 2 * rows // ROW_TILE

    def stack(p):
        window, _, masks = layout(p)
        query = q_ref[pl.ds(at, rows), window].astype(F32)
        return jnp.concatenate([jnp.where(m, query, 0.0).astype(BF16) for m in masks], axis=0)

    def score(p, n, stacked):
        part = slice(n * chunk, (n + 1) * chunk)
        score_s[p % 2][:, part] = dot(stacked, k_ref[layout(p)[0], part])

    def soften(p, n):
        for r in range(n * tiles // chunks * ROW_TILE, (n + 1) * tiles // chunks * ROW_TILE, ROW_TILE):
            bias = bias_ref[group * heads + 2 * p + r // rows, r % rows : r % rows + ROW_TILE, :].astype(F32)
            scores = score_s[p % 2][r : r + ROW_TILE, :] + bias
            top = jnp.max(scores, axis=-1, keepdims=True)
            term_s[p % 2][r : r + ROW_TILE, :] = jnp.exp(scores - top).astype(BF16)
            top_s[p % 2][r : r + ROW_TILE, :] = jnp.broadcast_to(top, (ROW_TILE, LANES))

    def mix(p, n, mixed):
        part = slice(n * chunk, (n + 1) * chunk)
        window, first, _ = layout(p)
        values = v_ref[part, window]
        column = lax.broadcasted_iota(jnp.int32, values.shape, 1)
        used = (column >= first) & (column < first + 2 * width)
        more = dot(term_s[p % 2][:, part], jnp.where(used, values.astype(F32), 1.0).astype(BF16))
        return more if mixed is None else mixed + more

    def close(p, mixed, lse):
        window, first, masks = layout(p)
        free = 0 if first >= 16 else 2 * width
        total = mixed[:, free : free + 1]
        mixed = mixed / total
        sums = top_s[p % 2][...] + jnp.log(total)
        result = mix_s[:, window]
        for j in range(2):
            result = jnp.where(masks[j], mixed[j * rows : (j + 1) * rows], result)
            lse = jnp.where(spot == 2 * p + j, sums[j * rows : (j + 1) * rows], lse)
        mix_s[:, window] = result
        return lse

    lse = jnp.zeros((rows, LANES), F32)
    stacked = stack(0)
    for n in range(chunks):
        score(0, n, stacked)
    for p in range(pairs):
        mixed = None
        if p + 1 < pairs:
            stacked = stack(p + 1)
        for n in range(chunks):
            if p + 1 < pairs:
                score(p + 1, n, stacked)
            if p:
                mixed = mix(p - 1, n, mixed)
            soften(p, n)
        if p:
            lse = close(p - 1, mixed, lse)
    mixed = None
    for n in range(chunks):
        mixed = mix(pairs - 1, n, mixed)
    lse = close(pairs - 1, mixed, lse)
    return mix_s[...], lse


def group_scratch(rows, keys, feats, heads):
    return [
        pltpu.VMEM((2 * rows, keys), F32),
        pltpu.VMEM((2 * rows, keys), F32),
        pltpu.VMEM((2 * rows, keys), BF16),
        pltpu.VMEM((2 * rows, keys), BF16),
        pltpu.VMEM((2 * rows, LANES), F32),
        pltpu.VMEM((2 * rows, LANES), F32),
        pltpu.VMEM((rows, feats), F32),
        pltpu.VMEM((2, 2 * feats, feats), BF16),
        pltpu.SemaphoreType.DMA((2,)),
    ]


def scratch_of(refs):
    return refs[:2], refs[2:4], refs[4:6], refs[6]


def weight_copies(group, weight_hbm, refs):
    weight_s, sems = refs[7:9]
    feats = weight_s.shape[2]
    return [
        pltpu.make_async_copy(
            weight_hbm.at[:, pl.ds((part * GROUPS + group) * feats, feats)], weight_s.at[part], sems.at[part]
        )
        for part in range(2)
    ]


def project_keys(x_ref, weight_s, copies, k_ref, v_ref):
    tile = x_ref.shape[0] // 2
    copies[0].wait()
    for r in range(0, x_ref.shape[0], tile):
        k_ref[:, r : r + tile] = dot(x_ref[r : r + tile, :], weight_s[0]).T.astype(BF16)
    copies[1].wait()
    for r in range(0, x_ref.shape[0], tile):
        v_ref[r : r + tile, :] = dot(x_ref[r : r + tile, :], weight_s[1]).astype(BF16)


def first_kernel(heads, width, half_ref, core_ref, q_ref, own_a, own_b, other_a, other_b, gain_ref, weight_hbm,
                 bias_ref, x_ref, k_ref, v_ref, msg_ref, *refs):
    scratch = scratch_of(refs)
    weights = weight_copies(0, weight_hbm, refs)
    for copy in weights:
        copy.start()
    rows = own_a.shape[0]
    core = core_ref[0]
    gain = gain_ref[...].reshape(1, -1)
    for place, parts in ((core, (own_a, own_b)), (1 - core, (other_a, other_b))):
        values = jnp.concatenate([part[...].astype(F32) for part in parts], axis=1)
        x_ref[pl.ds(pl.multiple_of(place * rows, rows), rows), :] = norm_rows(values, gain).astype(BF16)
    project_keys(x_ref, refs[7], weights, k_ref, v_ref)
    mixed, lse = attend_group(0, heads, width, half_ref[0], q_ref, k_ref, v_ref, bias_ref, scratch)
    msg_ref[...] = pack_message(mixed, lse, heads)


def next_kernel(group, heads, width, half_ref, q_ref, x_ref, weight_hbm, bias_ref, k_ref, v_ref, msg_ref, *refs):
    scratch = scratch_of(refs)
    weights = weight_copies(group, weight_hbm, refs)
    for copy in weights:
        copy.start()
    project_keys(x_ref, refs[7], weights, k_ref, v_ref)
    mixed, lse = attend_group(group, heads, width, half_ref[0], q_ref, k_ref, v_ref, bias_ref, scratch)
    msg_ref[...] = pack_message(mixed, lse, heads)


def keep_kernel(group, heads, width, half_ref, q_ref, k_ref, v_ref, near_ref, bias_ref, o_ref, lse_ref, msg_ref, *refs):
    scratch = scratch_of(refs)
    mixed, lse = attend_group(group, heads, width, half_ref[0], q_ref, k_ref, v_ref, bias_ref, scratch)
    rows = mixed.shape[0]
    mixed, lse = merge_parts(mixed, lse, *unpack_message(near_ref[...], rows, heads), heads)
    o_ref[...] = mixed
    lse_ref[...] = lse
    msg_ref[...] = pack_message(mixed, lse, heads)


def group_call(kernel, group, half, scalars, q, arrays, weights, bias, outs, name):
    tok_rows, all_feats = q.shape
    rows, keys, feats = tok_rows // 2, bias.shape[2], all_feats // GROUPS
    heads = TH // GROUPS
    shapes = {
        "x": ((keys, all_feats), BF16),
        "k": ((feats, keys), BF16),
        "v": ((keys, feats), BF16),
        "o": ((rows, feats), F32),
        "lse": ((rows, LANES), F32),
        "msg": ((rows + 2 * heads, feats), BF16),
    }
    return pl.pallas_call(
        functools.partial(kernel, heads, feats // heads),
        grid_spec=pltpu.PrefetchScalarGridSpec(
            num_scalar_prefetch=1 + len(scalars),
            grid=(1,),
            in_specs=[pl.BlockSpec((tok_rows, feats), lambda i, *_: (0, group))]
            + [full(array.shape) for array in arrays]
            + [pl.BlockSpec(memory_space=pl.ANY)] * (0 if weights is None else 1)
            + [pl.BlockSpec(memory_space=pltpu.VMEM)],
            out_specs=[full(shapes[out][0]) for out in outs],
            scratch_shapes=group_scratch(rows, keys, feats, heads),
        ),
        out_shape=[jax.ShapeDtypeStruct(*shapes[out]) for out in outs],
        compiler_params=params(VMEM_SMALL),
        cost_estimate=pl.CostEstimate(flops=4 * 10**9, bytes_accessed=4 * 10**6, transcendentals=10**6),
        name=name,
    )(half, *scalars, q, *arrays, *([] if weights is None else [weights]), bias)


def merge_kernel(heads, o_ref, lse_ref, msg_ref, out_ref, sum_ref, back_ref):
    rows = o_ref.shape[0]
    mixed, lse = merge_parts(o_ref[...], lse_ref[...], *unpack_message(msg_ref[...], rows, heads), heads)
    out_ref[...] = mixed
    sum_ref[...] = lse
    back_ref[...] = pack_message(mixed, lse, heads)


def merge(o, lse, msg):
    return pl.pallas_call(
        functools.partial(merge_kernel, TH // GROUPS),
        out_shape=[jax.ShapeDtypeStruct(a.shape, a.dtype) for a in (o, lse, msg)],
        compiler_params=params(VMEM_SMALL),
        name="merge",
    )(o, lse, msg)


def settle_kernel(heads, o_ref, lse_ref, msg_ref, out_ref):
    rows = o_ref.shape[0]
    mixed, _ = merge_parts(o_ref[...], lse_ref[...], *unpack_message(msg_ref[...], rows, heads), heads)
    out_ref[...] = mixed.astype(BF16)


def settle(o, lse, msg):
    return pl.pallas_call(
        functools.partial(settle_kernel, TH // GROUPS),
        out_shape=jax.ShapeDtypeStruct(o.shape, BF16),
        compiler_params=params(VMEM_SMALL),
        name="settle",
    )(o, lse, msg)


def output_kernel(half_ref, own_a, own_b, other_a, other_b, a_ref, b_ref, weight_ref, out_ref):
    rows, feats = own_a.shape
    for place, first, second in ((half_ref[0], own_a, own_b), (1 - half_ref[0], other_a, other_b)):
        mine = pl.ds(pl.multiple_of(place * rows, rows), rows)
        result = dot(first[...], weight_ref[:feats, :]) + dot(second[...], weight_ref[feats:, :])
        out_ref[mine, :feats] = (a_ref[mine, :].astype(F32) + result[:, :feats]).astype(BF16)
        out_ref[mine, feats:] = (b_ref[mine, :].astype(F32) + result[:, feats:]).astype(BF16)


def output_rows(half, own, other, token_repr, weight):
    rows = token_repr[0].shape[0]
    return pl.pallas_call(
        output_kernel,
        in_specs=[pl.BlockSpec(memory_space=pltpu.SMEM)] + [pl.BlockSpec(memory_space=pltpu.VMEM)] * 7,
        out_shape=jax.ShapeDtypeStruct((rows, weight.shape[1]), BF16),
        compiler_params=params(VMEM_SMALL),
        name="output_rows",
    )(half, *own, *other, *token_repr, weight)


def bits_of(count):
    return [1 << b for b in range(count.bit_length() - 1)]


def key_parts(halves):
    n_pb, n_ka = lax.axis_size("pb"), lax.axis_size("ka")
    cores = n_pb // n_ka
    chips = n_pb // cores
    shard, plane = lax.axis_index("pb"), lax.axis_index("ka")
    bits = bits_of(chips)
    core = lax.rem(shard, cores)
    away = jnp.bitwise_xor(shard // cores, plane)
    held = list(halves)
    for r in range(len(bits)):
        pairs = []
        gets = jnp.bool_(False)
        for c in range(cores):
            order = bits if c % 2 == 0 else bits[::-1]
            known = sum(order[:r])
            for k in range(n_ka):
                for j in range(chips):
                    if (j ^ k) & ~known == 0:
                        pairs.append(((j * cores + c) * n_ka + k, ((j ^ order[r]) * cores + c) * n_ka + k))
            fresh = (jnp.bitwise_and(away, ~(known + order[r])) == 0) & (jnp.bitwise_and(away, order[r]) != 0)
            gets = gets | (fresh & (core == c))
        held = [jnp.where(gets, lax.ppermute(part, ("pb", "ka"), pairs), part) for part in held]
    return held


def body(
    atoms,
    atom_gain,
    atom_qkv,
    atom_proj,
    atom_bias,
    window_shift,
    token_of_atom,
    agg_weight,
    token_gain,
    token_q,
    token_kv,
    token_o,
    pair_bias,
):
    n_pb, n_ka = lax.axis_size("pb"), lax.axis_size("ka")
    shard, plane = lax.axis_index("pb"), lax.axis_index("ka")
    rows, width = atoms.shape
    tok_rows = pair_bias.shape[1]
    half = WIN_K // 2
    up = [(i, i + 1) for i in range(n_pb - 1)]
    down = [(i + 1, i) for i in range(n_pb - 1)]
    pos = shard.astype(jnp.int32).reshape(1)
    tok2d = token_of_atom.reshape(rows // LANES, LANES)
    left = lax.ppermute(atoms[rows - half :], "pb", up)
    right = lax.ppermute(atoms[:half], "pb", down)
    atom_out, msg = atom_attention(
        window_shift, pos, atoms, left, right, atom_gain, atom_qkv, atom_proj,
        atom_bias, tok2d, tok_rows, rows * n_pb,
    )
    behind = lax.ppermute(msg, "pb", up)
    token_repr = []
    for part in range(PARTS):
        sums, counts = pool(pos, atom_out, agg_weight, tok2d, tok_rows, part)
        token_repr.append(finish(behind, agg_weight, sums, counts, part))
    parity = jnp.bitwise_and(plane ^ (plane >> 1), 1).astype(jnp.int32)
    core = lax.rem(shard, n_pb // n_ka).astype(jnp.int32)
    keep, send = parity.reshape(1), (1 - parity).reshape(1)
    share = tok_rows // 2
    queries = project_queries(token_repr, token_gain, token_q)
    own_keys = key_parts(token_repr)
    own_keys[0], queries = lax.optimization_barrier((own_keys[0], queries))
    other_keys = [lax.ppermute(part, "pb", [(p, p ^ 1) for p in range(n_pb)]) for part in own_keys]
    bias, *own_keys = lax.optimization_barrier((pair_bias, *own_keys))
    send_bias = lax.dynamic_slice_in_dim(bias, (1 - parity) * share, share, axis=1)
    swap = [(i, i ^ 1) for i in range(n_ka)]
    bits = bits_of(n_ka)[1:]

    def far(msg, bit):
        return lax.ppermute(msg, "ka", [(i, i ^ (2 * bit - 1)) for i in range(n_ka)])

    x, k, v, msg = group_call(
        first_kernel, 0, send, (core.reshape(1),), queries, (*own_keys, *other_keys, token_gain), token_kv,
        send_bias, ("x", "k", "v", "msg"), "attend_first",
    )
    held, near = [(k, v)], [lax.ppermute(msg, "ka", swap)]
    bias, x = lax.optimization_barrier((bias, x))
    keep_bias = lax.dynamic_slice_in_dim(bias, parity * share, share, axis=1)
    for g in range(1, GROUPS):
        k, v, msg = group_call(
            functools.partial(next_kernel, g), g, send, (), queries, (x,), token_kv,
            send_bias, ("k", "v", "msg"), "attend_next",
        )
        held.append((k, v))
        near.append(lax.ppermute(msg, "ka", swap))
    sums, gone = [], []
    for g in range(GROUPS):
        o, lse, msg = group_call(
            functools.partial(keep_kernel, g), g, keep, (), queries, (*held[g], near[g]), None,
            keep_bias, ("o", "lse", "msg"), "attend_keep",
        )
        sums.append((o, lse))
        gone.append(far(msg, bits[0]))
    own_mix, other_mix = [], []
    for g in range(GROUPS):
        (o, lse), got = sums[g], gone[g]
        for bit in bits[1:]:
            o, lse, msg = merge(o, lse, got)
            got = far(msg, bit)
        own_mix.append(settle(o, lse, got))
        other_mix.append(lax.ppermute(own_mix[g], "ka", swap))
    return atom_out, output_rows(keep, own_mix, other_mix, token_repr, token_o)


def solution(mesh):
    return jax.shard_map(
        body,
        mesh=mesh,
        in_specs=(
            P("pb", None),
            P(),
            P(),
            P(),
            P(None, "pb", None),
            P("pb"),
            P("pb"),
            P(),
            P(),
            P(),
            P(),
            P(),
            P(None, "pb", "ka"),
        ),
        out_specs=(P("pb", None), P("pb", None)),
        check_vma=False,
    )
```

```python
import functools
import math

import jax
import jax.numpy as jnp
from jax import lax
from jax.experimental import pallas as pl
from jax.experimental.pallas import tpu as pltpu
from jax.sharding import PartitionSpec as P

AH = 4
TH = 16
WIN_Q = 32
WIN_K = 128
SHIFT_MAX = 384
PARTS = 2
LANES = 128
F32 = jnp.float32
BF16 = jnp.bfloat16
VMEM_LIMIT = 56 * 1024 * 1024
VMEM_SMALL = 24 * 1024 * 1024


def full(shape):
    return pl.BlockSpec(shape, lambda *_: (0,) * len(shape))


def params(limit=VMEM_LIMIT):
    return pltpu.CompilerParams(vmem_limit_bytes=limit)


def norm_rows(as_float, gain):
    centre = jnp.mean(as_float, axis=-1, keepdims=True)
    spread = jnp.mean(jnp.square(as_float - centre), axis=-1, keepdims=True)
    return (as_float - centre) * lax.rsqrt(spread + 1e-05) * gain


def dot(a, b):
    return jnp.dot(a, b, preferred_element_type=F32)


def atom_kernel(
    chunks,
    atom_total,
    tok_rows,
    shift_ref,
    pos_ref,
    atoms_ref,
    left_ref,
    right_ref,
    gain_ref,
    qkv_ref,
    proj_ref,
    bias_ref,
    tok_ref,
    out_ref,
    msg_ref,
    q_s,
    k_s,
    v_s,
    x_s,
):
    step = pl.program_id(0)
    rows, width = atoms_ref.shape
    size = out_ref.shape[0]
    half = WIN_K // 2
    head = width // AH
    shard = pos_ref[0]

    @pl.when(step == 0)
    def _():
        gain = gain_ref[...].reshape(1, width)
        x_s[:half, :] = left_ref[...]
        x_s[half : half + rows, :] = atoms_ref[...]
        x_s[half + rows :, :] = right_ref[...]
        total = rows + 2 * half
        tile = 5 * WIN_K if total % (5 * WIN_K) == 0 else WIN_K

        def one(c, carry):
            at = pl.ds(pl.multiple_of(c * tile, tile), tile)
            normed = norm_rows(x_s[at, :].astype(F32), gain).astype(BF16)
            res = dot(normed, qkv_ref[...])
            q_s[at, :] = (res[:, :width] * (1.0 / math.sqrt(head))).astype(BF16)
            k_s[:, at] = res[:, width : 2 * width].T.astype(BF16)
            v_s[at, :width] = res[:, 2 * width :].astype(BF16)
            v_s[at, width:] = jnp.ones((tile, width), BF16)
            return carry

        lax.fori_loop(0, total // tile, one, 0, unroll=True)

    group = WIN_K // WIN_Q
    atoms_group = group * WIN_Q
    span = AH * WIN_Q
    lane_q = lax.broadcasted_iota(jnp.int32, (WIN_Q, width), 1)
    heads = [(lane_q >= h * head) & (lane_q < (h + 1) * head) for h in range(AH)]
    lane = lax.broadcasted_iota(jnp.int32, (span, WIN_K), 1)
    slot = lax.broadcasted_iota(jnp.int32, (1, WIN_K), 1)
    blocks = size // WIN_Q

    def region(n):
        return pl.ds(pl.multiple_of(step * size + n // group * atoms_group, atoms_group), 2 * WIN_K)

    def score(g):
        query = q_s[pl.ds(pl.multiple_of(step * size + g * atoms_group + half, half), atoms_group), :].astype(F32)
        stacked = [
            jnp.where(m, query[i * WIN_Q : (i + 1) * WIN_Q], 0.0).astype(BF16) for i in range(group) for m in heads
        ]
        return dot(jnp.concatenate(stacked, axis=0), k_s[:, region(g * group)])

    def soften(n, scores):
        offset = n % group * WIN_Q + half + shift_ref[step * blocks + n]
        early = lane >= offset
        begin = n * WIN_Q
        bias = bias_ref[:, begin : begin + WIN_Q, :].astype(F32).reshape(span, WIN_K)
        index = slot + jnp.where(slot >= offset, 0, WIN_K)
        index = index + (step * size + n // group * atoms_group + shard * rows - half)
        shut = jnp.where((index >= 0) & (index < atom_total), 0.0, -jnp.inf)
        logits = jnp.where(early, scores[:, :WIN_K], scores[:, WIN_K:]) + (
            pltpu.roll(bias, jnp.bitwise_and(offset, WIN_K - 1), 1) + shut
        )
        terms = jnp.exp(logits - jnp.max(logits, axis=-1, keepdims=True))
        return jnp.concatenate(
            [jnp.where(early, terms, 0.0).astype(BF16), jnp.where(early, 0.0, terms).astype(BF16)], axis=1
        )

    def mix(g, weights):
        mixed = dot(jnp.concatenate(weights, axis=0), v_s[region(g * group), :])
        merged = []
        for i in range(group):
            parts = [mixed[(i * AH + h) * WIN_Q : (i * AH + h + 1) * WIN_Q] for h in range(AH)]
            values, total = parts[0][:, :width], parts[0][:, width:]
            for h in range(1, AH):
                values = jnp.where(heads[h], parts[h][:, :width], values)
                total = jnp.where(heads[h], parts[h][:, width:], total)
            merged.append((values / total).astype(BF16))
        local = g * atoms_group
        at = pl.multiple_of(step * size + local, atoms_group)
        own = atoms_ref[pl.ds(at, atoms_group), :].astype(F32)
        result = own + dot(jnp.concatenate(merged, axis=0), proj_ref[...])
        out_ref[local : local + atoms_group, :] = result.astype(BF16)

    groups = blocks // group
    ahead = score(0)
    behind = None
    for g in range(groups):
        scores = ahead
        if g + 1 < groups:
            ahead = score(g + 1)
        if g:
            mix(g - 1, behind)
        behind = [soften(g * group + i, scores[i * span : (i + 1) * span]) for i in range(group)]
    mix(groups - 1, behind)

    @pl.when(step == chunks - 1)
    def _():
        ids = tok_ref[tok_ref.shape[0] - 8 :, :]
        code = jnp.maximum(ids - (shard + 1) * tok_rows + 1, 0)
        high = (code >> 4).astype(F32)
        low = (code & 15).astype(F32)
        msg_ref[:SHIFT_MAX, :] = out_ref[size - SHIFT_MAX :, :]
        msg_ref[SHIFT_MAX:, :] = jnp.concatenate([high, low], axis=0).astype(BF16)


def atom_attention(shift, pos, atoms, left, right, gain, qkv, proj, bias, tok2d, tok_rows, atom_total):
    rows, width = atoms.shape
    size = 2 * SHIFT_MAX
    chunks = rows // size
    half = WIN_K // 2
    return pl.pallas_call(
        functools.partial(atom_kernel, chunks, atom_total, tok_rows),
        grid_spec=pltpu.PrefetchScalarGridSpec(
            num_scalar_prefetch=2,
            grid=(chunks,),
            in_specs=[
                full((rows, width)),
                full((half, width)),
                full((half, width)),
                full((width,)),
                full(qkv.shape),
                full(proj.shape),
                pl.BlockSpec((AH, size, WIN_K), lambda i, *_: (0, i, 0)),
                full(tok2d.shape),
            ],
            out_specs=[
                pl.BlockSpec((size, width), lambda i, *_: (i, 0)),
                full((SHIFT_MAX + 16, width)),
            ],
            scratch_shapes=[
                pltpu.VMEM((rows + 2 * half, width), BF16),
                pltpu.VMEM((width, rows + 2 * half), BF16),
                pltpu.VMEM((rows + 2 * half, 2 * width), BF16),
                pltpu.VMEM((rows + 2 * half, width), BF16),
            ],
        ),
        out_shape=[
            jax.ShapeDtypeStruct((rows, width), BF16),
            jax.ShapeDtypeStruct((SHIFT_MAX + 16, width), BF16),
        ],
        compiler_params=params(),
        cost_estimate=pl.CostEstimate(flops=8 * 10**9, bytes_accessed=6 * 10**6, transcendentals=2 * 10**6),
        name="atom_attention",
    )(shift, pos, atoms, left, right, gain, qkv, proj, bias, tok2d)


def activate(rows, weight_half):
    u = dot(rows, weight_half)
    return (u + u * jnp.tanh(u)).astype(BF16)


def pool_kernel(tok_rows, pos_ref, out_ref, weight_ref, tok_ref, sum_ref, cnt_ref):
    step = pl.program_id(0)
    size = out_ref.shape[0]
    lines = size // LANES
    base = pos_ref[0] * tok_rows
    token = lax.broadcasted_iota(jnp.int32, (tok_rows, LANES), 0)
    weight_half = (weight_ref[...].astype(F32) * 0.5).astype(BF16)
    hidden = activate(out_ref[...], weight_half)
    ones = []
    for j in range(lines):
        ids = tok_ref[pl.ds(step * lines + j, 1), :] - base
        ones.append(jnp.where(token == ids, 1.0, 0.0))
    hot = jnp.concatenate(ones, axis=1).astype(BF16)
    count = functools.reduce(jnp.add, ones)
    more = dot(hot, hidden)

    @pl.when(step == 0)
    def _():
        sum_ref[...] = more
        cnt_ref[...] = count

    @pl.when(step > 0)
    def _():
        sum_ref[...] += more
        cnt_ref[...] += count


def pool(pos, atom_out, weight, tok2d, tok_rows, part):
    rows, width = atom_out.shape
    feats = weight.shape[1] // PARTS
    size = min(1024, rows)
    return pl.pallas_call(
        functools.partial(pool_kernel, tok_rows),
        grid_spec=pltpu.PrefetchScalarGridSpec(
            num_scalar_prefetch=1,
            grid=(rows // size,),
            in_specs=[
                pl.BlockSpec((size, width), lambda i, *_: (i, 0)),
                pl.BlockSpec((width, feats), lambda i, *_: (0, part)),
                full(tok2d.shape),
            ],
            out_specs=[full((tok_rows, feats)), full((tok_rows, LANES))],
        ),
        out_shape=[
            jax.ShapeDtypeStruct((tok_rows, feats), F32),
            jax.ShapeDtypeStruct((tok_rows, LANES), F32),
        ],
        compiler_params=params(VMEM_SMALL),
        cost_estimate=pl.CostEstimate(flops=2 * 10**9, bytes_accessed=2 * 10**6, transcendentals=10**6),
        name="pool",
    )(pos, atom_out, weight, tok2d)


def finish_kernel(msg_ref, weight_ref, sum_ref, cnt_ref, repr_ref):
    tok_rows = sum_ref.shape[0]
    size = msg_ref.shape[0] - 16
    lines = size // LANES
    token = lax.broadcasted_iota(jnp.int32, (tok_rows, LANES), 0).astype(F32)
    weight_half = (weight_ref[...].astype(F32) * 0.5).astype(BF16)
    hidden = activate(msg_ref[:size, :], weight_half)
    codes = msg_ref[size:, :].astype(F32)
    ids = codes[:8] * 16.0 + codes[8:] - 1.0
    ones = [jnp.where(token == ids[8 - lines + j : 9 - lines + j], 1.0, 0.0) for j in range(lines)]
    hot = jnp.concatenate(ones, axis=1).astype(BF16)
    count = functools.reduce(jnp.add, ones) + cnt_ref[...]
    sums = sum_ref[...] + dot(hot, hidden)
    repr_ref[...] = (sums / jnp.sum(count, axis=1, keepdims=True)).astype(BF16)


def finish(msg, weight, sums, counts, part):
    rows, feats = sums.shape
    return pl.pallas_call(
        finish_kernel,
        grid=(1,),
        in_specs=[
            full(msg.shape),
            pl.BlockSpec((weight.shape[0], feats), lambda i: (0, part)),
            full(sums.shape),
            full(counts.shape),
        ],
        out_specs=full((rows, feats)),
        out_shape=jax.ShapeDtypeStruct((rows, feats), BF16),
        compiler_params=params(VMEM_SMALL),
        cost_estimate=pl.CostEstimate(flops=2 * 10**8, bytes_accessed=2 * 10**6, transcendentals=2 * 10**5),
        name="token_finish",
    )(msg, weight, sums, counts)


def query_kernel(scale, a_ref, b_ref, gain_ref, weight_hbm, out_ref, weight_s, sem):
    copy = pltpu.make_async_copy(weight_hbm, weight_s, sem)
    copy.start()
    rows = jnp.concatenate([a_ref[...].astype(F32), b_ref[...].astype(F32)], axis=1)
    normed = norm_rows(rows, gain_ref[...].reshape(1, -1)).astype(BF16)
    copy.wait()
    out_ref[...] = (dot(normed, weight_s[...]) * scale).astype(BF16)


def project_queries(halves, gain, weight):
    rows = halves[0].shape[0]
    return pl.pallas_call(
        functools.partial(query_kernel, 1.0 / math.sqrt(weight.shape[1] // TH)),
        in_specs=[pl.BlockSpec(memory_space=pltpu.VMEM)] * 3 + [pl.BlockSpec(memory_space=pl.ANY)],
        out_shape=jax.ShapeDtypeStruct((rows, weight.shape[1]), BF16),
        scratch_shapes=[pltpu.VMEM(weight.shape, BF16), pltpu.SemaphoreType.DMA],
        compiler_params=params(VMEM_SMALL),
        cost_estimate=pl.CostEstimate(flops=5 * 10**8, bytes_accessed=3 * 10**6, transcendentals=0),
        name="queries",
    )(*halves, gain, weight)


GROUPS = 2
ROW_TILE = 32


def pack_message(mixed, lse, heads):
    lane = lax.broadcasted_iota(jnp.int32, lse.shape, 1)
    high = lse.astype(BF16).astype(F32)
    rest = lse - high
    middle = rest.astype(BF16).astype(F32)
    low = rest - middle
    first = jnp.where(lane < heads, high, pltpu.roll(middle, heads, 1))
    second = jnp.where(lane < heads, low, 0.0)
    turned = jnp.concatenate([first, second], axis=0).T
    return jnp.concatenate([mixed.astype(BF16), turned[: 2 * heads].astype(BF16)], axis=0)


def unpack_message(msg, rows, heads):
    coded = msg[rows:].astype(F32)
    coded = jnp.concatenate([coded, jnp.zeros((LANES - 2 * heads, coded.shape[1]), F32)], axis=0).T
    first = coded[:rows]
    return msg[:rows].astype(F32), first + pltpu.roll(first, LANES - heads, 1) + coded[rows:]


def merge_parts(mixed, lse, other, lse_b, heads):
    rows, feats = mixed.shape
    width = feats // heads
    spot = lax.broadcasted_iota(jnp.int32, (rows, LANES), 1)
    lse_b = jnp.where(spot < heads, lse_b, lse)
    top = jnp.maximum(lse, lse_b)
    part = jnp.exp(lse - top)
    total = part + jnp.exp(lse_b - top)
    share = part / total
    high = share.astype(BF16)
    low = (share - high.astype(F32)).astype(BF16)
    head = lax.broadcasted_iota(jnp.int32, (LANES, feats), 0) * width
    column = lax.broadcasted_iota(jnp.int32, (LANES, feats), 1)
    spread = jnp.where((column >= head) & (column < head + width), 1.0, 0.0).astype(BF16)
    wide = dot(high, spread) + dot(low, spread)
    return other + wide * (mixed - other), top + jnp.log(total)


def attend_group(group, heads, width, half, q_ref, k_ref, v_ref, bias_ref, scratch):
    score_s, term_s, top_s, mix_s = scratch
    rows = mix_s.shape[0]
    at = pl.multiple_of(half * rows, rows)
    pairs = heads // 2
    spot = lax.broadcasted_iota(jnp.int32, (rows, LANES), 1)

    def layout(p):
        first = 2 * p * width
        low = first // LANES * LANES
        wide = -(-(first + 2 * width) // LANES) * LANES - low
        lane = lax.broadcasted_iota(jnp.int32, (rows, wide), 1)
        first -= low
        masks = [(lane >= first + j * width) & (lane < first + (j + 1) * width) for j in range(2)]
        return slice(low, low + wide), first, masks

    keys = score_s[0].shape[1]
    chunk = min(256, keys)
    chunks = keys // chunk
    tiles = 2 * rows // ROW_TILE

    def stack(p):
        window, _, masks = layout(p)
        query = q_ref[pl.ds(at, rows), window].astype(F32)
        return jnp.concatenate([jnp.where(m, query, 0.0).astype(BF16) for m in masks], axis=0)

    def score(p, n, stacked):
        part = slice(n * chunk, (n + 1) * chunk)
        score_s[p % 2][:, part] = dot(stacked, k_ref[layout(p)[0], part])

    def soften(p, n):
        for r in range(n * tiles // chunks * ROW_TILE, (n + 1) * tiles // chunks * ROW_TILE, ROW_TILE):
            bias = bias_ref[group * heads + 2 * p + r // rows, r % rows : r % rows + ROW_TILE, :].astype(F32)
            scores = score_s[p % 2][r : r + ROW_TILE, :] + bias
            top = jnp.max(scores, axis=-1, keepdims=True)
            term_s[p % 2][r : r + ROW_TILE, :] = jnp.exp(scores - top).astype(BF16)
            top_s[p % 2][r : r + ROW_TILE, :] = jnp.broadcast_to(top, (ROW_TILE, LANES))

    def mix(p, n, mixed):
        part = slice(n * chunk, (n + 1) * chunk)
        window, first, _ = layout(p)
        values = v_ref[part, window]
        column = lax.broadcasted_iota(jnp.int32, values.shape, 1)
        used = (column >= first) & (column < first + 2 * width)
        more = dot(term_s[p % 2][:, part], jnp.where(used, values.astype(F32), 1.0).astype(BF16))
        return more if mixed is None else mixed + more

    def close(p, mixed, lse):
        window, first, masks = layout(p)
        free = 0 if first >= 16 else 2 * width
        total = mixed[:, free : free + 1]
        mixed = mixed / total
        sums = top_s[p % 2][...] + jnp.log(total)
        result = mix_s[:, window]
        for j in range(2):
            result = jnp.where(masks[j], mixed[j * rows : (j + 1) * rows], result)
            lse = jnp.where(spot == 2 * p + j, sums[j * rows : (j + 1) * rows], lse)
        mix_s[:, window] = result
        return lse

    lse = jnp.zeros((rows, LANES), F32)
    stacked = stack(0)
    for n in range(chunks):
        score(0, n, stacked)
    for p in range(pairs):
        mixed = None
        if p + 1 < pairs:
            stacked = stack(p + 1)
        for n in range(chunks):
            if p + 1 < pairs:
                score(p + 1, n, stacked)
            if p:
                mixed = mix(p - 1, n, mixed)
            soften(p, n)
        if p:
            lse = close(p - 1, mixed, lse)
    mixed = None
    for n in range(chunks):
        mixed = mix(pairs - 1, n, mixed)
    lse = close(pairs - 1, mixed, lse)
    return mix_s[...], lse


def group_scratch(rows, keys, feats, heads):
    return [
        pltpu.VMEM((2 * rows, keys), F32),
        pltpu.VMEM((2 * rows, keys), F32),
        pltpu.VMEM((2 * rows, keys), BF16),
        pltpu.VMEM((2 * rows, keys), BF16),
        pltpu.VMEM((2 * rows, LANES), F32),
        pltpu.VMEM((2 * rows, LANES), F32),
        pltpu.VMEM((rows, feats), F32),
        pltpu.VMEM((2, 2 * feats, feats), BF16),
        pltpu.SemaphoreType.DMA((2,)),
    ]


def scratch_of(refs):
    return refs[:2], refs[2:4], refs[4:6], refs[6]


def weight_copies(group, weight_hbm, refs):
    weight_s, sems = refs[7:9]
    feats = weight_s.shape[2]
    return [
        pltpu.make_async_copy(
            weight_hbm.at[:, pl.ds((part * GROUPS + group) * feats, feats)], weight_s.at[part], sems.at[part]
        )
        for part in range(2)
    ]


def project_keys(x_ref, weight_s, copies, k_ref, v_ref):
    tile = x_ref.shape[0] // 2
    copies[0].wait()
    for r in range(0, x_ref.shape[0], tile):
        k_ref[:, r : r + tile] = dot(x_ref[r : r + tile, :], weight_s[0]).T.astype(BF16)
    copies[1].wait()
    for r in range(0, x_ref.shape[0], tile):
        v_ref[r : r + tile, :] = dot(x_ref[r : r + tile, :], weight_s[1]).astype(BF16)


def first_kernel(heads, width, half_ref, core_ref, q_ref, own_a, own_b, other_a, other_b, gain_ref, weight_hbm,
                 bias_ref, x_ref, k_ref, v_ref, msg_ref, *refs):
    scratch = scratch_of(refs)
    weights = weight_copies(0, weight_hbm, refs)
    for copy in weights:
        copy.start()
    rows = own_a.shape[0]
    core = core_ref[0]
    gain = gain_ref[...].reshape(1, -1)
    for place, parts in ((core, (own_a, own_b)), (1 - core, (other_a, other_b))):
        values = jnp.concatenate([part[...].astype(F32) for part in parts], axis=1)
        x_ref[pl.ds(pl.multiple_of(place * rows, rows), rows), :] = norm_rows(values, gain).astype(BF16)
    project_keys(x_ref, refs[7], weights, k_ref, v_ref)
    mixed, lse = attend_group(0, heads, width, half_ref[0], q_ref, k_ref, v_ref, bias_ref, scratch)
    msg_ref[...] = pack_message(mixed, lse, heads)


def next_kernel(group, heads, width, half_ref, q_ref, x_ref, weight_hbm, bias_ref, k_ref, v_ref, msg_ref, *refs):
    scratch = scratch_of(refs)
    weights = weight_copies(group, weight_hbm, refs)
    for copy in weights:
        copy.start()
    project_keys(x_ref, refs[7], weights, k_ref, v_ref)
    mixed, lse = attend_group(group, heads, width, half_ref[0], q_ref, k_ref, v_ref, bias_ref, scratch)
    msg_ref[...] = pack_message(mixed, lse, heads)


def keep_kernel(group, heads, width, half_ref, q_ref, k_ref, v_ref, near_ref, bias_ref, o_ref, lse_ref, msg_ref, *refs):
    scratch = scratch_of(refs)
    mixed, lse = attend_group(group, heads, width, half_ref[0], q_ref, k_ref, v_ref, bias_ref, scratch)
    rows = mixed.shape[0]
    mixed, lse = merge_parts(mixed, lse, *unpack_message(near_ref[...], rows, heads), heads)
    o_ref[...] = mixed
    lse_ref[...] = lse
    msg_ref[...] = pack_message(mixed, lse, heads)


def group_call(kernel, group, half, scalars, q, arrays, weights, bias, outs, name):
    tok_rows, all_feats = q.shape
    rows, keys, feats = tok_rows // 2, bias.shape[2], all_feats // GROUPS
    heads = TH // GROUPS
    shapes = {
        "x": ((keys, all_feats), BF16),
        "k": ((feats, keys), BF16),
        "v": ((keys, feats), BF16),
        "o": ((rows, feats), F32),
        "lse": ((rows, LANES), F32),
        "msg": ((rows + 2 * heads, feats), BF16),
    }
    return pl.pallas_call(
        functools.partial(kernel, heads, feats // heads),
        grid_spec=pltpu.PrefetchScalarGridSpec(
            num_scalar_prefetch=1 + len(scalars),
            grid=(1,),
            in_specs=[pl.BlockSpec((tok_rows, feats), lambda i, *_: (0, group))]
            + [full(array.shape) for array in arrays]
            + [pl.BlockSpec(memory_space=pl.ANY)] * (0 if weights is None else 1)
            + [pl.BlockSpec(memory_space=pltpu.VMEM)],
            out_specs=[full(shapes[out][0]) for out in outs],
            scratch_shapes=group_scratch(rows, keys, feats, heads),
        ),
        out_shape=[jax.ShapeDtypeStruct(*shapes[out]) for out in outs],
        compiler_params=params(VMEM_SMALL),
        cost_estimate=pl.CostEstimate(flops=4 * 10**9, bytes_accessed=4 * 10**6, transcendentals=10**6),
        name=name,
    )(half, *scalars, q, *arrays, *([] if weights is None else [weights]), bias)


def merge_kernel(heads, o_ref, lse_ref, msg_ref, out_ref, sum_ref, back_ref):
    rows = o_ref.shape[0]
    mixed, lse = merge_parts(o_ref[...], lse_ref[...], *unpack_message(msg_ref[...], rows, heads), heads)
    out_ref[...] = mixed
    sum_ref[...] = lse
    back_ref[...] = pack_message(mixed, lse, heads)


def merge(o, lse, msg):
    return pl.pallas_call(
        functools.partial(merge_kernel, TH // GROUPS),
        out_shape=[jax.ShapeDtypeStruct(a.shape, a.dtype) for a in (o, lse, msg)],
        compiler_params=params(VMEM_SMALL),
        name="merge",
    )(o, lse, msg)


def settle_kernel(heads, o_ref, lse_ref, msg_ref, out_ref):
    rows = o_ref.shape[0]
    mixed, _ = merge_parts(o_ref[...], lse_ref[...], *unpack_message(msg_ref[...], rows, heads), heads)
    out_ref[...] = mixed.astype(BF16)


def settle(o, lse, msg):
    return pl.pallas_call(
        functools.partial(settle_kernel, TH // GROUPS),
        out_shape=jax.ShapeDtypeStruct(o.shape, BF16),
        compiler_params=params(VMEM_SMALL),
        name="settle",
    )(o, lse, msg)


def output_kernel(half_ref, own_a, own_b, other_a, other_b, a_ref, b_ref, weight_ref, out_ref):
    rows, feats = own_a.shape
    for place, first, second in ((half_ref[0], own_a, own_b), (1 - half_ref[0], other_a, other_b)):
        mine = pl.ds(pl.multiple_of(place * rows, rows), rows)
        result = dot(first[...], weight_ref[:feats, :]) + dot(second[...], weight_ref[feats:, :])
        out_ref[mine, :feats] = (a_ref[mine, :].astype(F32) + result[:, :feats]).astype(BF16)
        out_ref[mine, feats:] = (b_ref[mine, :].astype(F32) + result[:, feats:]).astype(BF16)


def output_rows(half, own, other, token_repr, weight):
    rows = token_repr[0].shape[0]
    return pl.pallas_call(
        output_kernel,
        in_specs=[pl.BlockSpec(memory_space=pltpu.SMEM)] + [pl.BlockSpec(memory_space=pltpu.VMEM)] * 7,
        out_shape=jax.ShapeDtypeStruct((rows, weight.shape[1]), BF16),
        compiler_params=params(VMEM_SMALL),
        name="output_rows",
    )(half, *own, *other, *token_repr, weight)


def bits_of(count):
    return [1 << b for b in range(count.bit_length() - 1)]


def key_parts(halves):
    n_pb, n_ka = lax.axis_size("pb"), lax.axis_size("ka")
    cores = n_pb // n_ka
    chips = n_pb // cores
    shard, plane = lax.axis_index("pb"), lax.axis_index("ka")
    bits = bits_of(chips)
    core = lax.rem(shard, cores)
    away = jnp.bitwise_xor(shard // cores, plane)
    held = list(halves)
    for r in range(len(bits)):
        pairs = []
        gets = jnp.bool_(False)
        for c in range(cores):
            order = bits if c % 2 == 0 else bits[::-1]
            known = sum(order[:r])
            for k in range(n_ka):
                for j in range(chips):
                    if (j ^ k) & ~known == 0:
                        pairs.append(((j * cores + c) * n_ka + k, ((j ^ order[r]) * cores + c) * n_ka + k))
            fresh = (jnp.bitwise_and(away, ~(known + order[r])) == 0) & (jnp.bitwise_and(away, order[r]) != 0)
            gets = gets | (fresh & (core == c))
        held = [jnp.where(gets, lax.ppermute(part, ("pb", "ka"), pairs), part) for part in held]
    return held


def body(
    atoms,
    atom_gain,
    atom_qkv,
    atom_proj,
    atom_bias,
    window_shift,
    token_of_atom,
    agg_weight,
    token_gain,
    token_q,
    token_kv,
    token_o,
    pair_bias,
):
    n_pb, n_ka = lax.axis_size("pb"), lax.axis_size("ka")
    shard, plane = lax.axis_index("pb"), lax.axis_index("ka")
    rows, width = atoms.shape
    tok_rows = pair_bias.shape[1]
    half = WIN_K // 2
    up = [(i, i + 1) for i in range(n_pb - 1)]
    down = [(i + 1, i) for i in range(n_pb - 1)]
    pos = shard.astype(jnp.int32).reshape(1)
    tok2d = token_of_atom.reshape(rows // LANES, LANES)
    left = lax.ppermute(atoms[rows - half :], "pb", up)
    right = lax.ppermute(atoms[:half], "pb", down)
    atom_out, msg = atom_attention(
        window_shift, pos, atoms, left, right, atom_gain, atom_qkv, atom_proj,
        atom_bias, tok2d, tok_rows, rows * n_pb,
    )
    behind = lax.ppermute(msg, "pb", up)
    token_repr = []
    for part in range(PARTS):
        sums, counts = pool(pos, atom_out, agg_weight, tok2d, tok_rows, part)
        token_repr.append(finish(behind, agg_weight, sums, counts, part))
    parity = jnp.bitwise_and(plane ^ (plane >> 1), 1).astype(jnp.int32)
    core = lax.rem(shard, n_pb // n_ka).astype(jnp.int32)
    keep, send = parity.reshape(1), (1 - parity).reshape(1)
    share = tok_rows // 2
    queries = project_queries(token_repr, token_gain, token_q)
    own_keys = key_parts(token_repr)
    own_keys[0], queries = lax.optimization_barrier((own_keys[0], queries))
    other_keys = [lax.ppermute(part, "pb", [(p, p ^ 1) for p in range(n_pb)]) for part in own_keys]
    bias, *own_keys = lax.optimization_barrier((pair_bias, *own_keys))
    send_bias = lax.dynamic_slice_in_dim(bias, (1 - parity) * share, share, axis=1)
    swap = [(i, i ^ 1) for i in range(n_ka)]
    bits = bits_of(n_ka)[1:]

    def far(msg, bit):
        return lax.ppermute(msg, "ka", [(i, i ^ (2 * bit - 1)) for i in range(n_ka)])

    x, k, v, msg = group_call(
        first_kernel, 0, send, (core.reshape(1),), queries, (*own_keys, *other_keys, token_gain), token_kv,
        send_bias, ("x", "k", "v", "msg"), "attend_first",
    )
    held, near = [(k, v)], [lax.ppermute(msg, "ka", swap)]
    bias, x = lax.optimization_barrier((bias, x))
    keep_bias = lax.dynamic_slice_in_dim(bias, parity * share, share, axis=1)
    for g in range(1, GROUPS):
        k, v, msg = group_call(
            functools.partial(next_kernel, g), g, send, (), queries, (x,), token_kv,
            send_bias, ("k", "v", "msg"), "attend_next",
        )
        held.append((k, v))
        near.append(lax.ppermute(msg, "ka", swap))
    sums, gone = [], []
    for g in range(GROUPS):
        o, lse, msg = group_call(
            functools.partial(keep_kernel, g), g, keep, (), queries, (*held[g], near[g]), None,
            keep_bias, ("o", "lse", "msg"), "attend_keep",
        )
        queries, msg = lax.optimization_barrier((queries, msg))
        sums.append((o, lse))
        gone.append(far(msg, bits[0]))
    own_mix, other_mix = [], []
    for g in range(GROUPS):
        (o, lse), got = sums[g], gone[g]
        for bit in bits[1:]:
            o, lse, msg = merge(o, lse, got)
            got = far(msg, bit)
        own_mix.append(settle(o, lse, got))
        other_mix.append(lax.ppermute(own_mix[g], "ka", swap))
    return atom_out, output_rows(keep, own_mix, other_mix, token_repr, token_o)


def solution(mesh):
    return jax.shard_map(
        body,
        mesh=mesh,
        in_specs=(
            P("pb", None),
            P(),
            P(),
            P(),
            P(None, "pb", None),
            P("pb"),
            P("pb"),
            P(),
            P(),
            P(),
            P(),
            P(),
            P(None, "pb", "ka"),
        ),
        out_specs=(P("pb", None), P("pb", None)),
        check_vma=False,
    )
```

```python
import functools
import math

import jax
import jax.numpy as jnp
from jax import lax
from jax.experimental import pallas as pl
from jax.experimental.pallas import tpu as pltpu
from jax.sharding import PartitionSpec as P

AH = 4
TH = 16
WIN_Q = 32
WIN_K = 128
SHIFT_MAX = 384
PARTS = 2
LANES = 128
F32 = jnp.float32
BF16 = jnp.bfloat16
VMEM_LIMIT = 56 * 1024 * 1024
VMEM_SMALL = 24 * 1024 * 1024


def full(shape):
    return pl.BlockSpec(shape, lambda *_: (0,) * len(shape))


def params(limit=VMEM_LIMIT):
    return pltpu.CompilerParams(vmem_limit_bytes=limit)


def norm_rows(as_float, gain):
    centre = jnp.mean(as_float, axis=-1, keepdims=True)
    spread = jnp.mean(jnp.square(as_float - centre), axis=-1, keepdims=True)
    return (as_float - centre) * lax.rsqrt(spread + 1e-05) * gain


def dot(a, b):
    return jnp.dot(a, b, preferred_element_type=F32)


def atom_kernel(
    chunks,
    atom_total,
    tok_rows,
    shift_ref,
    pos_ref,
    atoms_ref,
    left_ref,
    right_ref,
    gain_ref,
    qkv_ref,
    proj_ref,
    bias_ref,
    tok_ref,
    out_ref,
    msg_ref,
    q_s,
    k_s,
    v_s,
    x_s,
):
    step = pl.program_id(0)
    rows, width = atoms_ref.shape
    size = out_ref.shape[0]
    half = WIN_K // 2
    head = width // AH
    shard = pos_ref[0]

    @pl.when(step == 0)
    def _():
        gain = gain_ref[...].reshape(1, width)
        x_s[:half, :] = left_ref[...]
        x_s[half : half + rows, :] = atoms_ref[...]
        x_s[half + rows :, :] = right_ref[...]
        total = rows + 2 * half
        tile = 5 * WIN_K if total % (5 * WIN_K) == 0 else WIN_K

        def one(c, carry):
            at = pl.ds(pl.multiple_of(c * tile, tile), tile)
            normed = norm_rows(x_s[at, :].astype(F32), gain).astype(BF16)
            res = dot(normed, qkv_ref[...])
            q_s[at, :] = (res[:, :width] * (1.0 / math.sqrt(head))).astype(BF16)
            k_s[:, at] = res[:, width : 2 * width].T.astype(BF16)
            v_s[at, :width] = res[:, 2 * width :].astype(BF16)
            v_s[at, width:] = jnp.ones((tile, width), BF16)
            return carry

        lax.fori_loop(0, total // tile, one, 0, unroll=True)

    group = WIN_K // WIN_Q
    atoms_group = group * WIN_Q
    span = AH * WIN_Q
    lane_q = lax.broadcasted_iota(jnp.int32, (WIN_Q, width), 1)
    heads = [(lane_q >= h * head) & (lane_q < (h + 1) * head) for h in range(AH)]
    lane = lax.broadcasted_iota(jnp.int32, (span, WIN_K), 1)
    slot = lax.broadcasted_iota(jnp.int32, (1, WIN_K), 1)
    blocks = size // WIN_Q

    def region(n):
        return pl.ds(pl.multiple_of(step * size + n // group * atoms_group, atoms_group), 2 * WIN_K)

    def score(g):
        query = q_s[pl.ds(pl.multiple_of(step * size + g * atoms_group + half, half), atoms_group), :].astype(F32)
        stacked = [
            jnp.where(m, query[i * WIN_Q : (i + 1) * WIN_Q], 0.0).astype(BF16) for i in range(group) for m in heads
        ]
        return dot(jnp.concatenate(stacked, axis=0), k_s[:, region(g * group)])

    def soften(n, scores):
        offset = n % group * WIN_Q + half + shift_ref[step * blocks + n]
        early = lane >= offset
        begin = n * WIN_Q
        bias = bias_ref[:, begin : begin + WIN_Q, :].astype(F32).reshape(span, WIN_K)
        index = slot + jnp.where(slot >= offset, 0, WIN_K)
        index = index + (step * size + n // group * atoms_group + shard * rows - half)
        shut = jnp.where((index >= 0) & (index < atom_total), 0.0, -jnp.inf)
        logits = jnp.where(early, scores[:, :WIN_K], scores[:, WIN_K:]) + (
            pltpu.roll(bias, jnp.bitwise_and(offset, WIN_K - 1), 1) + shut
        )
        terms = jnp.exp(logits - jnp.max(logits, axis=-1, keepdims=True))
        return jnp.concatenate(
            [jnp.where(early, terms, 0.0).astype(BF16), jnp.where(early, 0.0, terms).astype(BF16)], axis=1
        )

    def mix(g, weights):
        mixed = dot(jnp.concatenate(weights, axis=0), v_s[region(g * group), :])
        merged = []
        for i in range(group):
            parts = [mixed[(i * AH + h) * WIN_Q : (i * AH + h + 1) * WIN_Q] for h in range(AH)]
            values, total = parts[0][:, :width], parts[0][:, width:]
            for h in range(1, AH):
                values = jnp.where(heads[h], parts[h][:, :width], values)
                total = jnp.where(heads[h], parts[h][:, width:], total)
            merged.append((values / total).astype(BF16))
        local = g * atoms_group
        at = pl.multiple_of(step * size + local, atoms_group)
        own = atoms_ref[pl.ds(at, atoms_group), :].astype(F32)
        result = own + dot(jnp.concatenate(merged, axis=0), proj_ref[...])
        out_ref[local : local + atoms_group, :] = result.astype(BF16)

    groups = blocks // group
    ahead = score(0)
    behind = None
    for g in range(groups):
        scores = ahead
        if g + 1 < groups:
            ahead = score(g + 1)
        if g:
            mix(g - 1, behind)
        behind = [soften(g * group + i, scores[i * span : (i + 1) * span]) for i in range(group)]
    mix(groups - 1, behind)

    @pl.when(step == chunks - 1)
    def _():
        ids = tok_ref[tok_ref.shape[0] - 8 :, :]
        code = jnp.maximum(ids - (shard + 1) * tok_rows + 1, 0)
        high = (code >> 4).astype(F32)
        low = (code & 15).astype(F32)
        msg_ref[:SHIFT_MAX, :] = out_ref[size - SHIFT_MAX :, :]
        msg_ref[SHIFT_MAX:, :] = jnp.concatenate([high, low], axis=0).astype(BF16)


def atom_attention(shift, pos, atoms, left, right, gain, qkv, proj, bias, tok2d, tok_rows, atom_total):
    rows, width = atoms.shape
    size = 2 * SHIFT_MAX
    chunks = rows // size
    half = WIN_K // 2
    return pl.pallas_call(
        functools.partial(atom_kernel, chunks, atom_total, tok_rows),
        grid_spec=pltpu.PrefetchScalarGridSpec(
            num_scalar_prefetch=2,
            grid=(chunks,),
            in_specs=[
                full((rows, width)),
                full((half, width)),
                full((half, width)),
                full((width,)),
                full(qkv.shape),
                full(proj.shape),
                pl.BlockSpec((AH, size, WIN_K), lambda i, *_: (0, i, 0)),
                full(tok2d.shape),
            ],
            out_specs=[
                pl.BlockSpec((size, width), lambda i, *_: (i, 0)),
                full((SHIFT_MAX + 16, width)),
            ],
            scratch_shapes=[
                pltpu.VMEM((rows + 2 * half, width), BF16),
                pltpu.VMEM((width, rows + 2 * half), BF16),
                pltpu.VMEM((rows + 2 * half, 2 * width), BF16),
                pltpu.VMEM((rows + 2 * half, width), BF16),
            ],
        ),
        out_shape=[
            jax.ShapeDtypeStruct((rows, width), BF16),
            jax.ShapeDtypeStruct((SHIFT_MAX + 16, width), BF16),
        ],
        compiler_params=params(),
        cost_estimate=pl.CostEstimate(flops=8 * 10**9, bytes_accessed=6 * 10**6, transcendentals=2 * 10**6),
        name="atom_attention",
    )(shift, pos, atoms, left, right, gain, qkv, proj, bias, tok2d)


def activate(rows, weight_half):
    u = dot(rows, weight_half)
    return (u + u * jnp.tanh(u)).astype(BF16)


def pool_kernel(tok_rows, pos_ref, out_ref, weight_ref, tok_ref, sum_ref, cnt_ref):
    step = pl.program_id(0)
    size = out_ref.shape[0]
    lines = size // LANES
    base = pos_ref[0] * tok_rows
    token = lax.broadcasted_iota(jnp.int32, (tok_rows, LANES), 0)
    weight_half = (weight_ref[...].astype(F32) * 0.5).astype(BF16)
    hidden = activate(out_ref[...], weight_half)
    ones = []
    for j in range(lines):
        ids = tok_ref[pl.ds(step * lines + j, 1), :] - base
        ones.append(jnp.where(token == ids, 1.0, 0.0))
    hot = jnp.concatenate(ones, axis=1).astype(BF16)
    count = functools.reduce(jnp.add, ones)
    more = dot(hot, hidden)

    @pl.when(step == 0)
    def _():
        sum_ref[...] = more
        cnt_ref[...] = count

    @pl.when(step > 0)
    def _():
        sum_ref[...] += more
        cnt_ref[...] += count


def pool(pos, atom_out, weight, tok2d, tok_rows, part):
    rows, width = atom_out.shape
    feats = weight.shape[1] // PARTS
    size = min(1024, rows)
    return pl.pallas_call(
        functools.partial(pool_kernel, tok_rows),
        grid_spec=pltpu.PrefetchScalarGridSpec(
            num_scalar_prefetch=1,
            grid=(rows // size,),
            in_specs=[
                pl.BlockSpec((size, width), lambda i, *_: (i, 0)),
                pl.BlockSpec((width, feats), lambda i, *_: (0, part)),
                full(tok2d.shape),
            ],
            out_specs=[full((tok_rows, feats)), full((tok_rows, LANES))],
        ),
        out_shape=[
            jax.ShapeDtypeStruct((tok_rows, feats), F32),
            jax.ShapeDtypeStruct((tok_rows, LANES), F32),
        ],
        compiler_params=params(VMEM_SMALL),
        cost_estimate=pl.CostEstimate(flops=2 * 10**9, bytes_accessed=2 * 10**6, transcendentals=10**6),
        name="pool",
    )(pos, atom_out, weight, tok2d)


def finish_kernel(msg_ref, weight_ref, sum_ref, cnt_ref, repr_ref):
    tok_rows = sum_ref.shape[0]
    size = msg_ref.shape[0] - 16
    lines = size // LANES
    token = lax.broadcasted_iota(jnp.int32, (tok_rows, LANES), 0).astype(F32)
    weight_half = (weight_ref[...].astype(F32) * 0.5).astype(BF16)
    hidden = activate(msg_ref[:size, :], weight_half)
    codes = msg_ref[size:, :].astype(F32)
    ids = codes[:8] * 16.0 + codes[8:] - 1.0
    ones = [jnp.where(token == ids[8 - lines + j : 9 - lines + j], 1.0, 0.0) for j in range(lines)]
    hot = jnp.concatenate(ones, axis=1).astype(BF16)
    count = functools.reduce(jnp.add, ones) + cnt_ref[...]
    sums = sum_ref[...] + dot(hot, hidden)
    repr_ref[...] = (sums / jnp.sum(count, axis=1, keepdims=True)).astype(BF16)


def finish(msg, weight, sums, counts, part):
    rows, feats = sums.shape
    return pl.pallas_call(
        finish_kernel,
        grid=(1,),
        in_specs=[
            full(msg.shape),
            pl.BlockSpec((weight.shape[0], feats), lambda i: (0, part)),
            full(sums.shape),
            full(counts.shape),
        ],
        out_specs=full((rows, feats)),
        out_shape=jax.ShapeDtypeStruct((rows, feats), BF16),
        compiler_params=params(VMEM_SMALL),
        cost_estimate=pl.CostEstimate(flops=2 * 10**8, bytes_accessed=2 * 10**6, transcendentals=2 * 10**5),
        name="token_finish",
    )(msg, weight, sums, counts)


def query_kernel(scale, a_ref, b_ref, gain_ref, weight_hbm, out_ref, weight_s, sem):
    copy = pltpu.make_async_copy(weight_hbm, weight_s, sem)
    copy.start()
    rows = jnp.concatenate([a_ref[...].astype(F32), b_ref[...].astype(F32)], axis=1)
    normed = norm_rows(rows, gain_ref[...].reshape(1, -1)).astype(BF16)
    copy.wait()
    out_ref[...] = (dot(normed, weight_s[...]) * scale).astype(BF16)


def project_queries(halves, gain, weight):
    rows = halves[0].shape[0]
    return pl.pallas_call(
        functools.partial(query_kernel, 1.0 / math.sqrt(weight.shape[1] // TH)),
        in_specs=[pl.BlockSpec(memory_space=pltpu.VMEM)] * 3 + [pl.BlockSpec(memory_space=pl.ANY)],
        out_shape=jax.ShapeDtypeStruct((rows, weight.shape[1]), BF16),
        scratch_shapes=[pltpu.VMEM(weight.shape, BF16), pltpu.SemaphoreType.DMA],
        compiler_params=params(VMEM_SMALL),
        cost_estimate=pl.CostEstimate(flops=5 * 10**8, bytes_accessed=3 * 10**6, transcendentals=0),
        name="queries",
    )(*halves, gain, weight)


GROUPS = 2
ROW_TILE = 32


def pack_message(mixed, lse, heads):
    lane = lax.broadcasted_iota(jnp.int32, lse.shape, 1)
    high = lse.astype(BF16).astype(F32)
    rest = lse - high
    middle = rest.astype(BF16).astype(F32)
    low = rest - middle
    first = jnp.where(lane < heads, high, pltpu.roll(middle, heads, 1))
    second = jnp.where(lane < heads, low, 0.0)
    turned = jnp.concatenate([first, second], axis=0).T
    return jnp.concatenate([mixed.astype(BF16), turned[: 2 * heads].astype(BF16)], axis=0)


def unpack_message(msg, rows, heads):
    coded = msg[rows:].astype(F32)
    coded = jnp.concatenate([coded, jnp.zeros((LANES - 2 * heads, coded.shape[1]), F32)], axis=0).T
    first = coded[:rows]
    return msg[:rows].astype(F32), first + pltpu.roll(first, LANES - heads, 1) + coded[rows:]


def merge_parts(mixed, lse, other, lse_b, heads):
    rows, feats = mixed.shape
    width = feats // heads
    spot = lax.broadcasted_iota(jnp.int32, (rows, LANES), 1)
    lse_b = jnp.where(spot < heads, lse_b, lse)
    top = jnp.maximum(lse, lse_b)
    part = jnp.exp(lse - top)
    total = part + jnp.exp(lse_b - top)
    share = part / total
    high = share.astype(BF16)
    low = (share - high.astype(F32)).astype(BF16)
    head = lax.broadcasted_iota(jnp.int32, (LANES, feats), 0) * width
    column = lax.broadcasted_iota(jnp.int32, (LANES, feats), 1)
    spread = jnp.where((column >= head) & (column < head + width), 1.0, 0.0).astype(BF16)
    wide = dot(high, spread) + dot(low, spread)
    return other + wide * (mixed - other), top + jnp.log(total)


def attend_group(group, heads, width, half, q_ref, k_ref, v_ref, bias_ref, scratch):
    score_s, term_s, top_s, mix_s = scratch
    rows = mix_s.shape[0]
    at = pl.multiple_of(half * rows, rows)
    pairs = heads // 2
    spot = lax.broadcasted_iota(jnp.int32, (rows, LANES), 1)

    def layout(p):
        first = 2 * p * width
        low = first // LANES * LANES
        wide = -(-(first + 2 * width) // LANES) * LANES - low
        lane = lax.broadcasted_iota(jnp.int32, (rows, wide), 1)
        first -= low
        masks = [(lane >= first + j * width) & (lane < first + (j + 1) * width) for j in range(2)]
        return slice(low, low + wide), first, masks

    keys = score_s[0].shape[1]
    chunk = min(256, keys)
    chunks = keys // chunk
    tiles = 2 * rows // ROW_TILE

    def stack(p):
        window, _, masks = layout(p)
        query = q_ref[pl.ds(at, rows), window].astype(F32)
        return jnp.concatenate([jnp.where(m, query, 0.0).astype(BF16) for m in masks], axis=0)

    def score(p, n, stacked):
        part = slice(n * chunk, (n + 1) * chunk)
        score_s[p % 2][:, part] = dot(stacked, k_ref[layout(p)[0], part])

    def soften(p, n):
        for r in range(n * tiles // chunks * ROW_TILE, (n + 1) * tiles // chunks * ROW_TILE, ROW_TILE):
            bias = bias_ref[group * heads + 2 * p + r // rows, r % rows : r % rows + ROW_TILE, :].astype(F32)
            scores = score_s[p % 2][r : r + ROW_TILE, :] + bias
            top = jnp.max(scores, axis=-1, keepdims=True)
            term_s[p % 2][r : r + ROW_TILE, :] = jnp.exp(scores - top).astype(BF16)
            top_s[p % 2][r : r + ROW_TILE, :] = jnp.broadcast_to(top, (ROW_TILE, LANES))

    def mix(p, n, mixed):
        part = slice(n * chunk, (n + 1) * chunk)
        window, first, _ = layout(p)
        values = v_ref[part, window]
        column = lax.broadcasted_iota(jnp.int32, values.shape, 1)
        used = (column >= first) & (column < first + 2 * width)
        more = dot(term_s[p % 2][:, part], jnp.where(used, values.astype(F32), 1.0).astype(BF16))
        return more if mixed is None else mixed + more

    def close(p, mixed, lse):
        window, first, masks = layout(p)
        free = 0 if first >= 16 else 2 * width
        total = mixed[:, free : free + 1]
        mixed = mixed / total
        sums = top_s[p % 2][...] + jnp.log(total)
        result = mix_s[:, window]
        for j in range(2):
            result = jnp.where(masks[j], mixed[j * rows : (j + 1) * rows], result)
            lse = jnp.where(spot == 2 * p + j, sums[j * rows : (j + 1) * rows], lse)
        mix_s[:, window] = result
        return lse

    lse = jnp.zeros((rows, LANES), F32)
    stacked = stack(0)
    for n in range(chunks):
        score(0, n, stacked)
    for p in range(pairs):
        mixed = None
        if p + 1 < pairs:
            stacked = stack(p + 1)
        for n in range(chunks):
            if p + 1 < pairs:
                score(p + 1, n, stacked)
            if p:
                mixed = mix(p - 1, n, mixed)
            soften(p, n)
        if p:
            lse = close(p - 1, mixed, lse)
    mixed = None
    for n in range(chunks):
        mixed = mix(pairs - 1, n, mixed)
    lse = close(pairs - 1, mixed, lse)
    return mix_s[...], lse


def group_scratch(rows, keys, feats, heads):
    return [
        pltpu.VMEM((2 * rows, keys), F32),
        pltpu.VMEM((2 * rows, keys), F32),
        pltpu.VMEM((2 * rows, keys), BF16),
        pltpu.VMEM((2 * rows, keys), BF16),
        pltpu.VMEM((2 * rows, LANES), F32),
        pltpu.VMEM((2 * rows, LANES), F32),
        pltpu.VMEM((rows, feats), F32),
        pltpu.VMEM((2, 2 * feats, feats), BF16),
        pltpu.SemaphoreType.DMA((2,)),
    ]


def scratch_of(refs):
    return refs[:2], refs[2:4], refs[4:6], refs[6]


def weight_copies(group, weight_hbm, refs):
    weight_s, sems = refs[7:9]
    feats = weight_s.shape[2]
    return [
        pltpu.make_async_copy(
            weight_hbm.at[:, pl.ds((part * GROUPS + group) * feats, feats)], weight_s.at[part], sems.at[part]
        )
        for part in range(2)
    ]


def project_keys(x_ref, weight_s, copies, k_ref, v_ref):
    tile = x_ref.shape[0] // 2
    copies[0].wait()
    for r in range(0, x_ref.shape[0], tile):
        k_ref[:, r : r + tile] = dot(x_ref[r : r + tile, :], weight_s[0]).T.astype(BF16)
    copies[1].wait()
    for r in range(0, x_ref.shape[0], tile):
        v_ref[r : r + tile, :] = dot(x_ref[r : r + tile, :], weight_s[1]).astype(BF16)


def first_kernel(heads, width, half_ref, core_ref, q_ref, own_a, own_b, other_a, other_b, gain_ref, weight_hbm,
                 bias_ref, x_ref, k_ref, v_ref, msg_ref, *refs):
    scratch = scratch_of(refs)
    weights = weight_copies(0, weight_hbm, refs)
    for copy in weights:
        copy.start()
    rows = own_a.shape[0]
    core = core_ref[0]
    gain = gain_ref[...].reshape(1, -1)
    for place, parts in ((core, (own_a, own_b)), (1 - core, (other_a, other_b))):
        values = jnp.concatenate([part[...].astype(F32) for part in parts], axis=1)
        x_ref[pl.ds(pl.multiple_of(place * rows, rows), rows), :] = norm_rows(values, gain).astype(BF16)
    project_keys(x_ref, refs[7], weights, k_ref, v_ref)
    mixed, lse = attend_group(0, heads, width, half_ref[0], q_ref, k_ref, v_ref, bias_ref, scratch)
    msg_ref[...] = pack_message(mixed, lse, heads)


def next_kernel(group, heads, width, half_ref, q_ref, x_ref, weight_hbm, bias_ref, k_ref, v_ref, msg_ref, *refs):
    scratch = scratch_of(refs)
    weights = weight_copies(group, weight_hbm, refs)
    for copy in weights:
        copy.start()
    project_keys(x_ref, refs[7], weights, k_ref, v_ref)
    mixed, lse = attend_group(group, heads, width, half_ref[0], q_ref, k_ref, v_ref, bias_ref, scratch)
    msg_ref[...] = pack_message(mixed, lse, heads)


def keep_kernel(group, heads, width, half_ref, q_ref, k_ref, v_ref, near_ref, bias_ref, o_ref, lse_ref, msg_ref, *refs):
    scratch = scratch_of(refs)
    mixed, lse = attend_group(group, heads, width, half_ref[0], q_ref, k_ref, v_ref, bias_ref, scratch)
    rows = mixed.shape[0]
    mixed, lse = merge_parts(mixed, lse, *unpack_message(near_ref[...], rows, heads), heads)
    o_ref[...] = mixed
    lse_ref[...] = lse
    msg_ref[...] = pack_message(mixed, lse, heads)


def group_call(kernel, group, half, scalars, q, arrays, weights, bias, outs, name):
    tok_rows, all_feats = q.shape
    rows, keys, feats = tok_rows // 2, bias.shape[2], all_feats // GROUPS
    heads = TH // GROUPS
    shapes = {
        "x": ((keys, all_feats), BF16),
        "k": ((feats, keys), BF16),
        "v": ((keys, feats), BF16),
        "o": ((rows, feats), F32),
        "lse": ((rows, LANES), F32),
        "msg": ((rows + 2 * heads, feats), BF16),
    }
    return pl.pallas_call(
        functools.partial(kernel, heads, feats // heads),
        grid_spec=pltpu.PrefetchScalarGridSpec(
            num_scalar_prefetch=1 + len(scalars),
            grid=(1,),
            in_specs=[pl.BlockSpec((tok_rows, feats), lambda i, *_: (0, group))]
            + [full(array.shape) for array in arrays]
            + [pl.BlockSpec(memory_space=pl.ANY)] * (0 if weights is None else 1)
            + [pl.BlockSpec(memory_space=pltpu.VMEM)],
            out_specs=[full(shapes[out][0]) for out in outs],
            scratch_shapes=group_scratch(rows, keys, feats, heads),
        ),
        out_shape=[jax.ShapeDtypeStruct(*shapes[out]) for out in outs],
        compiler_params=params(VMEM_SMALL),
        cost_estimate=pl.CostEstimate(flops=4 * 10**9, bytes_accessed=4 * 10**6, transcendentals=10**6),
        name=name,
    )(half, *scalars, q, *arrays, *([] if weights is None else [weights]), bias)


def merge_kernel(heads, o_ref, lse_ref, msg_ref, out_ref, sum_ref, back_ref):
    rows = o_ref.shape[0]
    mixed, lse = merge_parts(o_ref[...], lse_ref[...], *unpack_message(msg_ref[...], rows, heads), heads)
    out_ref[...] = mixed
    sum_ref[...] = lse
    back_ref[...] = pack_message(mixed, lse, heads)


def merge(o, lse, msg):
    return pl.pallas_call(
        functools.partial(merge_kernel, TH // GROUPS),
        out_shape=[jax.ShapeDtypeStruct(a.shape, a.dtype) for a in (o, lse, msg)],
        compiler_params=params(VMEM_SMALL),
        name="merge",
    )(o, lse, msg)


def settle_kernel(heads, o_ref, lse_ref, msg_ref, out_ref):
    rows = o_ref.shape[0]
    mixed, _ = merge_parts(o_ref[...], lse_ref[...], *unpack_message(msg_ref[...], rows, heads), heads)
    out_ref[...] = mixed.astype(BF16)


def settle(o, lse, msg):
    return pl.pallas_call(
        functools.partial(settle_kernel, TH // GROUPS),
        out_shape=jax.ShapeDtypeStruct(o.shape, BF16),
        compiler_params=params(VMEM_SMALL),
        name="settle",
    )(o, lse, msg)


def output_kernel(half_ref, own_a, own_b, other_a, other_b, a_ref, b_ref, weight_ref, out_ref):
    rows, feats = own_a.shape
    for place, first, second in ((half_ref[0], own_a, own_b), (1 - half_ref[0], other_a, other_b)):
        mine = pl.ds(pl.multiple_of(place * rows, rows), rows)
        result = dot(first[...], weight_ref[:feats, :]) + dot(second[...], weight_ref[feats:, :])
        out_ref[mine, :feats] = (a_ref[mine, :].astype(F32) + result[:, :feats]).astype(BF16)
        out_ref[mine, feats:] = (b_ref[mine, :].astype(F32) + result[:, feats:]).astype(BF16)


def output_rows(half, own, other, token_repr, weight):
    rows = token_repr[0].shape[0]
    return pl.pallas_call(
        output_kernel,
        in_specs=[pl.BlockSpec(memory_space=pltpu.SMEM)] + [pl.BlockSpec(memory_space=pltpu.VMEM)] * 7,
        out_shape=jax.ShapeDtypeStruct((rows, weight.shape[1]), BF16),
        compiler_params=params(VMEM_SMALL),
        name="output_rows",
    )(half, *own, *other, *token_repr, weight)


def bits_of(count):
    return [1 << b for b in range(count.bit_length() - 1)]


def key_parts(halves):
    n_pb, n_ka = lax.axis_size("pb"), lax.axis_size("ka")
    cores = n_pb // n_ka
    chips = n_pb // cores
    shard, plane = lax.axis_index("pb"), lax.axis_index("ka")
    bits = bits_of(chips)
    core = lax.rem(shard, cores)
    away = jnp.bitwise_xor(shard // cores, plane)
    held = list(halves)
    for r in range(len(bits)):
        pairs = []
        gets = jnp.bool_(False)
        for c in range(cores):
            order = bits if c % 2 == 0 else bits[::-1]
            known = sum(order[:r])
            for k in range(n_ka):
                for j in range(chips):
                    if (j ^ k) & ~known == 0:
                        pairs.append(((j * cores + c) * n_ka + k, ((j ^ order[r]) * cores + c) * n_ka + k))
            fresh = (jnp.bitwise_and(away, ~(known + order[r])) == 0) & (jnp.bitwise_and(away, order[r]) != 0)
            gets = gets | (fresh & (core == c))
        held = [jnp.where(gets, lax.ppermute(part, ("pb", "ka"), pairs), part) for part in held]
    return held


def body(
    atoms,
    atom_gain,
    atom_qkv,
    atom_proj,
    atom_bias,
    window_shift,
    token_of_atom,
    agg_weight,
    token_gain,
    token_q,
    token_kv,
    token_o,
    pair_bias,
):
    n_pb, n_ka = lax.axis_size("pb"), lax.axis_size("ka")
    shard, plane = lax.axis_index("pb"), lax.axis_index("ka")
    rows, width = atoms.shape
    tok_rows = pair_bias.shape[1]
    half = WIN_K // 2
    up = [(i, i + 1) for i in range(n_pb - 1)]
    down = [(i + 1, i) for i in range(n_pb - 1)]
    pos = shard.astype(jnp.int32).reshape(1)
    tok2d = token_of_atom.reshape(rows // LANES, LANES)
    left = lax.ppermute(atoms[rows - half :], "pb", up)
    right = lax.ppermute(atoms[:half], "pb", down)
    atom_out, msg = atom_attention(
        window_shift, pos, atoms, left, right, atom_gain, atom_qkv, atom_proj,
        atom_bias, tok2d, tok_rows, rows * n_pb,
    )
    behind = lax.ppermute(msg, "pb", up)
    token_repr = []
    for part in range(PARTS):
        sums, counts = pool(pos, atom_out, agg_weight, tok2d, tok_rows, part)
        token_repr.append(finish(behind, agg_weight, sums, counts, part))
    parity = jnp.bitwise_and(plane ^ (plane >> 1), 1).astype(jnp.int32)
    core = lax.rem(shard, n_pb // n_ka).astype(jnp.int32)
    keep, send = parity.reshape(1), (1 - parity).reshape(1)
    share = tok_rows // 2
    queries = project_queries(token_repr, token_gain, token_q)
    own_keys = key_parts(token_repr)
    own_keys[0], queries = lax.optimization_barrier((own_keys[0], queries))
    other_keys = [lax.ppermute(part, "pb", [(p, p ^ 1) for p in range(n_pb)]) for part in own_keys]
    bias, *own_keys = lax.optimization_barrier((pair_bias, *own_keys))
    send_bias = lax.dynamic_slice_in_dim(bias, (1 - parity) * share, share, axis=1)
    swap = [(i, i ^ 1) for i in range(n_ka)]
    bits = bits_of(n_ka)[1:]

    def far(msg, bit):
        return lax.ppermute(msg, "ka", [(i, i ^ (2 * bit - 1)) for i in range(n_ka)])

    x, k, v, msg = group_call(
        first_kernel, 0, send, (core.reshape(1),), queries, (*own_keys, *other_keys, token_gain), token_kv,
        send_bias, ("x", "k", "v", "msg"), "attend_first",
    )
    held, near = [(k, v)], [lax.ppermute(msg, "ka", swap)]
    bias, x = lax.optimization_barrier((bias, x))
    keep_bias = lax.dynamic_slice_in_dim(bias, parity * share, share, axis=1)
    x, keep_bias = lax.optimization_barrier((x, keep_bias))
    for g in range(1, GROUPS):
        k, v, msg = group_call(
            functools.partial(next_kernel, g), g, send, (), queries, (x,), token_kv,
            send_bias, ("k", "v", "msg"), "attend_next",
        )
        held.append((k, v))
        near.append(lax.ppermute(msg, "ka", swap))
    sums, gone = [], []
    for g in range(GROUPS):
        o, lse, msg = group_call(
            functools.partial(keep_kernel, g), g, keep, (), queries, (*held[g], near[g]), None,
            keep_bias, ("o", "lse", "msg"), "attend_keep",
        )
        sums.append((o, lse))
        gone.append(far(msg, bits[0]))
    own_mix, other_mix = [], []
    for g in range(GROUPS):
        (o, lse), got = sums[g], gone[g]
        for bit in bits[1:]:
            o, lse, msg = merge(o, lse, got)
            got = far(msg, bit)
        own_mix.append(settle(o, lse, got))
        other_mix.append(lax.ppermute(own_mix[g], "ka", swap))
    return atom_out, output_rows(keep, own_mix, other_mix, token_repr, token_o)


def solution(mesh):
    return jax.shard_map(
        body,
        mesh=mesh,
        in_specs=(
            P("pb", None),
            P(),
            P(),
            P(),
            P(None, "pb", None),
            P("pb"),
            P("pb"),
            P(),
            P(),
            P(),
            P(),
            P(),
            P(None, "pb", "ka"),
        ),
        out_specs=(P("pb", None), P("pb", None)),
        check_vma=False,
    )
```
